128 devices in a mesh: tm: 32 (over x, y_lo, z), rows: 4 (over y_hi, core).
Axes of the slice: x: 4, y: 4 (y_hi: 2, y_lo: 2; y = y_hi * 2 + y_lo), z: 4, core: 2. Of those that a mesh axis runs over, the one named last changes fastest.
Arguments:
- tokens: bfloat16 [512, 28, 28, 256], P('tm', 'rows')
- region_ids: int32 [512, 28, 28], P('tm', 'rows'), may hold values from 0 to 7, as said below
- gain_attn: float32 [256], replicated, may hold values from 0.25 to 1.75
- qkv_weight: bfloat16 [256, 768], replicated
- proj_weight: bfloat16 [256, 256], replicated, may hold values from -0.375 to 0.375
- gain_mlp: float32 [256], replicated, may hold values from 0.25 to 1.75
- up_weight: bfloat16 [256, 1024], replicated, may hold values from -0.375 to 0.375
- down_weight: bfloat16 [1024, 256], replicated, may hold values from -0.1875 to 0.1875
- gain_merge: float32 [1024], replicated, may hold values from 0.25 to 1.75
- reduce_weight: bfloat16 [1024, 512], replicated, may hold values from -0.1875 to 0.1875
- grad_merged: bfloat16 [512, 14, 14, 512], P(('tm', 'rows')), may hold values from -6 to 6
Outputs:
- merged: bfloat16 [512, 14, 14, 512], P(('tm', 'rows'))
- grad_tokens: bfloat16 [512, 28, 28, 256], P('tm', 'rows')
- grad_qkv: float32 [256, 768], replicated
- grad_proj: float32 [256, 256], replicated
- grad_up: float32 [256, 1024], replicated
- grad_down: float32 [1024, 256], replicated
- grad_reduce: float32 [1024, 512], replicated
- grad_gain_attn: float32 [256], replicated
- grad_gain_mlp: float32 [256], replicated
- grad_gain_merge: float32 [1024], replicated
The draws below stay inside these ranges and needn't reach their ends.
Inputs may be any that keep to these rules, and one draw needn't show every extreme that they name: `region_ids`: along time, rows and columns every aligned window of 8, 7 and 7 positions has one cut position, possibly at its end; a position's id is 4 a + 2 b + c, where a, b, c are 1 if it lies at or past the cut of its window along time, rows and columns, and 0 otherwise.
All inputs are finite; a program needn't handle non-finite values.
Results may differ from the reference program's by a relative error of at most 0.029.
Values may be sent and summed in bfloat16 or wider, within the bound.
A program may use at most 256 MiB of HBM per device.

```python
import math
import jax
import jax.numpy as jnp
from jax import lax

W = 28
C = 256
HEADS = 8
HID = 1024
C3 = 512
TT = 512
H = 28


def draw_tokens(key, part):
    key = jax.random.fold_in(key, 11)
    first = jax.random.fold_in(key, 0)
    values = jnp.clip(jax.random.normal(first, (TT, H, W, C), jnp.float32), -6.0, 6.0)
    return values.astype(jnp.bfloat16)


def draw_qkv_weight(key, part):
    key = jax.random.fold_in(key, 12)
    first = jax.random.fold_in(key, 0)
    spread = 1.0 / math.sqrt(C)
    values = jax.random.normal(first, (C, 3 * C), jnp.float32) * spread
    return values.astype(jnp.bfloat16)


def draw_region_ids(key, part):
    key = jax.random.fold_in(key, 13)
    first, second, third = jax.random.split(key, 3)
    cut_frames = jax.random.randint(first, (TT // 8,), 1, 9).at[0].set(4)
    cut_rows = jax.random.randint(second, (H // 7,), 1, 8).at[0].set(3)
    cut_cols = jax.random.randint(third, (W // 7,), 1, 8).at[0].set(3)
    frame_pos = jnp.arange(TT, dtype=jnp.int32)
    row_pos = jnp.arange(H, dtype=jnp.int32)
    col_pos = jnp.arange(W, dtype=jnp.int32)
    past_frames = (frame_pos % 8 >= cut_frames[frame_pos // 8]).astype(jnp.int32)
    past_rows = (row_pos % 7 >= cut_rows[row_pos // 7]).astype(jnp.int32)
    past_cols = (col_pos % 7 >= cut_cols[col_pos // 7]).astype(jnp.int32)
    return (4 * past_frames[:, None, None] + 2 * past_rows[None, :, None] + past_cols[None, None, :]).astype(jnp.int32)


def block_levels(own_key, extent, shards, low, high):
    loudness, own = 1.0, jax.random.fold_in(own_key, 6)
    for dim, blocks in shards:
        draws = jnp.exp(jax.random.uniform(jax.random.fold_in(own, dim), (blocks,), jnp.float32, low / len(shards), high / len(shards)))
        loudness = loudness * jnp.repeat(draws, extent[dim] // blocks).reshape([-1 if axis == dim else 1 for axis in range(len(extent))])
    return loudness


def noise(key, shape, width, most, cuts=(), kind=jnp.bfloat16):
    drawn = jax.random.normal(key, shape, jnp.float32) * width
    if len(cuts) > 0:
        drawn = block_levels(key, shape, cuts, -0.22, 0.18) * drawn
    return jnp.clip(drawn, min=-most, max=most).astype(kind)


def setup_inputs(seed: int = 0) -> dict:
    splits = jax.random.split(jax.random.key(seed), 12)
    tokens = draw_tokens(jax.random.fold_in(splits[11], 71), 0)
    region_ids = draw_region_ids(jax.random.fold_in(splits[11], 71), 0)
    gain_attn = jnp.clip(1.0 + 0.15 * jax.random.normal(splits[2], (C,), jnp.float32), 0.25, 1.75)
    qkv_weight = draw_qkv_weight(jax.random.fold_in(splits[11], 71), 0)
    proj_weight = noise(splits[4], (C, C), C ** -0.5, 0.375)
    gain_mlp = jnp.clip(1.0 + 0.15 * jax.random.normal(splits[5], (C,), jnp.float32), 0.25, 1.75)
    up_weight = noise(splits[6], (C, HID), C ** -0.5, 0.375)
    down_weight = noise(splits[7], (HID, C), HID ** -0.5, 0.1875)
    gain_merge = jnp.clip(1.0 + 0.15 * jax.random.normal(splits[8], (4 * C,), jnp.float32), 0.25, 1.75)
    reduce_weight = noise(splits[9], (4 * C, C3), (4 * C) ** -0.5, 0.1875)
    grad_merged = noise(splits[10], (TT, H // 2, W // 2, C3), 1.0, 6.0, ((0, 128),))
    return dict(tokens=tokens, region_ids=region_ids, gain_attn=gain_attn, qkv_weight=qkv_weight, proj_weight=proj_weight, gain_mlp=gain_mlp, up_weight=up_weight, down_weight=down_weight, gain_merge=gain_merge, reduce_weight=reduce_weight, grad_merged=grad_merged)


norm_eps = 1e-05

def rounded(values):
    return lax.optimization_barrier(values.astype(jnp.bfloat16))

def norm_forward(values):
    centre = lax.optimization_barrier(jnp.mean(values, axis=-1, keepdims=True))
    centred = values - centre
    spread = lax.optimization_barrier(jnp.mean(centred * centred, axis=-1, keepdims=True))
    inverse = lax.rsqrt(spread + norm_eps)
    return (centred * inverse, inverse)

def norm_backward(normed, inverse, gain, incoming):
    gated = incoming * gain
    first_mean = lax.optimization_barrier(jnp.mean(gated, axis=-1, keepdims=True))
    second_mean = lax.optimization_barrier(jnp.mean(gated * normed, axis=-1, keepdims=True))
    grad_input = inverse * (gated - first_mean - normed * second_mean)
    grad_gain = lax.optimization_barrier(jnp.sum(incoming * normed, axis=0))
    return (grad_input, grad_gain)

def contract_rows(left, right):
    return lax.dot_general(left, right, (((0,), (0,)), ((), ())), preferred_element_type=jnp.float32)

def times_transposed(left, right):
    return lax.dot_general(left, right, (((1,), (1,)), ((), ())), preferred_element_type=jnp.float32)

def gelu_slope(up_rows):
    normal_cdf = 0.5 * (1.0 + lax.erf(up_rows * 0.7071067811865476))
    normal_pdf = jnp.exp(-0.5 * up_rows * up_rows) * 0.3989422804014327
    return normal_cdf + up_rows * normal_pdf

def to_windows(grid_cells):
    frames, height, across, features = grid_cells.shape
    blocked = grid_cells.reshape(frames // 8, 8, height // 7, 7, across // 7, 7, features)
    return blocked.transpose(0, 2, 4, 1, 3, 5, 6).reshape(-1, 392, features)

def from_windows(windows, frames, height, across):
    features = windows.shape[-1]
    blocked = windows.reshape(frames // 8, height // 7, across // 7, 8, 7, 7, features)
    return blocked.transpose(0, 3, 1, 4, 2, 5, 6).reshape(frames, height, across, features)

def split_heads(qkv_win):
    window_count = qkv_win.shape[0]
    features = qkv_win.shape[-1] // 3
    head_size = features // HEADS
    query_vecs = qkv_win[..., :features].reshape(window_count, 392, HEADS, head_size)
    key_vecs = qkv_win[..., features:2 * features].reshape(window_count, 392, HEADS, head_size)
    value_vecs = qkv_win[..., 2 * features:].reshape(window_count, 392, HEADS, head_size)
    return (query_vecs, key_vecs, value_vecs, head_size)

def attend_forward(qkv_win, id_win):
    query_vecs, key_vecs, value_vecs, head_size = split_heads(qkv_win)
    scores = jnp.einsum('nqhd,nkhd->nhqk', query_vecs.astype(jnp.float32), key_vecs.astype(jnp.float32)) / math.sqrt(head_size)
    allowed = (id_win[:, :, None] == id_win[:, None, :])[:, None]
    scores = jnp.where(allowed, scores, -1e+30)
    row_top = lax.optimization_barrier(jnp.max(scores, axis=-1, keepdims=True))
    expon = jnp.exp(scores - row_top)
    probs = rounded(expon / lax.optimization_barrier(jnp.sum(expon, axis=-1, keepdims=True)))
    attended = jnp.einsum('nhqk,nkhd->nqhd', probs.astype(jnp.float32), value_vecs.astype(jnp.float32))
    return (rounded(attended).reshape(qkv_win.shape[0], 392, -1), probs)

def attend_backward(qkv_win, probs, grad_att):
    query_vecs, key_vecs, value_vecs, head_size = split_heads(qkv_win)
    window_count = qkv_win.shape[0]
    grad_heads = grad_att.reshape(window_count, 392, HEADS, head_size).astype(jnp.float32)
    probs_wide = probs.astype(jnp.float32)
    grad_probs = jnp.einsum('nqhd,nkhd->nhqk', grad_heads, value_vecs.astype(jnp.float32))
    grad_values = rounded(jnp.einsum('nhqk,nqhd->nkhd', probs_wide, grad_heads))
    inner_sum = lax.optimization_barrier(jnp.sum(grad_probs * probs_wide, axis=-1, keepdims=True))
    grad_scores = rounded(probs_wide * (grad_probs - inner_sum) / math.sqrt(head_size)).astype(jnp.float32)
    grad_queries = rounded(jnp.einsum('nhqk,nkhd->nqhd', grad_scores, key_vecs.astype(jnp.float32)))
    grad_keys = rounded(jnp.einsum('nhqk,nqhd->nkhd', grad_scores, query_vecs.astype(jnp.float32)))
    pieces = [grad_queries, grad_keys, grad_values]
    return jnp.concatenate([piece.reshape(window_count, 392, -1) for piece in pieces], axis=-1)

def block_forward(rolled, region, gain_attn, qkv_weight, proj_weight, gain_mlp, up_weight, down_weight):
    frames, height, across, features = rolled.shape
    flat = rolled.reshape(-1, features).astype(jnp.float32)
    normed1, inverse1 = norm_forward(flat)
    first_in = rounded(normed1 * gain_attn)
    qkv_rows = rounded(jnp.dot(first_in, qkv_weight, preferred_element_type=jnp.float32))
    per_step = across // 7
    qkv_win = to_windows(qkv_rows.reshape(frames, height, across, 3 * features))
    groups = qkv_win.shape[0] // per_step
    qkv_win = qkv_win.reshape(groups, per_step, 392, 3 * features)
    id_win = to_windows(region[..., None])[..., 0].reshape(groups, per_step, 392)

    def attend_group(bundle):
        return attend_forward(bundle[0], bundle[1])
    attended, probs = lax.map(attend_group, (qkv_win, id_win))
    attended = from_windows(attended.reshape(-1, 392, features), frames, height, across).reshape(-1, features)
    hidden1 = rounded(flat + jnp.dot(attended, proj_weight, preferred_element_type=jnp.float32))
    normed2, inverse2 = norm_forward(hidden1.astype(jnp.float32))
    second_in = rounded(normed2 * gain_mlp)
    up_rows = jnp.dot(second_in, up_weight, preferred_element_type=jnp.float32)
    act_rows = rounded(jax.nn.gelu(up_rows, approximate=False))
    out_rows = rounded(hidden1.astype(jnp.float32) + jnp.dot(act_rows, down_weight, preferred_element_type=jnp.float32))
    saved = (first_in, qkv_win, probs, attended, hidden1, second_in, up_rows, act_rows)
    return (out_rows.reshape(frames, height, across, features), saved)

def block_backward(rolled, saved, grad_out, gain_attn, qkv_weight, proj_weight, gain_mlp, up_weight, down_weight):
    first_in, qkv_win, probs, attended, hidden1, second_in, up_rows, act_rows = saved
    frames, height, across, features = rolled.shape
    grad_rows = grad_out.reshape(-1, features)
    grad_down = contract_rows(act_rows, grad_rows)
    grad_act = times_transposed(grad_rows, down_weight)
    grad_up_in = rounded(grad_act * gelu_slope(up_rows))
    grad_up = contract_rows(second_in, grad_up_in)
    grad_second = times_transposed(grad_up_in, up_weight)
    normed2, inverse2 = norm_forward(hidden1.astype(jnp.float32))
    back_mlp, grad_gain2 = norm_backward(normed2, inverse2, gain_mlp, grad_second)
    grad_hidden = grad_rows.astype(jnp.float32) + back_mlp
    grad_hidden_b = rounded(grad_hidden)
    grad_proj = contract_rows(attended, grad_hidden_b)
    grad_att = rounded(times_transposed(grad_hidden_b, proj_weight))
    att_win = to_windows(grad_att.reshape(frames, height, across, features)).reshape(qkv_win.shape[0], qkv_win.shape[1], 392, features)

    def attend_group_back(bundle):
        return attend_backward(bundle[0], bundle[1], bundle[2])
    grad_qkv_win = lax.map(attend_group_back, (qkv_win, probs, att_win))
    grad_qkv_rows = from_windows(grad_qkv_win.reshape(-1, 392, 3 * features), frames, height, across).reshape(-1, 3 * features)
    grad_qkv = contract_rows(first_in, grad_qkv_rows)
    grad_first = times_transposed(grad_qkv_rows, qkv_weight)
    normed1, inverse1 = norm_forward(rolled.reshape(-1, features).astype(jnp.float32))
    back_attn, grad_gain1 = norm_backward(normed1, inverse1, gain_attn, grad_first)
    grad_input = rounded(grad_hidden + back_attn)
    return (grad_input.reshape(frames, height, across, features), (grad_qkv, grad_proj, grad_up, grad_down, grad_gain1, grad_gain2))

def merge_both(section, gain_merge, reduce_weight, grad_merged):
    frames, height, across, features = section.shape
    joined = section.reshape(frames, height // 2, 2, across // 2, 2, features).transpose(0, 1, 3, 4, 2, 5).reshape(-1, 4 * features)
    normed3, inverse3 = norm_forward(joined.astype(jnp.float32))
    third_in = rounded(normed3 * gain_merge)
    merged = rounded(jnp.dot(third_in, reduce_weight, preferred_element_type=jnp.float32))
    grad_rows = grad_merged.reshape(-1, reduce_weight.shape[1])
    grad_reduce = contract_rows(third_in, grad_rows)
    grad_third = times_transposed(grad_rows, reduce_weight)
    back_merge, grad_gain3 = norm_backward(normed3, inverse3, gain_merge, grad_third)
    grad_joined = rounded(back_merge)
    grad_section = grad_joined.reshape(frames, height // 2, across // 2, 2, 2, features).transpose(0, 1, 4, 2, 3, 5).reshape(frames, height, across, features)
    return (merged.reshape(frames, height // 2, across // 2, -1), grad_section, grad_reduce, grad_gain3)

def reference(tokens, region_ids, gain_attn, qkv_weight, proj_weight, gain_mlp, up_weight, down_weight, gain_merge, reduce_weight, grad_merged):
    weights = (gain_attn, qkv_weight, proj_weight, gain_mlp, up_weight, down_weight)
    rolled = jnp.roll(tokens, (-4, -3, -3), (0, 1, 2))
    slabs = rolled.reshape(TT // 8, 8, H, W, C)
    regions = region_ids.reshape(TT // 8, 8, H, W)

    def forward_slab(bundle):
        return block_forward(bundle[0], bundle[1], *weights)[0]
    out_rolled = lax.map(forward_slab, (slabs, regions)).reshape(TT, H, W, C)
    initial = jnp.roll(out_rolled, (4, 3, 3), (0, 1, 2))

    def merge_slab(bundle):
        return merge_both(bundle[0], gain_merge, reduce_weight, bundle[1])
    merged, grad_section, grad_reduce, grad_gain3 = lax.map(merge_slab, (initial.reshape(TT // 8, 8, H, W, C), grad_merged.reshape(TT // 8, 8, H // 2, W // 2, C3)))
    merged = merged.reshape(TT, H // 2, W // 2, C3)
    grad_reduce = lax.optimization_barrier(jnp.sum(grad_reduce, axis=0))
    grad_gain3 = lax.optimization_barrier(jnp.sum(grad_gain3, axis=0))
    grad_rolled = jnp.roll(grad_section.reshape(TT, H, W, C), (-4, -3, -3), (0, 1, 2)).reshape(TT // 8, 8, H, W, C)

    def backward_slab(totals, bundle):
        outputs, saved = block_forward(bundle[0], bundle[1], *weights)
        grad_input, grads = block_backward(bundle[0], saved, bundle[2], *weights)
        return (jax.tree.map(jnp.add, totals, grads), grad_input)
    start = (jnp.zeros((C, 3 * C), jnp.float32), jnp.zeros((C, C), jnp.float32), jnp.zeros((C, HID), jnp.float32), jnp.zeros((HID, C), jnp.float32), jnp.zeros((C,), jnp.float32), jnp.zeros((C,), jnp.float32))
    totals, grad_slabs = lax.scan(backward_slab, start, (slabs, regions, grad_rolled))
    grad_tokens = jnp.roll(grad_slabs.reshape(TT, H, W, C), (4, 3, 3), (0, 1, 2))
    return (merged, grad_tokens, totals[0], totals[1], totals[2], totals[3], grad_reduce, totals[4], totals[5], grad_gain3)
```

```python
import math

import jax
import jax.numpy as jnp
from jax import lax
from jax.experimental import pallas as pl
from jax.experimental.pallas import tpu as pltpu
from jax.sharding import PartitionSpec as P

HEADS = 8
HEAD = 32
NPOS = 392
C = 256
HID = 1024
C3 = 512
EPS = 1e-05
LOG2E = 1.4426950408889634
LN2 = 0.6931471805599453
SCALE = 1.0 / math.sqrt(HEAD)
FAR = 1e30
F32 = jnp.float32
BF16 = jnp.bfloat16
MIB = 1024 * 1024


def dot_nn(left, right):
    return lax.dot_general(left, right, (((1,), (0,)), ((), ())), preferred_element_type=F32)


def dot_nt(left, right):
    return lax.dot_general(left, right, (((1,), (1,)), ((), ())), preferred_element_type=F32)


def dot_tn(left, right):
    return lax.dot_general(left, right, (((0,), (0,)), ((), ())), preferred_element_type=F32)


def norm_forward(values):
    centre = jnp.mean(values, axis=-1, keepdims=True)
    centred = values - centre
    spread = jnp.mean(centred * centred, axis=-1, keepdims=True)
    inverse = lax.rsqrt(spread + EPS)
    return centred * inverse, inverse


def norm_backward(normed, inverse, gain, incoming):
    gated = incoming * gain
    first_mean = jnp.mean(gated, axis=-1, keepdims=True)
    second_mean = jnp.mean(gated * normed, axis=-1, keepdims=True)
    return inverse * (gated - first_mean - normed * second_mean)


def gelu_and_slope(up):
    size = jnp.abs(up)
    base = 1.0 + (0.3275911 * 0.7071067811865476) * size
    guess = pl.reciprocal(base, approx=True)
    t = guess * (2.0 - base * guess)
    bell = jnp.exp2((-0.5 * LOG2E) * (up * up))
    series = 0.5 * 1.061405429 * t - 0.5 * 1.453152027
    series = series * t + 0.5 * 1.421413741
    series = series * t - 0.5 * 0.284496736
    series = series * t + 0.5 * 0.254829592
    tail = series * t * bell
    cdf = jnp.where(up >= 0.0, 1.0 - tail, tail)
    return up * cdf, cdf + up * (bell * 0.3989422804014327)


MESH = pl.DeviceIdType.MESH
RUNS = ((3, 0, 7), (10, 7, 7), (17, 14, 7), (24, 21, 4), (0, 25, 3))


def runs_of(wc):
    return range(wc, wc + 1) if wc < 3 else range(3, 5)


class Place:
    def __init__(self):
        self.m, self.r = lax.axis_index("tm"), lax.axis_index("rows")
        self.n_tm = lax.axis_size("tm")
        self.odd = lax.rem(self.r, 2)
        self.edge = jnp.where(self.r == 0, 1, 0)

    def at(self, dm, dr):
        return (lax.rem(self.m + dm + self.n_tm, self.n_tm), lax.rem(self.r + dr + 4, 4))

    def across(self):
        return (self.m, 3 - self.r)

    def holder(self, k):
        r = lax.rem(self.r - k + 4, 4)
        return self.at(-self.edge, k), self.at(jnp.where(r == 0, 1, 0), -k)

    def owner(self, k):
        r = lax.rem(self.r + k, 4)
        return self.at(jnp.where(r == 0, 1, 0), k), self.at(-self.edge, -k)

    def greet(self, sources, extra):
        barrier = pltpu.get_barrier_semaphore()
        for dev in sources:
            pl.semaphore_signal(barrier, inc=1, device_id=dev, device_id_type=MESH)

        @pl.when(self.r == 0)
        def _():
            pl.semaphore_signal(barrier, inc=1, device_id=extra, device_id_type=MESH)
            pl.semaphore_wait(barrier, len(sources) + 1)

        @pl.when(self.r != 0)
        def _():
            pl.semaphore_wait(barrier, len(sources))


def remote(src, dst, sems, n, dev):
    return pltpu.make_async_remote_copy(
        src_ref=src, dst_ref=dst, send_sem=sems[0].at[n], recv_sem=sems[1].at[n],
        device_id=dev, device_id_type=MESH,
    )


def pack(quarters):
    padded = jnp.concatenate([quarters, jnp.zeros((3, 4, C), F32)], axis=0).reshape(13, 4, 4, C)
    return jnp.concatenate([padded[:, n] for n in range(4)], axis=1).astype(BF16)


def unpack(packed):
    wide = packed.astype(F32)
    parts = [wide[:, 4 * n : 4 * (n + 1)].reshape(13, 1, 4, C) for n in range(4)]
    return jnp.concatenate(parts, axis=1).reshape(52, 4, C)[0:49]


def mask_rows(ids, pos, tw, wc):
    lane = lax.broadcasted_iota(jnp.int32, (1, 28), 1)
    first = lane == 7 * wc
    here = (lane >= 7 * wc) & (lane < 7 * wc + 7)
    frames = ids[0, pl.ds(pl.multiple_of(8 * tw, 8), 8), :]
    rows = ids[:, pl.ds(pl.multiple_of(8 * tw, 8), 8), :]

    def count(bits, kept):
        kept_bits = jnp.where(kept, bits.astype(F32), 0.0)
        return jnp.sum(jnp.sum(kept_bits, axis=0, keepdims=True), axis=1, keepdims=True)

    past = [
        count((frames >> 2) & 1, first),
        count(jnp.concatenate([(rows[i, 0:1] >> 1) & 1 for i in range(7)], axis=0), first),
        count(frames[0:1] & 1, here),
    ]
    bits = [
        jnp.where(pos[n : n + 1] >= extent - past[n], 1.0, 0.0)
        for n, extent in enumerate((8.0, 7.0, 7.0))
    ]
    none = [jnp.zeros((10, NPOS), F32)]
    keys = jnp.concatenate([v for b in bits for v in (b, 1.0 - b)] + none, axis=0)
    queries = jnp.concatenate([v for b in bits for v in (1.0 - b, b)] + none, axis=0) * -FAR
    return keys.astype(BF16), queries.astype(BF16)


def forward_kernel(
    tokens, gm, ids, pos, qkv_w, proj, gain1, gain2, up_w, down_w,
    x_out, qkv_out, exp_out, inv_out, att_out, hid_out, act_out, slope_out, out_out, qkv_t,
    gm_in, edge_in,
    tok, x_now, pack_t, halo_t, edge_out, own_sem, row_out, row_in, t_out, t_in, gm_out_sem, gm_in_sem,
    gm_own, edge_out_sem, edge_in_sem,
):
    tw, wc = pl.program_id(0), pl.program_id(1)
    place = Place()
    row_sems, t_sems = (row_out, row_in), (t_out, t_in)
    gm_sems, edge_sems = (gm_out_sem, gm_in_sem), (edge_out_sem, edge_in_sem)

    def own_copies():
        return [
            pltpu.make_async_copy(
                tokens.at[3:7, a : a + n], tok.at[0:4, b : b + n], own_sem.at[at]
            )
            for at, (a, b, n) in enumerate(((3, 0, 25), (0, 25, 3)))
        ]

    def row_copy(at):
        a, b, n = RUNS[at]
        return remote(
            tokens.at[0:3, a : a + n], tok.at[4:7, b : b + n], row_sems, at, place.at(0, -1)
        )

    def t_copy():
        return remote(pack_t.at[wc], halo_t.at[wc], t_sems, wc, place.at(-1, 0))

    def gm_copy(k, part):
        dev, _ = place.holder(k)
        band = lax.rem(place.r + k, 4)
        first = lax.rem(4 * band + 1 - band // 2 + 2 * part, 14)
        slot = lax.rem(place.r + 3, 4)
        src, dst = gm.at[pl.ds(first, 2)], gm_in.at[slot, 2 * part : 2 * part + 2]
        return remote(src, dst, gm_sems, 2 * k + part, dev)

    def gm_local(part):
        band = place.r
        first = lax.rem(4 * band + 1 - band // 2 + 2 * part, 14)
        slot = lax.rem(place.r + 3, 4)
        return pltpu.make_async_copy(
            gm.at[pl.ds(first, 2)], gm_in.at[slot, 2 * part : 2 * part + 2], gm_own.at[part]
        )

    def edge_copy(half):
        return remote(edge_out.at[half], edge_in.at[half], edge_sems, half, place.across())

    @pl.when((tw == 0) & (wc == 0))
    def _():
        for copy in own_copies():
            copy.start()
        sources = [place.at(0, 1), place.at(1, 0), place.across()]
        place.greet(sources + [place.holder(k)[1] for k in (1, 2, 3)], place.holder(0)[1])
        for at in range(5):
            row_copy(at).start()
        qkv_t[...] = qkv_w[...].astype(F32).T.astype(BF16)
        for copy in own_copies():
            copy.wait()

    @pl.when((tw == 0) & (wc == 1))
    def _():
        for k in (1, 2, 3):
            for part in range(2):
                gm_copy(k, part).start()

        @pl.when(place.r == 0)
        def _():
            for part in range(2):
                gm_copy(0, part).start()

        @pl.when(place.r != 0)
        def _():
            for part in range(2):
                gm_local(part).start()

    for window in range(4):

        @pl.when((tw == 0) & (wc == window))
        def _(window=window):
            for at in runs_of(window):
                row_copy(at).wait_recv()

    @pl.when(tw == 0)
    def _():
        block = tok[:, pl.ds(7 * wc, 7)].astype(F32).reshape(49, 16, C)
        pack_t[wc] = pack(block[:, 0:4])
        t_copy().start()
        x_now[...] = block[:, 4:12]

    @pl.when(tw == 1)
    def _():
        t_copy().wait_recv()
        block = tok[:, pl.ds(7 * wc, 7)].astype(F32).reshape(49, 16, C)
        x_now[...] = jnp.concatenate([block[:, 12:16], unpack(halo_t[wc])], axis=1)

    x = x_now[...].reshape(NPOS, C)
    x_out[0] = x.astype(BF16)
    mask_k, mask_q = mask_rows(ids, pos, tw, wc)
    normed, _ = norm_forward(x)
    first_in = (normed * gain1[...]).astype(BF16)
    rows = dot_nt(qkv_t[...], first_in)
    qkv_out[0, 0:C] = (rows[0:C] * (SCALE * LOG2E)).astype(BF16)
    qkv_out[0, C:] = rows[C:].astype(BF16)
    for h in range(HEADS):
        here = slice(HEAD * h, HEAD * (h + 1))
        q = jnp.concatenate([qkv_out[0, HEAD * h : HEAD * (h + 1)], mask_q], axis=0)
        k = jnp.concatenate([qkv_out[0, C + HEAD * h : C + HEAD * (h + 1)], mask_k], axis=0)
        v = qkv_out[0, 2 * C + HEAD * h : 2 * C + HEAD * (h + 1)]
        scores = dot_tn(k, q)
        top = jnp.max(scores, axis=0, keepdims=True)
        expon = jnp.exp2(scores - top)
        inverse = 1.0 / jnp.sum(expon, axis=0, keepdims=True)
        expon = expon.astype(BF16)
        exp_out[0, h] = expon
        inv_out[0, h : h + 1] = inverse
        att_out[0, here] = (dot_nn(v, expon) * inverse).astype(BF16)
    hidden = (x + dot_tn(att_out[0], proj[...])).astype(BF16)
    hid_out[0] = hidden
    hidden = hidden.astype(F32)
    normed, _ = norm_forward(hidden)
    second_in = (normed * gain2[...]).astype(BF16)
    result = hidden
    for part in range(4):
        cols = slice(256 * part, 256 * (part + 1))
        act, slope = gelu_and_slope(dot_nn(second_in, up_w[:, cols]))
        act = act.astype(BF16)
        act_out[0, :, cols] = act
        slope_out[0, :, cols] = slope.astype(BF16)
        result = result + dot_nn(act, down_w[cols])
    out_out[0] = result.astype(BF16)
    edge = jnp.where(place.odd == 1, result[336:392], result[0:56])
    edge_out[tw, wc] = edge.astype(BF16)

    @pl.when((tw == 0) & (wc == 3))
    def _():
        edge_copy(0).start()

    @pl.when((tw == 1) & (wc == 3))
    def _():
        edge_copy(1).start()
        for at in range(5):
            row_copy(at).wait_send()
        for n in range(4):
            remote(pack_t.at[n], halo_t.at[n], t_sems, n, place.at(-1, 0)).wait_send()
        for k in (1, 2, 3):
            for part in range(2):
                gm_copy(k, part).wait()

        @pl.when(place.r == 0)
        def _():
            for part in range(2):
                gm_copy(0, part).wait()

        @pl.when(place.r != 0)
        def _():
            for part in range(2):
                gm_local(part).wait()

        for half in range(2):
            edge_copy(half).wait()


def whole(shape):
    return pl.BlockSpec(shape, lambda *_: (0,) * len(shape))


def by_window(shape, backwards=False):
    def index(tw, wc):
        return (4 * (1 - tw if backwards else tw) + wc,) + (0,) * len(shape)

    return pl.BlockSpec((1,) + shape, index)


SMEM_SPEC = pl.BlockSpec(memory_space=pltpu.SMEM)
ANY_SPEC = pl.BlockSpec(memory_space=pl.ANY)
DMA = pltpu.SemaphoreType.DMA


def positions():
    at = jnp.arange(NPOS)
    rows = [at % 8, at // 56, (at // 8) % 7]
    return jnp.concatenate([jnp.stack(rows), jnp.zeros((5, NPOS), at.dtype)]).astype(F32)


def run_forward(tokens, gm, ids, qkv_w, proj, gain1, gain2, up_w, down_w):
    saved = [
        ((NPOS, C), BF16),
        ((3 * C, NPOS), BF16),
        ((HEADS, NPOS, NPOS), BF16),
        ((HEADS, NPOS), F32),
        ((C, NPOS), BF16),
        ((NPOS, C), BF16),
        ((NPOS, HID), BF16),
        ((NPOS, HID), BF16),
        ((NPOS, C), BF16),
    ]
    pos = positions()
    return pl.pallas_call(
        forward_kernel,
        grid=(2, 4),
        out_shape=[jax.ShapeDtypeStruct((8,) + shape, kind) for shape, kind in saved]
        + [
            jax.ShapeDtypeStruct((3 * C, C), BF16),
            jax.ShapeDtypeStruct((4, 4, 14, 4, C3), BF16),
            jax.ShapeDtypeStruct((2, 4, 56, C), BF16),
        ],
        in_specs=[ANY_SPEC, ANY_SPEC, whole(ids.shape), whole(pos.shape)]
        + [whole(w.shape) for w in (qkv_w, proj, gain1, gain2, up_w, down_w)],
        out_specs=[by_window(shape) for shape, _ in saved]
        + [whole((3 * C, C)), ANY_SPEC, ANY_SPEC],
        scratch_shapes=[
            pltpu.VMEM((7, 28, 16, C), BF16),
            pltpu.VMEM((49, 8, C), F32),
            pltpu.VMEM((4, 13, 16, C), BF16),
            pltpu.VMEM((4, 13, 16, C), BF16),
            pltpu.VMEM((2, 4, 56, C), BF16),
            DMA((2,)), DMA((5,)), DMA((5,)), DMA((4,)), DMA((4,)), DMA((8,)), DMA((8,)),
            DMA((2,)), DMA((2,)), DMA((2,)),
        ],
        compiler_params=pltpu.CompilerParams(
            vmem_limit_bytes=58 * MIB, collective_id=1, has_side_effects=True
        ),
        name="forward",
    )(tokens, gm, ids, pos, qkv_w, proj, gain1, gain2, up_w, down_w)


def to_blocks(blocks, first, values):
    height, width = values.shape
    for a in range(height // 256):
        for b in range(width // 128):
            part = values[256 * a : 256 * (a + 1), 128 * b : 128 * (b + 1)]
            blocks[first + a * (width // 128) + b] = part.astype(BF16)


def from_blocks(blocks, first, height, width):
    rows, cols = height // 256, width // 128
    part = blocks[first : first + rows * cols].reshape(rows, cols, 256, 128)
    return part.transpose(0, 2, 1, 3).reshape(height, width).astype(F32)


def column_runs(wc):
    if wc < 3:
        return [(7 * wc + 3, 0, 7)]
    return [(24, 0, 4), (0, 4, 7)]


def merge_kernel(
    out_win, edge, gm, gain3, reduce_w, place,
    grad_out, m_all, reduce_blocks, grad_gain,
    rows, third_all, gm_rows, grad_reduce,
):
    tw = pl.program_id(0)
    r = place[0]
    odd = lax.rem(r, 2)

    @pl.when(tw == 0)
    def _():
        grad_reduce[...] = jnp.zeros_like(grad_reduce)
        grad_gain[...] = jnp.zeros_like(grad_gain)

    for wc in range(4):
        block = out_win[wc].astype(F32).reshape(7, 7, 8, C)
        strip = edge[0, wc].astype(F32).reshape(7, 8, C)
        for start, first, last in column_runs(wc):
            cols = slice(start, start + last - first)
            rows[pl.ds(1 - odd, 7), cols] = block[:, first:last]
            rows[7 * odd, cols] = strip[first:last]

    gain = gain3[...]
    for a in range(4):
        upper = rows[2 * a].reshape(14, 2, 8, C)
        lower = rows[2 * a + 1].reshape(14, 2, 8, C)
        joined = jnp.concatenate(
            [upper[:, 0], lower[:, 0], upper[:, 1], lower[:, 1]], axis=-1
        ).reshape(112, 4 * C)
        normed, inverse = norm_forward(joined)
        third = normed * gain
        merged = dot_nn(third.astype(BF16), reduce_w[...])
        merged = merged.reshape(14, 8, C3)
        m_all[0, a] = merged[:, 0:4].astype(BF16)
        m_all[1, a] = merged[:, 4:8].astype(BF16)
        grads = jnp.concatenate([gm[0, a].astype(F32), gm[1, a].astype(F32)], axis=1)
        grads = grads.reshape(112, C3).astype(BF16)
        gz = dot_nt(grads, reduce_w[...])
        gz_sum = jnp.sum(gz * normed, axis=0, keepdims=True)
        if a == 0:
            counted = jnp.where((odd == 0) & (tw == 1), 0.0, 1.0)
        elif a == 3:
            counted = jnp.where((odd == 1) & (tw == 0), 0.0, 1.0)
        else:
            counted = None
        if counted is not None:
            third = third * counted
            gz_sum = gz_sum * counted
        grad_gain[...] += gz_sum
        third_all[112 * a : 112 * (a + 1)] = third.astype(BF16)
        gm_rows[112 * a : 112 * (a + 1)] = grads
        back = norm_backward(normed, inverse, gain, gz).reshape(14, 8, 4 * C)
        pieces = [back[:, :, C * n : C * (n + 1)].reshape(14, 1, 8, C) for n in range(4)]
        rows[2 * a] = jnp.concatenate([pieces[0], pieces[2]], axis=1).reshape(28, 8, C)
        rows[2 * a + 1] = jnp.concatenate([pieces[1], pieces[3]], axis=1).reshape(28, 8, C)
    grad_reduce[...] += dot_tn(third_all[...], gm_rows[...])
    for wc in range(4):
        runs = [
            rows[pl.ds(1 - odd, 7), start : start + last - first]
            for start, first, last in column_runs(wc)
        ]
        block = runs[0] if len(runs) == 1 else jnp.concatenate(runs, axis=1)
        grad_out[wc] = block.reshape(NPOS, C).astype(BF16)

    @pl.when(tw == 1)
    def _():
        to_blocks(reduce_blocks, 0, grad_reduce)


def run_merge(out_win, edge, gm, gain3, reduce_w, place):
    def by_tw(shape):
        return pl.BlockSpec(shape, lambda tw: (tw,) + (0,) * (len(shape) - 1))

    pieces = (2, 4, 14, 4, C3)
    return pl.pallas_call(
        merge_kernel,
        grid=(2,),
        out_shape=[
            jax.ShapeDtypeStruct((8, NPOS, C), BF16),
            jax.ShapeDtypeStruct((4, 4, 14, 4, C3), BF16),
            jax.ShapeDtypeStruct((16, 256, 128), BF16),
            jax.ShapeDtypeStruct((1, 4 * C), F32),
        ],
        in_specs=[by_tw((4, NPOS, C)), by_tw((1, 4, 56, C)), by_tw(pieces)]
        + [whole((1, 4 * C)), whole((4 * C, C3)), SMEM_SPEC],
        out_specs=[by_tw((4, NPOS, C)), by_tw(pieces), whole((16, 256, 128)), whole((1, 4 * C))],
        scratch_shapes=[
            pltpu.VMEM((8, 28, 8, C), F32),
            pltpu.VMEM((448, 4 * C), BF16),
            pltpu.VMEM((448, C3), BF16),
            pltpu.VMEM((4 * C, C3), F32),
        ],
        compiler_params=pltpu.CompilerParams(vmem_limit_bytes=58 * MIB),
        name="merge",
    )(out_win, edge, gm, gain3, reduce_w, place)


def backward_kernel(
    grad_out, x_in, qkv_in, exp_in, inv_in, att_in, hid_in, act_in, slope_in,
    qkv_t, proj, gain1, gain2, up_w, down_w, reduce_blocks, grad_gain3, pieces,
    blocks, merged, grad_tokens,
    grad_rows_t, grad_qkv_t, grad_proj, grad_up, grad_down_t, grad_gain1, grad_gain2,
    late, final, pack_t, halo_t, t_out, t_in, row_out, row_in, own_sem, m_out, m_in, m_own,
):
    tw, wc = 1 - pl.program_id(0), pl.program_id(1)
    place = Place()
    t_sems, row_sems, m_sems = (t_out, t_in), (row_out, row_in), (m_out, m_in)

    def m_ends(k, n):
        c = lax.rem(place.r + k + 3, 4)
        start = 4 * place.r + 1 - place.r // 2
        first = (1 - place.odd, 3 - place.odd, 3)[n]
        count = (2, 1, 1)[n]
        return (
            pieces.at[c, pl.ds(first, count)],
            merged.at[pl.ds(lax.rem(start + first, 14), count)],
        )

    def m_copy(k, n):
        return remote(*m_ends(k, n), m_sems, 3 * k + n, place.owner(k)[0])

    def m_local(n):
        return pltpu.make_async_copy(*m_ends(0, n), m_own.at[n])

    def m_each(act_remote, act_local):
        for k in (1, 2, 3):
            act_remote(k, 0)
            act_remote(k, 1)

        @pl.when(place.r == 0)
        def _():
            act_remote(0, 0)
            act_remote(0, 1)

        @pl.when(place.r != 0)
        def _():
            act_local(0)
            act_local(1)

    def t_copy(n):
        return remote(pack_t.at[n], halo_t.at[n], t_sems, n, place.at(1, 0))

    def row_copy(at):
        a, b, n = RUNS[at]
        window, first = (at, 0) if at < 3 else (3, b - 21)
        return remote(
            final.at[window, 4:7, first : first + n], grad_tokens.at[0:3, a : a + n],
            row_sems, at, place.at(0, 1),
        )

    def own_copy(at):
        a, b, n = RUNS[at]
        window, first = (at, 0) if at < 3 else (3, b - 21)
        return pltpu.make_async_copy(
            final.at[window, 0:4, first : first + n], grad_tokens.at[3:7, a : a + n], own_sem.at[at]
        )

    @pl.when((tw == 1) & (wc == 0))
    def _():
        sources = [place.at(0, -1), place.at(-1, 0)]
        place.greet(sources + [place.owner(k)[1] for k in (1, 2, 3)], place.owner(0)[1])
        m_each(lambda k, n: m_copy(k, n).start(), lambda n: m_local(n).start())

        @pl.when(place.odd == 1)
        def _():
            for k in (1, 2, 3):
                m_copy(k, 2).start()
            m_local(2).start()

        for ref in (grad_qkv_t, grad_proj, grad_up, grad_down_t, grad_gain1, grad_gain2):
            ref[...] = jnp.zeros_like(ref)

    grad_rows = grad_out[0]
    normed2, inverse2 = norm_forward(hid_in[0].astype(F32))
    second_in = (normed2 * gain2[...]).astype(BF16)
    grad_second = jnp.zeros((NPOS, C), F32)
    for part in range(4):
        cols = slice(256 * part, 256 * (part + 1))
        grad_down_t[:, cols] += dot_tn(grad_rows, act_in[0, :, cols])
        grad_act = dot_nt(grad_rows, down_w[cols])
        grad_up_in = (grad_act * slope_in[0, :, cols].astype(F32)).astype(BF16)
        grad_up[:, cols] += dot_tn(second_in, grad_up_in)
        grad_second = grad_second + dot_nt(grad_up_in, up_w[:, cols])
    grad_gain2[...] += jnp.sum(grad_second * normed2, axis=0, keepdims=True)
    grad_hidden = grad_rows.astype(F32) + norm_backward(normed2, inverse2, gain2[...], grad_second)
    grad_hidden_b = grad_hidden.astype(BF16)
    grad_proj[...] += dot_nn(att_in[0], grad_hidden_b)
    grad_att = dot_nt(proj[...], grad_hidden_b).astype(BF16)
    for h in range(HEADS):
        at_q = slice(HEAD * h, HEAD * (h + 1))
        at_k = slice(C + HEAD * h, C + HEAD * (h + 1))
        at_v = slice(2 * C + HEAD * h, 2 * C + HEAD * (h + 1))
        expon = exp_in[0, h]
        incoming = (grad_att[at_q].astype(F32) * inv_in[0, h : h + 1]).astype(BF16)
        inner = jnp.sum(incoming.astype(F32) * att_in[0, at_q].astype(F32), axis=0, keepdims=True)
        grad_probs = dot_tn(qkv_in[0, at_v], incoming)
        grad_scores = (expon.astype(F32) * (grad_probs - inner)).astype(BF16)
        grad_rows_t[at_q] = (dot_nn(qkv_in[0, at_k], grad_scores) * SCALE).astype(BF16)
        grad_rows_t[at_k] = (dot_nt(qkv_in[0, at_q], grad_scores) * LN2).astype(BF16)
        grad_rows_t[at_v] = dot_nt(incoming, expon).astype(BF16)
    normed1, inverse1 = norm_forward(x_in[0].astype(F32))
    first_in = (normed1 * gain1[...]).astype(BF16)
    grad_qkv_t[...] += dot_nn(grad_rows_t[...], first_in)
    grad_first = dot_tn(grad_rows_t[...], qkv_t[...])
    grad_gain1[...] += jnp.sum(grad_first * normed1, axis=0, keepdims=True)
    grad_x = grad_hidden + norm_backward(normed1, inverse1, gain1[...], grad_first)
    block = grad_x.reshape(49, 8, C)

    @pl.when(tw == 1)
    def _():
        late[wc] = block[:, 0:4].astype(BF16)
        pack_t[wc] = pack(block[:, 4:8])
        t_copy(wc).start()

    @pl.when(tw == 0)
    def _():
        t_copy(wc).wait_recv()
        frames = jnp.concatenate([unpack(halo_t[wc]), block, late[wc].astype(F32)], axis=1)
        final[wc] = frames.astype(BF16).reshape(7, 7, 16, C)

    for window in range(4):

        @pl.when((tw == 0) & (wc == window))
        def _(window=window):
            for at in runs_of(window):
                row_copy(at).start()
                own_copy(at).start()

    @pl.when((tw == 0) & (wc == 3))
    def _():
        blocks[0:16] = reduce_blocks[...]
        to_blocks(blocks, 16, grad_up)
        to_blocks(blocks, 24, grad_down_t[...].T)
        to_blocks(blocks, 32, grad_qkv_t[...].T)
        to_blocks(blocks, 38, grad_proj)
        gains = [grad_gain1, grad_gain1, grad_gain2, grad_gain2] + [grad_gain3] * 8
        lanes = [0, 1, 0, 1] + list(range(8))
        rows = [ref[:, 128 * n : 128 * (n + 1)] for ref, n in zip(gains, lanes)]
        blocks[40, 0:16] = jnp.concatenate(rows + [jnp.zeros((4, 128), F32)], axis=0).astype(BF16)
        blocks[40, 16:256] = jnp.zeros((240, 128), BF16)
        blocks[41:48] = jnp.zeros((7, 256, 128), BF16)
        for at in range(5):
            row_copy(at).wait()
            own_copy(at).wait()
        for n in range(4):
            t_copy(n).wait_send()
        m_each(lambda k, n: m_copy(k, n).wait(), lambda n: m_local(n).wait())

        @pl.when(place.odd == 1)
        def _():
            for k in (1, 2, 3):
                m_copy(k, 2).wait_send()
            m_local(2).wait()
            m_copy(2, 2).wait_recv()

        @pl.when(place.odd == 0)
        def _():
            for k in (1, 3):
                m_copy(k, 2).wait_recv()


def run_backward(grad_out, saved, *weights):
    sums = [(3 * C, C), (C, C), (C, HID), (C, HID), (1, C), (1, C)]
    *vmem_weights, _ = weights
    return pl.pallas_call(
        backward_kernel,
        grid=(2, 4),
        out_shape=[
            jax.ShapeDtypeStruct((48, 256, 128), BF16),
            jax.ShapeDtypeStruct((14, 14, 4, C3), BF16),
            jax.ShapeDtypeStruct((7, 28, 16, C), BF16),
        ],
        in_specs=[by_window(array.shape[1:], True) for array in (grad_out, *saved)]
        + [whole(w.shape) for w in vmem_weights]
        + [ANY_SPEC],
        out_specs=[whole((48, 256, 128)), ANY_SPEC, ANY_SPEC],
        scratch_shapes=[pltpu.VMEM((3 * C, NPOS), BF16)]
        + [pltpu.VMEM(shape, F32) for shape in sums]
        + [
            pltpu.VMEM((4, 49, 4, C), BF16),
            pltpu.VMEM((4, 7, 7, 16, C), BF16),
            pltpu.VMEM((4, 13, 16, C), BF16),
            pltpu.VMEM((4, 13, 16, C), BF16),
            DMA((4,)), DMA((4,)), DMA((5,)), DMA((5,)), DMA((5,)), DMA((12,)), DMA((12,)), DMA((3,)),
        ],
        compiler_params=pltpu.CompilerParams(
            vmem_limit_bytes=58 * MIB, collective_id=2, has_side_effects=True
        ),
        name="backward",
    )(grad_out, *saved, *weights)


ORDERS = (("x", "y", "z"), ("y", "z", "x"), ("z", "x", "y"))
PART = 2048


def torus(n_tm):
    return {32: (4, 2, 4), 8: (2, 2, 2), 4: (1, 2, 2), 2: (1, 2, 1)}[n_tm]


class Torus:
    def __init__(self, dims):
        self.dims = dims
        _, n_yl, n_z = dims
        m, r = lax.axis_index("tm"), lax.axis_index("rows")
        self.core = lax.rem(r, 2)
        self.sizes = {"x": dims[0], "y": 2 * n_yl, "z": n_z}
        self.at = {
            "x": m // (n_yl * n_z),
            "y": (r // 2) * n_yl + lax.rem(m // n_z, n_yl),
            "z": lax.rem(m, n_z),
        }

    def device(self, core=None, **moved):
        _, n_yl, n_z = self.dims
        at = {**self.at, **moved}
        core = self.core if core is None else core
        m = (at["x"] * n_yl + lax.rem(at["y"], n_yl)) * n_z + at["z"]
        return (m, (at["y"] // n_yl) * 2 + core)

    def partners(self, axis):
        size = self.sizes[axis]
        places = [lax.rem(self.at[axis] + j, size) for j in range(1, size)]
        return [(place, self.device(**{axis: place})) for place in places]


def sum_kernel(dims, blocks, total, core_in, acc0, acc1, acc2, in1, in2, in3, *sems):
    core_send, core_recv, rs_send, rs_recv, ag_send, ag_recv, back_send, back_recv = sems
    here = Torus(dims)
    other = here.device(core=1 - here.core)
    everyone = [other] + [dev for axis in "xyz" for _, dev in here.partners(axis)]
    barrier = pltpu.get_barrier_semaphore()
    for dev in everyone:
        pl.semaphore_signal(barrier, inc=1, device_id=dev, device_id_type=pl.DeviceIdType.MESH)
    pl.semaphore_wait(barrier, len(everyone))

    def send(src, dst, out_sem, in_sem, dev):
        copy = pltpu.make_async_remote_copy(
            src_ref=src, dst_ref=dst, send_sem=out_sem, recv_sem=in_sem,
            device_id=dev, device_id_type=pl.DeviceIdType.MESH,
        )
        copy.start()
        return copy

    def rows(start, length):
        return pl.ds(pl.multiple_of(start, length), length)

    mine = here.core * (3 * PART)
    theirs = (1 - here.core) * (3 * PART)
    copies = [
        send(
            blocks.at[rows(theirs + p * PART, PART)], core_in.at[p],
            core_send.at[p], core_recv.at[p], other,
        )
        for p in range(3)
    ]
    finished = list(copies)
    accs, ins = (acc0, acc1, acc2), (in1, in2, in3)
    in_flight = [[copy] for copy in copies]
    starts = [mine + p * PART for p in range(3)]
    lengths = [PART] * 3
    regions = [[] for _ in range(3)]
    for s in range(4):
        for p in range(3):
            for copy in in_flight[p]:
                copy.wait_recv()
            if s == 0:
                value = blocks[rows(starts[p], PART)].astype(F32) + core_in[p].astype(F32)
            else:
                axis = ORDERS[p][s - 1]
                place, length = here.at[axis], lengths[p] // here.sizes[axis]
                value = accs[s - 1][p, rows(place * length, length)].astype(F32)
                for j in range(here.sizes[axis] - 1):
                    value = value + ins[s - 1][p, j].astype(F32)
                starts[p] = starts[p] + place * length
                lengths[p] = length
            regions[p].append((starts[p], lengths[p]))
            if s == 3:
                total[rows(starts[p], lengths[p])] = value.astype(BF16)
                continue
            accs[s][p] = value.astype(BF16)
            axis = ORDERS[p][s]
            length = lengths[p] // here.sizes[axis]
            in_flight[p] = [
                send(
                    accs[s].at[p, rows(place * length, length)], ins[s].at[p, j],
                    rs_send.at[s, p, j], rs_recv.at[s, p, j], dev,
                )
                for j, (place, dev) in enumerate(here.partners(axis))
            ]
            finished += in_flight[p]

    in_flight = [[], [], []]
    for s in (3, 2, 1, 0):
        for p in range(3):
            for copy in in_flight[p]:
                copy.wait_recv()
            region = total.at[rows(*regions[p][s])]
            if s == 0:
                in_flight[p] = [send(region, region, back_send.at[p], back_recv.at[p], other)]
            else:
                in_flight[p] = [
                    send(region, region, ag_send.at[s - 1, p, j], ag_recv.at[s - 1, p, j], dev)
                    for j, (_, dev) in enumerate(here.partners(ORDERS[p][s - 1]))
                ]
            finished += in_flight[p]
    for p in range(3):
        for copy in in_flight[p]:
            copy.wait_recv()
    for copy in finished:
        copy.wait_send()


def run_sum(blocks, n_tm):
    dims = torus(n_tm)
    sizes = (dims[0], 2 * dims[1], dims[2])
    assert min(sizes) == max(sizes) or n_tm != 32
    lengths, ins = [PART], []
    if min(sizes) == max(sizes):
        for size in sizes:
            lengths.append(lengths[-1] // size)
            ins.append((3, size - 1, lengths[-1], 128))
    sem = pltpu.SemaphoreType.DMA
    most = max(sizes) - 1
    return pl.pallas_call(
        lambda *refs: sum_kernel(dims, *refs),
        out_shape=jax.ShapeDtypeStruct((6 * PART, 128), BF16),
        in_specs=[pl.BlockSpec(memory_space=pltpu.VMEM)],
        out_specs=pl.BlockSpec(memory_space=pltpu.VMEM),
        scratch_shapes=[pltpu.VMEM((3, PART, 128), BF16)]
        + [pltpu.VMEM((3, length, 128), BF16) for length in lengths[:3]]
        + [pltpu.VMEM(shape, BF16) for shape in ins]
        + [sem((3,)), sem((3,)), sem((3, 3, most)), sem((3, 3, most)), sem((3, 3, most)), sem((3, 3, most))]
        + [sem((3,)), sem((3,))],
        compiler_params=pltpu.CompilerParams(
            collective_id=0, has_side_effects=True, vmem_limit_bytes=32 * MIB
        ),
        name="sum_all",
    )(blocks.reshape(6 * PART, 128)).reshape(48, 256, 128)


def spread_kernel(blocks, qkv, proj, up, down, reduce_w, gains):
    for ref, first in ((qkv, 32), (proj, 38), (up, 16), (down, 24), (reduce_w, 0)):
        height, width = ref.shape
        for a in range(height // 256):
            for b in range(width // 128):
                part = blocks[first + a * (width // 128) + b].astype(F32)
                ref[256 * a : 256 * (a + 1), 128 * b : 128 * (b + 1)] = part
    gains[...] = blocks[40, 0:16].astype(F32)


def run_spread(blocks):
    shapes = [(C, 3 * C), (C, C), (C, HID), (HID, C), (4 * C, C3), (16, 128)]
    return pl.pallas_call(
        spread_kernel,
        out_shape=[jax.ShapeDtypeStruct(shape, F32) for shape in shapes],
        compiler_params=pltpu.CompilerParams(vmem_limit_bytes=32 * MIB),
        name="spread",
    )(blocks)


def local(
    tokens, region_ids, gain_attn, qkv_weight, proj_weight, gain_mlp, up_weight, down_weight,
    gain_merge, reduce_weight, grad_merged,
):
    n_tm = lax.axis_size("tm")
    place = lax.axis_index("rows").astype(jnp.int32).reshape(1)
    gain1, gain2, gain3 = (g.reshape(1, -1) for g in (gain_attn, gain_mlp, gain_merge))
    *saved, out_win, qkv_t, gm, edge = run_forward(
        tokens.transpose(1, 2, 0, 3), grad_merged.transpose(1, 2, 0, 3),
        region_ids.transpose(1, 0, 2), qkv_weight, proj_weight, gain1, gain2, up_weight, down_weight,
    )
    grad_out, pieces, grad_reduce, grad_gain3 = run_merge(
        out_win, edge, gm, gain3, reduce_weight, place
    )
    blocks, merged, grad_tokens = run_backward(
        grad_out, saved, qkv_t, proj_weight, gain1, gain2, up_weight, down_weight, grad_reduce,
        grad_gain3, pieces,
    )
    *grads, gains = run_spread(run_sum(blocks, n_tm))
    gains = gains.reshape(-1)
    return (
        merged.transpose(2, 0, 1, 3),
        grad_tokens.transpose(2, 0, 1, 3),
        *grads,
        gains[0:256],
        gains[256:512],
        gains[512:1536],
    )


def solution(mesh):
    placed = (
        P("tm", "rows", None, None),
        P("tm", "rows", None),
        P(), P(), P(), P(), P(), P(), P(), P(),
        P(("tm", "rows"), None, None, None),
    )
    return jax.shard_map(
        local,
        mesh=mesh,
        in_specs=placed,
        out_specs=(
            P(("tm", "rows"), None, None, None),
            P("tm", "rows", None, None),
            P(), P(), P(), P(), P(), P(), P(), P(),
        ),
        check_vma=False,
    )
```

```python
import math

import jax
import jax.numpy as jnp
from jax import lax
from jax.experimental import pallas as pl
from jax.experimental.pallas import tpu as pltpu
from jax.sharding import PartitionSpec as P

HEADS = 8
HEAD = 32
NPOS = 392
C = 256
HID = 1024
C3 = 512
EPS = 1e-05
LOG2E = 1.4426950408889634
LN2 = 0.6931471805599453
SCALE = 1.0 / math.sqrt(HEAD)
FAR = 1e30
F32 = jnp.float32
BF16 = jnp.bfloat16
MIB = 1024 * 1024


def dot_nn(left, right):
    return lax.dot_general(left, right, (((1,), (0,)), ((), ())), preferred_element_type=F32)


def dot_nt(left, right):
    return lax.dot_general(left, right, (((1,), (1,)), ((), ())), preferred_element_type=F32)


def dot_tn(left, right):
    return lax.dot_general(left, right, (((0,), (0,)), ((), ())), preferred_element_type=F32)


def norm_forward(values):
    centre = jnp.mean(values, axis=-1, keepdims=True)
    centred = values - centre
    spread = jnp.mean(centred * centred, axis=-1, keepdims=True)
    inverse = lax.rsqrt(spread + EPS)
    return centred * inverse, inverse


def norm_backward(normed, inverse, gain, incoming):
    gated = incoming * gain
    first_mean = jnp.mean(gated, axis=-1, keepdims=True)
    second_mean = jnp.mean(gated * normed, axis=-1, keepdims=True)
    return inverse * (gated - first_mean - normed * second_mean)


def gelu_and_slope(up):
    size = jnp.abs(up)
    base = 1.0 + (0.3275911 * 0.7071067811865476) * size
    guess = pl.reciprocal(base, approx=True)
    t = guess * (2.0 - base * guess)
    bell = jnp.exp2((-0.5 * LOG2E) * (up * up))
    series = 0.5 * 1.061405429 * t - 0.5 * 1.453152027
    series = series * t + 0.5 * 1.421413741
    series = series * t - 0.5 * 0.284496736
    series = series * t + 0.5 * 0.254829592
    tail = series * t * bell
    cdf = jnp.where(up >= 0.0, 1.0 - tail, tail)
    return up * cdf, cdf + up * (bell * 0.3989422804014327)


MESH = pl.DeviceIdType.MESH
RUNS = ((3, 0, 7), (10, 7, 7), (17, 14, 7), (24, 21, 4), (0, 25, 3))


def runs_of(wc):
    return range(wc, wc + 1) if wc < 3 else range(3, 5)


class Place:
    def __init__(self):
        self.m, self.r = lax.axis_index("tm"), lax.axis_index("rows")
        self.n_tm = lax.axis_size("tm")
        self.odd = lax.rem(self.r, 2)
        self.edge = jnp.where(self.r == 0, 1, 0)

    def at(self, dm, dr):
        return (lax.rem(self.m + dm + self.n_tm, self.n_tm), lax.rem(self.r + dr + 4, 4))

    def across(self):
        return (self.m, 3 - self.r)

    def holder(self, k):
        r = lax.rem(self.r - k + 4, 4)
        return self.at(-self.edge, k), self.at(jnp.where(r == 0, 1, 0), -k)

    def owner(self, k):
        r = lax.rem(self.r + k, 4)
        return self.at(jnp.where(r == 0, 1, 0), k), self.at(-self.edge, -k)

    def greet(self, sources, extra):
        barrier = pltpu.get_barrier_semaphore()
        for dev in sources:
            pl.semaphore_signal(barrier, inc=1, device_id=dev, device_id_type=MESH)

        @pl.when(self.r == 0)
        def _():
            pl.semaphore_signal(barrier, inc=1, device_id=extra, device_id_type=MESH)
            pl.semaphore_wait(barrier, len(sources) + 1)

        @pl.when(self.r != 0)
        def _():
            pl.semaphore_wait(barrier, len(sources))


def remote(src, dst, sems, n, dev):
    return pltpu.make_async_remote_copy(
        src_ref=src, dst_ref=dst, send_sem=sems[0].at[n], recv_sem=sems[1].at[n],
        device_id=dev, device_id_type=MESH,
    )


def pack(quarters):
    padded = jnp.concatenate([quarters, jnp.zeros((3, 4, C), F32)], axis=0).reshape(13, 4, 4, C)
    return jnp.concatenate([padded[:, n] for n in range(4)], axis=1).astype(BF16)


def unpack(packed):
    wide = packed.astype(F32)
    parts = [wide[:, 4 * n : 4 * (n + 1)].reshape(13, 1, 4, C) for n in range(4)]
    return jnp.concatenate(parts, axis=1).reshape(52, 4, C)[0:49]


def mask_rows(ids, pos, tw, wc):
    lane = lax.broadcasted_iota(jnp.int32, (1, 28), 1)
    first = lane == 7 * wc
    here = (lane >= 7 * wc) & (lane < 7 * wc + 7)
    frames = ids[0, pl.ds(pl.multiple_of(8 * tw, 8), 8), :]
    rows = ids[:, pl.ds(pl.multiple_of(8 * tw, 8), 8), :]

    def count(bits, kept):
        kept_bits = jnp.where(kept, bits.astype(F32), 0.0)
        return jnp.sum(jnp.sum(kept_bits, axis=0, keepdims=True), axis=1, keepdims=True)

    past = [
        count((frames >> 2) & 1, first),
        count(jnp.concatenate([(rows[i, 0:1] >> 1) & 1 for i in range(7)], axis=0), first),
        count(frames[0:1] & 1, here),
    ]
    bits = [
        jnp.where(pos[n : n + 1] >= extent - past[n], 1.0, 0.0)
        for n, extent in enumerate((8.0, 7.0, 7.0))
    ]
    none = [jnp.zeros((10, NPOS), F32)]
    keys = jnp.concatenate([v for b in bits for v in (b, 1.0 - b)] + none, axis=0)
    queries = jnp.concatenate([v for b in bits for v in (1.0 - b, b)] + none, axis=0) * -FAR
    return keys.astype(BF16), queries.astype(BF16)


def forward_kernel(
    tokens, gm, ids, pos, qkv_w, proj, gain1, gain2, up_w, down_w,
    x_out, qkv_out, exp_out, inv_out, att_out, hid_out, act_out, slope_out, out_out, qkv_t,
    gm_in, edge_in,
    tok, x_now, pack_t, halo_t, edge_out, own_sem, row_out, row_in, t_out, t_in, gm_out_sem, gm_in_sem,
    gm_own, edge_out_sem, edge_in_sem,
):
    tw, wc = pl.program_id(0), pl.program_id(1)
    place = Place()
    row_sems, t_sems = (row_out, row_in), (t_out, t_in)
    gm_sems, edge_sems = (gm_out_sem, gm_in_sem), (edge_out_sem, edge_in_sem)

    def own_copies():
        return [
            pltpu.make_async_copy(
                tokens.at[3:7, a : a + n], tok.at[0:4, b : b + n], own_sem.at[at]
            )
            for at, (a, b, n) in enumerate(((3, 0, 25), (0, 25, 3)))
        ]

    def row_copy(at):
        a, b, n = RUNS[at]
        return remote(
            tokens.at[0:3, a : a + n], tok.at[4:7, b : b + n], row_sems, at, place.at(0, -1)
        )

    def t_copy():
        return remote(pack_t.at[wc], halo_t.at[wc], t_sems, wc, place.at(-1, 0))

    def gm_copy(k, part):
        dev, _ = place.holder(k)
        band = lax.rem(place.r + k, 4)
        first = lax.rem(4 * band + 1 - band // 2 + 2 * part, 14)
        slot = lax.rem(place.r + 3, 4)
        src, dst = gm.at[pl.ds(first, 2)], gm_in.at[slot, 2 * part : 2 * part + 2]
        return remote(src, dst, gm_sems, 2 * k + part, dev)

    def gm_local(part):
        band = place.r
        first = lax.rem(4 * band + 1 - band // 2 + 2 * part, 14)
        slot = lax.rem(place.r + 3, 4)
        return pltpu.make_async_copy(
            gm.at[pl.ds(first, 2)], gm_in.at[slot, 2 * part : 2 * part + 2], gm_own.at[part]
        )

    def edge_copy(half):
        return remote(edge_out.at[half], edge_in.at[half], edge_sems, half, place.across())

    @pl.when((tw == 0) & (wc == 0))
    def _():
        for copy in own_copies():
            copy.start()
        sources = [place.at(0, 1), place.at(1, 0), place.across()]
        place.greet(sources + [place.holder(k)[1] for k in (1, 2, 3)], place.holder(0)[1])
        for at in range(5):
            row_copy(at).start()
        qkv_t[...] = qkv_w[...].astype(F32).T.astype(BF16)
        for copy in own_copies():
            copy.wait()

    @pl.when((tw == 0) & (wc == 1))
    def _():
        for k in (1, 2, 3):
            for part in range(2):
                gm_copy(k, part).start()

        @pl.when(place.r == 0)
        def _():
            for part in range(2):
                gm_copy(0, part).start()

        @pl.when(place.r != 0)
        def _():
            for part in range(2):
                gm_local(part).start()

    for window in range(4):

        @pl.when((tw == 0) & (wc == window))
        def _(window=window):
            for at in runs_of(window):
                row_copy(at).wait_recv()

    @pl.when(tw == 0)
    def _():
        block = tok[:, pl.ds(7 * wc, 7)].astype(F32).reshape(49, 16, C)
        pack_t[wc] = pack(block[:, 0:4])
        t_copy().start()
        x_now[...] = block[:, 4:12]

    @pl.when(tw == 1)
    def _():
        t_copy().wait_recv()
        block = tok[:, pl.ds(7 * wc, 7)].astype(F32).reshape(49, 16, C)
        x_now[...] = jnp.concatenate([block[:, 12:16], unpack(halo_t[wc])], axis=1)

    x = x_now[...].reshape(NPOS, C)
    x_out[0] = x.astype(BF16)
    mask_k, mask_q = mask_rows(ids, pos, tw, wc)
    normed, _ = norm_forward(x)
    first_in = (normed * gain1[...]).astype(BF16)
    rows = dot_nt(qkv_t[...], first_in)
    qkv_out[0, 0:C] = (rows[0:C] * (SCALE * LOG2E)).astype(BF16)
    qkv_out[0, C:] = rows[C:].astype(BF16)
    for h in range(HEADS):
        here = slice(HEAD * h, HEAD * (h + 1))
        q = jnp.concatenate([qkv_out[0, HEAD * h : HEAD * (h + 1)], mask_q], axis=0)
        k = jnp.concatenate([qkv_out[0, C + HEAD * h : C + HEAD * (h + 1)], mask_k], axis=0)
        v = qkv_out[0, 2 * C + HEAD * h : 2 * C + HEAD * (h + 1)]
        scores = dot_tn(k, q)
        top = jnp.max(scores, axis=0, keepdims=True)
        expon = jnp.exp2(scores - top)
        inverse = 1.0 / jnp.sum(expon, axis=0, keepdims=True)
        expon = expon.astype(BF16)
        exp_out[0, h] = expon
        inv_out[0, h : h + 1] = inverse
        att_out[0, here] = (dot_nn(v, expon) * inverse).astype(BF16)
    hidden = (x + dot_tn(att_out[0], proj[...])).astype(BF16)
    hid_out[0] = hidden
    hidden = hidden.astype(F32)
    normed, _ = norm_forward(hidden)
    second_in = (normed * gain2[...]).astype(BF16)
    result = hidden
    for part in range(4):
        cols = slice(256 * part, 256 * (part + 1))
        act, slope = gelu_and_slope(dot_nn(second_in, up_w[:, cols]))
        act = act.astype(BF16)
        act_out[0, :, cols] = act
        slope_out[0, :, cols] = slope.astype(BF16)
        result = result + dot_nn(act, down_w[cols])
    out_out[0] = result.astype(BF16)
    edge = jnp.where(place.odd == 1, result[336:392], result[0:56])
    edge_out[tw, wc] = edge.astype(BF16)

    @pl.when((tw == 0) & (wc == 3))
    def _():
        edge_copy(0).start()

    @pl.when((tw == 1) & (wc == 3))
    def _():
        edge_copy(1).start()
        for at in range(5):
            row_copy(at).wait_send()
        for n in range(4):
            remote(pack_t.at[n], halo_t.at[n], t_sems, n, place.at(-1, 0)).wait_send()
        for k in (1, 2, 3):
            for part in range(2):
                gm_copy(k, part).wait()

        @pl.when(place.r == 0)
        def _():
            for part in range(2):
                gm_copy(0, part).wait()

        @pl.when(place.r != 0)
        def _():
            for part in range(2):
                gm_local(part).wait()

        for half in range(2):
            edge_copy(half).wait()


def whole(shape):
    return pl.BlockSpec(shape, lambda *_: (0,) * len(shape))


def by_window(shape, backwards=False):
    def index(tw, wc):
        return (4 * (1 - tw if backwards else tw) + wc,) + (0,) * len(shape)

    return pl.BlockSpec((1,) + shape, index)


SMEM_SPEC = pl.BlockSpec(memory_space=pltpu.SMEM)
ANY_SPEC = pl.BlockSpec(memory_space=pl.ANY)
DMA = pltpu.SemaphoreType.DMA


def positions():
    at = jnp.arange(NPOS)
    rows = [at % 8, at // 56, (at // 8) % 7]
    return jnp.concatenate([jnp.stack(rows), jnp.zeros((5, NPOS), at.dtype)]).astype(F32)


def run_forward(tokens, gm, ids, qkv_w, proj, gain1, gain2, up_w, down_w):
    saved = [
        ((NPOS, C), BF16),
        ((3 * C, NPOS), BF16),
        ((HEADS, NPOS, NPOS), BF16),
        ((HEADS, NPOS), F32),
        ((C, NPOS), BF16),
        ((NPOS, C), BF16),
        ((NPOS, HID), BF16),
        ((NPOS, HID), BF16),
        ((NPOS, C), BF16),
    ]
    pos = positions()
    return pl.pallas_call(
        forward_kernel,
        grid=(2, 4),
        out_shape=[jax.ShapeDtypeStruct((8,) + shape, kind) for shape, kind in saved]
        + [
            jax.ShapeDtypeStruct((3 * C, C), BF16),
            jax.ShapeDtypeStruct((4, 4, 14, 4, C3), BF16),
            jax.ShapeDtypeStruct((2, 4, 56, C), BF16),
        ],
        in_specs=[ANY_SPEC, ANY_SPEC, whole(ids.shape), whole(pos.shape)]
        + [whole(w.shape) for w in (qkv_w, proj, gain1, gain2, up_w, down_w)],
        out_specs=[by_window(shape) for shape, _ in saved]
        + [whole((3 * C, C)), ANY_SPEC, ANY_SPEC],
        scratch_shapes=[
            pltpu.VMEM((7, 28, 16, C), BF16),
            pltpu.VMEM((49, 8, C), F32),
            pltpu.VMEM((4, 13, 16, C), BF16),
            pltpu.VMEM((4, 13, 16, C), BF16),
            pltpu.VMEM((2, 4, 56, C), BF16),
            DMA((2,)), DMA((5,)), DMA((5,)), DMA((4,)), DMA((4,)), DMA((8,)), DMA((8,)),
            DMA((2,)), DMA((2,)), DMA((2,)),
        ],
        compiler_params=pltpu.CompilerParams(
            vmem_limit_bytes=58 * MIB, collective_id=1, has_side_effects=True
        ),
        name="forward",
    )(tokens, gm, ids, pos, qkv_w, proj, gain1, gain2, up_w, down_w)


def to_blocks(blocks, first, values):
    height, width = values.shape
    for a in range(height // 256):
        for b in range(width // 128):
            part = values[256 * a : 256 * (a + 1), 128 * b : 128 * (b + 1)]
            blocks[first + a * (width // 128) + b] = part.astype(BF16)


def store_blocks(flat, first, values):
    height, width = values.shape
    for a in range(height // 256):
        for b in range(width // 128):
            at = 256 * (first + a * (width // 128) + b)
            part = values[256 * a : 256 * (a + 1), 128 * b : 128 * (b + 1)]
            flat[at : at + 256] = part.astype(BF16)


def column_runs(wc):
    if wc < 3:
        return [(7 * wc + 3, 0, 7)]
    return [(24, 0, 4), (0, 4, 7)]


def merge_kernel(
    out_win, edge, gm, gain3, reduce_w, place,
    grad_out, m_all, reduce_blocks, grad_gain,
    rows, third_all, gm_rows, grad_reduce,
):
    tw = pl.program_id(0)
    r = place[0]
    odd = lax.rem(r, 2)

    @pl.when(tw == 0)
    def _():
        grad_reduce[...] = jnp.zeros_like(grad_reduce)
        grad_gain[...] = jnp.zeros_like(grad_gain)

    for wc in range(4):
        block = out_win[wc].astype(F32).reshape(7, 7, 8, C)
        strip = edge[0, wc].astype(F32).reshape(7, 8, C)
        for start, first, last in column_runs(wc):
            cols = slice(start, start + last - first)
            rows[pl.ds(1 - odd, 7), cols] = block[:, first:last]
            rows[7 * odd, cols] = strip[first:last]

    gain = gain3[...]
    for a in range(4):
        upper = rows[2 * a].reshape(14, 2, 8, C)
        lower = rows[2 * a + 1].reshape(14, 2, 8, C)
        joined = jnp.concatenate(
            [upper[:, 0], lower[:, 0], upper[:, 1], lower[:, 1]], axis=-1
        ).reshape(112, 4 * C)
        normed, inverse = norm_forward(joined)
        third = normed * gain
        merged = dot_nn(third.astype(BF16), reduce_w[...])
        merged = merged.reshape(14, 8, C3)
        m_all[0, a] = merged[:, 0:4].astype(BF16)
        m_all[1, a] = merged[:, 4:8].astype(BF16)
        grads = jnp.concatenate([gm[0, a].astype(F32), gm[1, a].astype(F32)], axis=1)
        grads = grads.reshape(112, C3).astype(BF16)
        gz = dot_nt(grads, reduce_w[...])
        gz_sum = jnp.sum(gz * normed, axis=0, keepdims=True)
        if a == 0:
            counted = jnp.where((odd == 0) & (tw == 1), 0.0, 1.0)
        elif a == 3:
            counted = jnp.where((odd == 1) & (tw == 0), 0.0, 1.0)
        else:
            counted = None
        if counted is not None:
            third = third * counted
            gz_sum = gz_sum * counted
        grad_gain[...] += gz_sum
        third_all[112 * a : 112 * (a + 1)] = third.astype(BF16)
        gm_rows[112 * a : 112 * (a + 1)] = grads
        back = norm_backward(normed, inverse, gain, gz).reshape(14, 8, 4 * C)
        pieces = [back[:, :, C * n : C * (n + 1)].reshape(14, 1, 8, C) for n in range(4)]
        rows[2 * a] = jnp.concatenate([pieces[0], pieces[2]], axis=1).reshape(28, 8, C)
        rows[2 * a + 1] = jnp.concatenate([pieces[1], pieces[3]], axis=1).reshape(28, 8, C)
    grad_reduce[...] += dot_tn(third_all[...], gm_rows[...])
    for wc in range(4):
        runs = [
            rows[pl.ds(1 - odd, 7), start : start + last - first]
            for start, first, last in column_runs(wc)
        ]
        block = runs[0] if len(runs) == 1 else jnp.concatenate(runs, axis=1)
        grad_out[wc] = block.reshape(NPOS, C).astype(BF16)

    @pl.when(tw == 1)
    def _():
        to_blocks(reduce_blocks, 0, grad_reduce)


def run_merge(out_win, edge, gm, gain3, reduce_w, place):
    def by_tw(shape):
        return pl.BlockSpec(shape, lambda tw: (tw,) + (0,) * (len(shape) - 1))

    pieces = (2, 4, 14, 4, C3)
    return pl.pallas_call(
        merge_kernel,
        grid=(2,),
        out_shape=[
            jax.ShapeDtypeStruct((8, NPOS, C), BF16),
            jax.ShapeDtypeStruct((4, 4, 14, 4, C3), BF16),
            jax.ShapeDtypeStruct((16, 256, 128), BF16),
            jax.ShapeDtypeStruct((1, 4 * C), F32),
        ],
        in_specs=[by_tw((4, NPOS, C)), by_tw((1, 4, 56, C)), by_tw(pieces)]
        + [whole((1, 4 * C)), whole((4 * C, C3)), SMEM_SPEC],
        out_specs=[by_tw((4, NPOS, C)), by_tw(pieces), whole((16, 256, 128)), whole((1, 4 * C))],
        scratch_shapes=[
            pltpu.VMEM((8, 28, 8, C), F32),
            pltpu.VMEM((448, 4 * C), BF16),
            pltpu.VMEM((448, C3), BF16),
            pltpu.VMEM((4 * C, C3), F32),
        ],
        compiler_params=pltpu.CompilerParams(vmem_limit_bytes=58 * MIB),
        name="merge",
    )(out_win, edge, gm, gain3, reduce_w, place)


ORDERS = (("x", "y", "z"), ("y", "z", "x"), ("z", "x", "y"))


def torus(n_tm):
    return {32: (4, 2, 4), 4: (2, 1, 2)}[n_tm]


class Torus:
    def __init__(self, dims):
        self.dims = dims
        _, n_yl, n_z = dims
        m, r = lax.axis_index("tm"), lax.axis_index("rows")
        self.core = lax.rem(r, 2)
        self.size = dims[0]
        self.at = {
            "x": m // (n_yl * n_z),
            "y": (r // 2) * n_yl + lax.rem(m // n_z, n_yl),
            "z": lax.rem(m, n_z),
        }

    def device(self, core=None, **moved):
        _, n_yl, n_z = self.dims
        at = {**self.at, **moved}
        core = self.core if core is None else core
        m = (at["x"] * n_yl + lax.rem(at["y"], n_yl)) * n_z + at["z"]
        return (m, (at["y"] // n_yl) * 2 + core)

    def partners(self, axis):
        places = [lax.rem(self.at[axis] + j, self.size) for j in range(1, self.size)]
        return [(place, self.device(**{axis: place})) for place in places]

    def other(self):
        return self.device(core=1 - self.core)

    def everyone(self):
        return [self.other()] + [dev for axis in "xyz" for _, dev in self.partners(axis)]


def at_rows(start, length):
    return pl.ds(pl.multiple_of(start, 16), length)


class Sum:
    def __init__(self, here, lengths, whole_last, source, total, base, scratch):
        self.here, self.lengths, self.whole_last = here, lengths, whole_last
        self.source, self.total, self.base = source, total, base
        self.core_in, *rest = scratch
        self.accs, self.ins = rest[0:3], rest[3:6]
        self.core_sems, self.rs_sems, self.ag_sems, self.back_sems = (
            tuple(rest[6 + 2 * n : 8 + 2 * n]) for n in range(4)
        )

    @staticmethod
    def scratch(size, lengths, whole_last):
        most, length = max(lengths), max(lengths)
        shapes = [(3, most, 128)]
        accs, ins = [], []
        for s in range(3):
            accs.append((3, length, 128))
            length = length if s == 2 and whole_last else length // size
            ins.append((3, size - 1, length, 128))
        sems = [(3,), (3,), (9 * (size - 1),), (9 * (size - 1),), (9 * (size - 1),), (9 * (size - 1),), (3,), (3,)]
        return [pltpu.VMEM(shape, BF16) for shape in shapes + accs + ins] + [DMA(n) for n in sems]

    def half(self, core, p):
        return core * sum(self.lengths) + sum(self.lengths[:p])

    def piece(self, p, s):
        start, length = self.half(self.here.core, p), self.lengths[p]
        for n in range(s):
            if not (n == 2 and self.whole_last):
                length = length // self.here.size
                start = start + self.here.at[ORDERS[p][n]] * length
        return start, length

    def core_copy(self, p):
        start = self.half(1 - self.here.core, p)
        return remote(
            self.source.at[at_rows(start, self.lengths[p])],
            self.core_in.at[p, 0 : self.lengths[p]],
            self.core_sems, p, self.here.other(),
        )

    def rs_copies(self, p, s):
        _, length = self.piece(p, s)
        whole_piece = s == 3 and self.whole_last
        return [
            remote(
                self.accs[s - 1].at[p, 0:length]
                if whole_piece
                else self.accs[s - 1].at[p, at_rows(place * length, length)],
                self.ins[s - 1].at[p, j, 0:length],
                self.rs_sems, (3 * (s - 1) + p) * (self.here.size - 1) + j, dev,
            )
            for j, (place, dev) in enumerate(self.here.partners(ORDERS[p][s - 1]))
        ]

    def ag_copies(self, p, s):
        start, length = self.piece(p, s)
        region = self.total.at[at_rows(self.base + start, length)]
        return [
            remote(region, region, self.ag_sems, (3 * (s - 1) + p) * (self.here.size - 1) + j, dev)
            for j, (_, dev) in enumerate(self.here.partners(ORDERS[p][s - 1]))
        ]

    def back_copy(self, p):
        start, length = self.piece(p, 0)
        region = self.total.at[at_rows(self.base + start, length)]
        return remote(region, region, self.back_sems, p, self.here.other())

    def start(self):
        for p in range(3):
            self.core_copy(p).start()

    def reduce(self, s):
        for p in range(3):
            start, length = self.piece(p, s)
            if s == 0:
                self.core_copy(p).wait_recv()
                value = self.source[at_rows(start, length)].astype(F32)
                value = value + self.core_in[p, 0:length].astype(F32)
            else:
                for copy in self.rs_copies(p, s):
                    copy.wait_recv()
                if s == 3 and self.whole_last:
                    value = self.accs[2][p, 0:length].astype(F32)
                else:
                    place = self.here.at[ORDERS[p][s - 1]]
                    value = self.accs[s - 1][p, at_rows(place * length, length)].astype(F32)
                for j in range(self.here.size - 1):
                    value = value + self.ins[s - 1][p, j, 0:length].astype(F32)
            if s < 3:
                self.accs[s][p, 0:length] = value.astype(BF16)
                for copy in self.rs_copies(p, s + 1):
                    copy.start()
            else:
                self.total[at_rows(self.base + start, length)] = value.astype(BF16)
                for copy in self.ag_copies(p, 2 if self.whole_last else 3):
                    copy.start()

    def gather(self, s):
        for p in range(3):
            for copy in self.ag_copies(p, s):
                copy.wait_recv()
            for copy in self.ag_copies(p, s - 1) if s > 1 else [self.back_copy(p)]:
                copy.start()

    def finish(self):
        for p in range(3):
            self.back_copy(p).wait()
            self.core_copy(p).wait_send()
            for s in (1, 2, 3):
                for copy in self.rs_copies(p, s):
                    copy.wait_send()
                if s < 3 or not self.whole_last:
                    for copy in self.ag_copies(p, s):
                        copy.wait_send()


EARLY, LATE = (2048, 2048, 1024), (512, 256, 256)
EARLY_ROWS, LATE_ROWS = 2 * sum(EARLY), 2 * sum(LATE)


def backward_kernel(
    dims, grad_out, att_a, hid_in, act_in, slope_in, x_in, qkv_in, exp_in, inv_in, att_in,
    qkv_t, proj, gain1, gain2, up_w, down_w, reduce_blocks, grad_gain3, pieces,
    totals, merged, grad_tokens,
    grad_hidden_all, grad_att_all, grad_rows_t, grad_qkv_t, grad_proj, grad_up, grad_down_t,
    grad_gain1, grad_gain2, late, final, pack_t, halo_t, early_blocks, late_blocks, total,
    t_out, t_in, row_out, row_in, own_sem, m_out, m_in, m_own, total_sem, *sum_scratch,
):
    step = pl.program_id(0)
    tw, wc = 1 - lax.rem(step, 8) // 4, lax.rem(step, 4)
    window = 4 * tw + wc
    first_phase, second_phase = step < 8, step >= 8
    place, here = Place(), Torus(dims)
    t_sems, row_sems, m_sems = (t_out, t_in), (row_out, row_in), (m_out, m_in)
    half = len(sum_scratch) // 2
    early_sum = Sum(here, EARLY, False, early_blocks, total, 0, sum_scratch[:half])
    late_sum = Sum(here, LATE, True, late_blocks, total, EARLY_ROWS, sum_scratch[half:])

    def m_ends(k, n):
        c = lax.rem(place.r + k + 3, 4)
        start = 4 * place.r + 1 - place.r // 2
        first = (1 - place.odd, 3 - place.odd, 3)[n]
        count = (2, 1, 1)[n]
        return (
            pieces.at[c, pl.ds(first, count)],
            merged.at[pl.ds(lax.rem(start + first, 14), count)],
        )

    def m_copy(k, n):
        return remote(*m_ends(k, n), m_sems, 3 * k + n, place.owner(k)[0])

    def m_local(n):
        return pltpu.make_async_copy(*m_ends(0, n), m_own.at[n])

    def m_each(act_remote, act_local):
        for k in (1, 2, 3):
            act_remote(k, 0)
            act_remote(k, 1)

        @pl.when(place.r == 0)
        def _():
            act_remote(0, 0)
            act_remote(0, 1)

        @pl.when(place.r != 0)
        def _():
            act_local(0)
            act_local(1)

    def t_copy(n):
        return remote(pack_t.at[n], halo_t.at[n], t_sems, n, place.at(1, 0))

    def row_copy(at):
        a, b, n = RUNS[at]
        part, first = (at, 0) if at < 3 else (3, b - 21)
        return remote(
            final.at[part, 4:7, first : first + n], grad_tokens.at[0:3, a : a + n],
            row_sems, at, place.at(0, 1),
        )

    def own_copy(at):
        a, b, n = RUNS[at]
        part, first = (at, 0) if at < 3 else (3, b - 21)
        return pltpu.make_async_copy(
            final.at[part, 0:4, first : first + n], grad_tokens.at[3:7, a : a + n], own_sem.at[at]
        )

    def total_copy(n):
        start, length = ((0, EARLY_ROWS), (EARLY_ROWS, LATE_ROWS))[n]
        region = pl.ds(start, length)
        return pltpu.make_async_copy(total.at[region], totals.at[region], total_sem.at[n])

    @pl.when(step == 0)
    def _():
        for ref in (grad_qkv_t, grad_proj, grad_up, grad_down_t, grad_gain1, grad_gain2):
            ref[...] = jnp.zeros_like(ref)
        sources = [place.at(0, -1), place.at(-1, 0)] + [place.owner(k)[1] for k in (1, 2, 3)]
        place.greet(sources + here.everyone(), place.owner(0)[1])

    @pl.when(step == 1)
    def _():
        m_each(lambda k, n: m_copy(k, n).start(), lambda n: m_local(n).start())

        @pl.when(place.odd == 1)
        def _():
            for k in (1, 2, 3):
                m_copy(k, 2).start()
            m_local(2).start()

    @pl.when(first_phase)
    def _():
        grad_rows = grad_out[0]
        normed2, inverse2 = norm_forward(hid_in[0].astype(F32))
        second_in = (normed2 * gain2[...]).astype(BF16)
        grad_second = jnp.zeros((NPOS, C), F32)
        for part in range(4):
            cols = slice(256 * part, 256 * (part + 1))
            grad_down_t[:, cols] += dot_tn(grad_rows, act_in[0, :, cols])
            grad_act = dot_nt(grad_rows, down_w[cols])
            grad_up_in = (grad_act * slope_in[0, :, cols].astype(F32)).astype(BF16)
            grad_up[:, cols] += dot_tn(second_in, grad_up_in)
            grad_second = grad_second + dot_nt(grad_up_in, up_w[:, cols])
        grad_gain2[...] += jnp.sum(grad_second * normed2, axis=0, keepdims=True)
        back = norm_backward(normed2, inverse2, gain2[...], grad_second)
        grad_hidden = grad_rows.astype(F32) + back
        grad_hidden_all[window] = grad_hidden
        grad_hidden_b = grad_hidden.astype(BF16)
        grad_proj[...] += dot_nn(att_a[0], grad_hidden_b)
        grad_att_all[window] = dot_nt(proj[...], grad_hidden_b).astype(BF16)

    @pl.when(step == 7)
    def _():
        flat = early_blocks
        store_blocks(flat, 16, grad_up[...])
        store_blocks(flat, 24, grad_down_t[...].T)
        store_blocks(flat, 32, grad_proj[...])
        flat[0:4096] = reduce_blocks[...].reshape(4096, 128)
        rows = [grad_gain2[:, 0:128], grad_gain2[:, 128:256]]
        rows += [grad_gain3[:, 128 * n : 128 * (n + 1)] for n in range(8)]
        rows.append(jnp.zeros((6, 128), F32))
        flat[34 * 256 : 34 * 256 + 16] = jnp.concatenate(rows, axis=0).astype(BF16)
        flat[34 * 256 + 16 :] = jnp.zeros((EARLY_ROWS - 34 * 256 - 16, 128), BF16)
        early_sum.start()

    for at, run in (
        (9, lambda: early_sum.reduce(0)),
        (11, lambda: early_sum.reduce(1)),
        (12, lambda: early_sum.reduce(2)),
        (13, lambda: early_sum.reduce(3)),
        (14, lambda: early_sum.gather(3)),
        (15, lambda: early_sum.gather(2)),
    ):
        pl.when(step == at)(run)

    @pl.when(second_phase)
    def _():
        for h in range(HEADS):
            at_q = slice(HEAD * h, HEAD * (h + 1))
            at_k = slice(C + HEAD * h, C + HEAD * (h + 1))
            at_v = slice(2 * C + HEAD * h, 2 * C + HEAD * (h + 1))
            expon = exp_in[0, h]
            incoming = grad_att_all[window, at_q].astype(F32) * inv_in[0, h : h + 1]
            incoming = incoming.astype(BF16)
            inner = incoming.astype(F32) * att_in[0, at_q].astype(F32)
            inner = jnp.sum(inner, axis=0, keepdims=True)
            grad_probs = dot_tn(qkv_in[0, at_v], incoming)
            grad_scores = (expon.astype(F32) * (grad_probs - inner)).astype(BF16)
            grad_rows_t[at_q] = (dot_nn(qkv_in[0, at_k], grad_scores) * SCALE).astype(BF16)
            grad_rows_t[at_k] = (dot_nt(qkv_in[0, at_q], grad_scores) * LN2).astype(BF16)
            grad_rows_t[at_v] = dot_nt(incoming, expon).astype(BF16)
        normed1, inverse1 = norm_forward(x_in[0].astype(F32))
        first_in = (normed1 * gain1[...]).astype(BF16)
        grad_qkv_t[...] += dot_nn(grad_rows_t[...], first_in)
        grad_first = dot_tn(grad_rows_t[...], qkv_t[...])
        grad_gain1[...] += jnp.sum(grad_first * normed1, axis=0, keepdims=True)
        back = norm_backward(normed1, inverse1, gain1[...], grad_first)
        block = (grad_hidden_all[window] + back).reshape(49, 8, C)

        @pl.when(tw == 1)
        def _():
            late[wc] = block[:, 0:4].astype(BF16)
            pack_t[wc] = pack(block[:, 4:8])
            t_copy(wc).start()

        @pl.when(tw == 0)
        def _():
            t_copy(wc).wait_recv()
            frames = jnp.concatenate([unpack(halo_t[wc]), block, late[wc].astype(F32)], axis=1)
            final[wc] = frames.astype(BF16).reshape(7, 7, 16, C)

    for part in range(4):

        @pl.when(step == 12 + part)
        def _(part=part):
            for at in runs_of(part):
                row_copy(at).start()
                own_copy(at).start()

    @pl.when(step == 15)
    def _():
        store_blocks(late_blocks, 0, grad_qkv_t[...].T)
        rows = [grad_gain1[:, 0:128], grad_gain1[:, 128:256], jnp.zeros((14, 128), F32)]
        late_blocks[1536:1552] = jnp.concatenate(rows, axis=0).astype(BF16)
        late_blocks[1552:] = jnp.zeros((LATE_ROWS - 1552, 128), BF16)
        late_sum.start()
        late_sum.reduce(0)
        early_sum.gather(1)
        late_sum.reduce(1)
        late_sum.reduce(2)
        late_sum.reduce(3)
        early_sum.finish()
        total_copy(0).start()
        late_sum.gather(2)
        late_sum.gather(1)
        for at in range(5):
            row_copy(at).wait()
            own_copy(at).wait()
        for n in range(4):
            t_copy(n).wait_send()
        m_each(lambda k, n: m_copy(k, n).wait(), lambda n: m_local(n).wait())

        @pl.when(place.odd == 1)
        def _():
            for k in (1, 2, 3):
                m_copy(k, 2).wait_send()
            m_local(2).wait()
            m_copy(2, 2).wait_recv()

        @pl.when(place.odd == 0)
        def _():
            for k in (1, 3):
                m_copy(k, 2).wait_recv()

        late_sum.finish()
        total_copy(1).start()
        total_copy(0).wait()
        total_copy(1).wait()


def run_backward(n_tm, grad_out, saved, *weights):
    sums = [(3 * C, C), (C, C), (C, HID), (C, HID), (1, C), (1, C)]
    dims = torus(n_tm)
    x, qkv, expon, inverse, att, hid, act, slope = saved
    *vmem_weights, _ = weights

    def window(step):
        return 4 * (1 - lax.rem(step, 8) // 4) + lax.rem(step, 4)

    def in_first(array):
        shape = array.shape[1:]
        return pl.BlockSpec(
            (1,) + shape, lambda s: (window(jnp.minimum(s, 7)),) + (0,) * len(shape)
        )

    def in_second(array):
        shape = array.shape[1:]
        return pl.BlockSpec(
            (1,) + shape, lambda s: (window(jnp.maximum(s - 8, 0)),) + (0,) * len(shape)
        )

    first, second = (grad_out, att, hid, act, slope), (x, qkv, expon, inverse, att)
    return pl.pallas_call(
        lambda *refs: backward_kernel(dims, *refs),
        grid=(16,),
        out_shape=[
            jax.ShapeDtypeStruct((EARLY_ROWS + LATE_ROWS, 128), BF16),
            jax.ShapeDtypeStruct((14, 14, 4, C3), BF16),
            jax.ShapeDtypeStruct((7, 28, 16, C), BF16),
        ],
        in_specs=[in_first(array) for array in first]
        + [in_second(array) for array in second]
        + [whole(w.shape) for w in vmem_weights]
        + [ANY_SPEC],
        out_specs=[ANY_SPEC] * 3,
        scratch_shapes=[
            pltpu.VMEM((8, NPOS, C), F32),
            pltpu.VMEM((8, C, NPOS), BF16),
            pltpu.VMEM((3 * C, NPOS), BF16),
        ]
        + [pltpu.VMEM(shape, F32) for shape in sums]
        + [
            pltpu.VMEM((4, 49, 4, C), BF16),
            pltpu.VMEM((4, 7, 7, 16, C), BF16),
            pltpu.VMEM((4, 13, 16, C), BF16),
            pltpu.VMEM((4, 13, 16, C), BF16),
            pltpu.VMEM((EARLY_ROWS, 128), BF16),
            pltpu.VMEM((LATE_ROWS, 128), BF16),
            pltpu.VMEM((EARLY_ROWS + LATE_ROWS, 128), BF16),
            DMA((4,)), DMA((4,)), DMA((5,)), DMA((5,)), DMA((5,)), DMA((12,)), DMA((12,)), DMA((3,)),
            DMA((2,)),
        ]
        + Sum.scratch(dims[0], EARLY, False)
        + Sum.scratch(dims[0], LATE, True),
        compiler_params=pltpu.CompilerParams(
            vmem_limit_bytes=58 * MIB, collective_id=2, has_side_effects=True
        ),
        name="backward",
    )(*first, *second, *weights)


def spread_kernel(blocks, qkv, proj, up, down, reduce_w, gains):
    for ref, first in ((qkv, 40), (proj, 32), (up, 16), (down, 24), (reduce_w, 0)):
        height, width = ref.shape
        for a in range(height // 256):
            for b in range(width // 128):
                part = blocks[first + a * (width // 128) + b].astype(F32)
                ref[256 * a : 256 * (a + 1), 128 * b : 128 * (b + 1)] = part
    gains[0:16] = blocks[34, 0:16].astype(F32)
    gains[16:32] = blocks[46, 0:16].astype(F32)


def run_spread(blocks):
    shapes = [(C, 3 * C), (C, C), (C, HID), (HID, C), (4 * C, C3), (32, 128)]
    return pl.pallas_call(
        spread_kernel,
        out_shape=[jax.ShapeDtypeStruct(shape, F32) for shape in shapes],
        compiler_params=pltpu.CompilerParams(vmem_limit_bytes=32 * MIB),
        name="spread",
    )(blocks)


def local(
    tokens, region_ids, gain_attn, qkv_weight, proj_weight, gain_mlp, up_weight, down_weight,
    gain_merge, reduce_weight, grad_merged,
):
    n_tm = lax.axis_size("tm")
    place = lax.axis_index("rows").astype(jnp.int32).reshape(1)
    gain1, gain2, gain3 = (g.reshape(1, -1) for g in (gain_attn, gain_mlp, gain_merge))
    *saved, out_win, qkv_t, gm, edge = run_forward(
        tokens.transpose(1, 2, 0, 3), grad_merged.transpose(1, 2, 0, 3),
        region_ids.transpose(1, 0, 2), qkv_weight, proj_weight, gain1, gain2, up_weight, down_weight,
    )
    grad_out, pieces, grad_reduce, grad_gain3 = run_merge(
        out_win, edge, gm, gain3, reduce_weight, place
    )
    totals, merged, grad_tokens = run_backward(
        n_tm, grad_out, saved, qkv_t, proj_weight, gain1, gain2, up_weight, down_weight,
        grad_reduce, grad_gain3, pieces,
    )
    *grads, gains = run_spread(totals.reshape(48, 256, 128))
    return (
        merged.transpose(2, 0, 1, 3),
        grad_tokens.transpose(2, 0, 1, 3),
        *grads,
        gains[16:18].reshape(-1),
        gains[0:2].reshape(-1),
        gains[2:10].reshape(-1),
    )


def solution(mesh):
    placed = (
        P("tm", "rows", None, None),
        P("tm", "rows", None),
        P(), P(), P(), P(), P(), P(), P(), P(),
        P(("tm", "rows"), None, None, None),
    )
    return jax.shard_map(
        local,
        mesh=mesh,
        in_specs=placed,
        out_specs=(
            P(("tm", "rows"), None, None, None),
            P("tm", "rows", None, None),
            P(), P(), P(), P(), P(), P(), P(), P(),
        ),
        check_vma=False,
    )
```

```python
import math

import jax
import jax.numpy as jnp
from jax import lax
from jax.experimental import pallas as pl
from jax.experimental.pallas import tpu as pltpu
from jax.sharding import PartitionSpec as P

HEADS = 8
HEAD = 32
NPOS = 392
C = 256
HID = 1024
C3 = 512
EPS = 1e-05
LOG2E = 1.4426950408889634
LN2 = 0.6931471805599453
SCALE = 1.0 / math.sqrt(HEAD)
FAR = 1e30
F32 = jnp.float32
BF16 = jnp.bfloat16
MIB = 1024 * 1024


def dot_nn(left, right):
    return lax.dot_general(left, right, (((1,), (0,)), ((), ())), preferred_element_type=F32)


def dot_nt(left, right):
    return lax.dot_general(left, right, (((1,), (1,)), ((), ())), preferred_element_type=F32)


def dot_tn(left, right):
    return lax.dot_general(left, right, (((0,), (0,)), ((), ())), preferred_element_type=F32)


def norm_forward(values):
    centre = jnp.mean(values, axis=-1, keepdims=True)
    centred = values - centre
    spread = jnp.mean(centred * centred, axis=-1, keepdims=True)
    inverse = lax.rsqrt(spread + EPS)
    return centred * inverse, inverse


def norm_backward(normed, inverse, gain, incoming):
    gated = incoming * gain
    first_mean = jnp.mean(gated, axis=-1, keepdims=True)
    second_mean = jnp.mean(gated * normed, axis=-1, keepdims=True)
    return inverse * (gated - first_mean - normed * second_mean)


def gelu_and_slope(up):
    size = jnp.abs(up)
    t = pl.reciprocal(1.0 + (0.3275911 * 0.7071067811865476) * size, approx=True)
    bell = jnp.exp2((-0.5 * LOG2E) * (up * up))
    series = 0.5 * 1.061405429 * t - 0.5 * 1.453152027
    series = series * t + 0.5 * 1.421413741
    series = series * t - 0.5 * 0.284496736
    series = series * t + 0.5 * 0.254829592
    tail = series * t * bell
    cdf = jnp.where(up >= 0.0, 1.0 - tail, tail)
    return up * cdf, cdf + up * (bell * 0.3989422804014327)


MESH = pl.DeviceIdType.MESH
RUNS = ((3, 0, 7), (10, 7, 7), (17, 14, 7), (24, 21, 4), (0, 25, 3))


def runs_of(wc):
    return range(wc, wc + 1) if wc < 3 else range(3, 5)


class Place:
    def __init__(self):
        self.m, self.r = lax.axis_index("tm"), lax.axis_index("rows")
        self.n_tm = lax.axis_size("tm")
        self.odd = lax.rem(self.r, 2)
        self.edge = jnp.where(self.r == 0, 1, 0)

    def at(self, dm, dr):
        return (lax.rem(self.m + dm + self.n_tm, self.n_tm), lax.rem(self.r + dr + 4, 4))

    def across(self):
        return (self.m, 3 - self.r)

    def holder(self, k):
        r = lax.rem(self.r - k + 4, 4)
        return self.at(-self.edge, k), self.at(jnp.where(r == 0, 1, 0), -k)

    def owner(self, k):
        r = lax.rem(self.r + k, 4)
        return self.at(jnp.where(r == 0, 1, 0), k), self.at(-self.edge, -k)

    def greet(self, sources, extra):
        barrier = pltpu.get_barrier_semaphore()
        for dev in sources:
            pl.semaphore_signal(barrier, inc=1, device_id=dev, device_id_type=MESH)

        @pl.when(self.r == 0)
        def _():
            pl.semaphore_signal(barrier, inc=1, device_id=extra, device_id_type=MESH)
            pl.semaphore_wait(barrier, len(sources) + 1)

        @pl.when(self.r != 0)
        def _():
            pl.semaphore_wait(barrier, len(sources))


def remote(src, dst, sems, n, dev):
    return pltpu.make_async_remote_copy(
        src_ref=src, dst_ref=dst, send_sem=sems[0].at[n], recv_sem=sems[1].at[n],
        device_id=dev, device_id_type=MESH,
    )


def pack(quarters):
    padded = jnp.concatenate([quarters, jnp.zeros((3, 4, C), F32)], axis=0).reshape(13, 4, 4, C)
    return jnp.concatenate([padded[:, n] for n in range(4)], axis=1).astype(BF16)


def unpack(packed):
    wide = packed.astype(F32)
    parts = [wide[:, 4 * n : 4 * (n + 1)].reshape(13, 1, 4, C) for n in range(4)]
    return jnp.concatenate(parts, axis=1).reshape(52, 4, C)[0:49]


def store_blocks(flat, first, values):
    height, width = values.shape
    for a in range(height // 256):
        for b in range(width // 128):
            at = 256 * (first + a * (width // 128) + b)
            part = values[256 * a : 256 * (a + 1), 128 * b : 128 * (b + 1)]
            flat[at : at + 256] = part.astype(BF16)


def column_runs(wc):
    if wc < 3:
        return [(7 * wc + 3, 0, 7)]
    return [(24, 0, 4), (0, 4, 7)]


def merge_half(
    tw, odd, out_all, edge, gm, gain3, reduce_w, grad_out, m_all, grad_gain, rows, third_all, gm_rows,
    grad_reduce,
):
    for wc in range(4):
        block = out_all[4 * tw + wc].astype(F32).reshape(7, 7, 8, C)
        strip = edge[tw, wc].astype(F32).reshape(7, 8, C)
        for start, first, last in column_runs(wc):
            cols = slice(start, start + last - first)
            rows[pl.ds(1 - odd, 7), cols] = block[:, first:last]
            rows[7 * odd, cols] = strip[first:last]

    gain = gain3[...]
    for a in range(4):
        upper = rows[2 * a].reshape(14, 2, 8, C)
        lower = rows[2 * a + 1].reshape(14, 2, 8, C)
        joined = jnp.concatenate(
            [upper[:, 0], lower[:, 0], upper[:, 1], lower[:, 1]], axis=-1
        ).reshape(112, 4 * C)
        normed, inverse = norm_forward(joined)
        third = normed * gain
        merged = dot_nn(third.astype(BF16), reduce_w[...]).reshape(14, 8, C3)
        m_all[2 * tw, a] = merged[:, 0:4].astype(BF16)
        m_all[2 * tw + 1, a] = merged[:, 4:8].astype(BF16)
        grads = jnp.concatenate(
            [gm[2 * tw, a].astype(F32), gm[2 * tw + 1, a].astype(F32)], axis=1
        )
        grads = grads.reshape(112, C3).astype(BF16)
        gz = dot_nt(grads, reduce_w[...])
        gz_sum = jnp.sum(gz * normed, axis=0, keepdims=True)
        if a == 0:
            counted = jnp.where((odd == 0) & (tw == 1), 0.0, 1.0)
        elif a == 3:
            counted = jnp.where((odd == 1) & (tw == 0), 0.0, 1.0)
        else:
            counted = None
        if counted is not None:
            third = third * counted
            gz_sum = gz_sum * counted
        grad_gain[...] += gz_sum
        third_all[112 * a : 112 * (a + 1)] = third.astype(BF16)
        gm_rows[112 * a : 112 * (a + 1)] = grads
        back = norm_backward(normed, inverse, gain, gz).reshape(14, 8, 4 * C)
        pieces = [back[:, :, C * n : C * (n + 1)].reshape(14, 1, 8, C) for n in range(4)]
        rows[2 * a] = jnp.concatenate([pieces[0], pieces[2]], axis=1).reshape(28, 8, C)
        rows[2 * a + 1] = jnp.concatenate([pieces[1], pieces[3]], axis=1).reshape(28, 8, C)
    grad_reduce[...] += dot_tn(third_all[...], gm_rows[...])
    for wc in range(4):
        runs = [
            rows[pl.ds(1 - odd, 7), start : start + last - first]
            for start, first, last in column_runs(wc)
        ]
        block = runs[0] if len(runs) == 1 else jnp.concatenate(runs, axis=1)
        grad_out[4 * tw + wc] = block.reshape(NPOS, C).astype(BF16)


def mask_rows(ids, pos, tw, wc):
    lane = lax.broadcasted_iota(jnp.int32, (1, 28), 1)
    first = lane == 7 * wc
    here = (lane >= 7 * wc) & (lane < 7 * wc + 7)
    frames = ids[0, pl.ds(pl.multiple_of(8 * tw, 8), 8), :]
    rows = ids[:, pl.ds(pl.multiple_of(8 * tw, 8), 8), :]

    def count(bits, kept):
        kept_bits = jnp.where(kept, bits.astype(F32), 0.0)
        return jnp.sum(jnp.sum(kept_bits, axis=0, keepdims=True), axis=1, keepdims=True)

    past = [
        count((frames >> 2) & 1, first),
        count(jnp.concatenate([(rows[i, 0:1] >> 1) & 1 for i in range(7)], axis=0), first),
        count(frames[0:1] & 1, here),
    ]
    bits = [
        jnp.where(pos[n : n + 1] >= extent - past[n], 1.0, 0.0)
        for n, extent in enumerate((8.0, 7.0, 7.0))
    ]
    none = [jnp.zeros((10, NPOS), F32)]
    keys = jnp.concatenate([v for b in bits for v in (b, 1.0 - b)] + none, axis=0)
    queries = jnp.concatenate([v for b in bits for v in (1.0 - b, b)] + none, axis=0) * -FAR
    return keys.astype(BF16), queries.astype(BF16)


def forward_kernel(
    tokens, gm, ids, pos, qkv_w, proj, gain1, gain2, up_w, down_w, gain3, reduce_w,
    x_out, qkv_out, exp_out, inv_out, att_out, hid_out, act_out, slope_out, qkv_t, grad_out, m_all,
    reduce_rows, grad_gain3,
    tok, x_now, pack_t, halo_t, edge_out, edge_in, gm_in, out_all, rows_all, third_all, gm_rows,
    grad_reduce, own_sem, row_out, row_in, t_out, t_in, gm_out_sem, gm_in_sem, gm_own, edge_out_sem,
    edge_in_sem,
):
    step = pl.program_id(0)
    tw, wc = step // 4, lax.rem(step, 4)
    place = Place()
    row_sems, t_sems = (row_out, row_in), (t_out, t_in)
    gm_sems, edge_sems = (gm_out_sem, gm_in_sem), (edge_out_sem, edge_in_sem)

    def own_copies():
        return [
            pltpu.make_async_copy(
                tokens.at[3:7, a : a + n], tok.at[0:4, b : b + n], own_sem.at[at]
            )
            for at, (a, b, n) in enumerate(((3, 0, 25), (0, 25, 3)))
        ]

    def row_copy(at):
        a, b, n = RUNS[at]
        return remote(
            tokens.at[0:3, a : a + n], tok.at[4:7, b : b + n], row_sems, at, place.at(0, -1)
        )

    def t_copy():
        return remote(pack_t.at[wc], halo_t.at[wc], t_sems, wc, place.at(-1, 0))

    def gm_copy(k, part):
        dev, _ = place.holder(k)
        band = lax.rem(place.r + k, 4)
        first = lax.rem(4 * band + 1 - band // 2 + 2 * part, 14)
        slot = lax.rem(place.r + 3, 4)
        src, dst = gm.at[pl.ds(first, 2)], gm_in.at[slot, 2 * part : 2 * part + 2]
        return remote(src, dst, gm_sems, 2 * k + part, dev)

    def gm_local(part):
        band = place.r
        first = lax.rem(4 * band + 1 - band // 2 + 2 * part, 14)
        slot = lax.rem(place.r + 3, 4)
        return pltpu.make_async_copy(
            gm.at[pl.ds(first, 2)], gm_in.at[slot, 2 * part : 2 * part + 2], gm_own.at[part]
        )

    def edge_copy(half):
        return remote(edge_out.at[half], edge_in.at[half], edge_sems, half, place.across())

    @pl.when((tw == 0) & (wc == 0))
    def _():
        for copy in own_copies():
            copy.start()
        sources = [place.at(0, 1), place.at(1, 0), place.across()]
        place.greet(sources + [place.holder(k)[1] for k in (1, 2, 3)], place.holder(0)[1])
        for at in range(5):
            row_copy(at).start()
        qkv_t[...] = qkv_w[...].astype(F32).T.astype(BF16)
        for copy in own_copies():
            copy.wait()

    @pl.when((tw == 0) & (wc == 1))
    def _():
        for k in (1, 2, 3):
            for part in range(2):
                gm_copy(k, part).start()

        @pl.when(place.r == 0)
        def _():
            for part in range(2):
                gm_copy(0, part).start()

        @pl.when(place.r != 0)
        def _():
            for part in range(2):
                gm_local(part).start()

    for window in range(4):

        @pl.when((tw == 0) & (wc == window))
        def _(window=window):
            for at in runs_of(window):
                row_copy(at).wait_recv()

    @pl.when(tw == 0)
    def _():
        block = tok[:, pl.ds(7 * wc, 7)].astype(F32).reshape(49, 16, C)
        pack_t[wc] = pack(block[:, 0:4])
        t_copy().start()
        x_now[...] = block[:, 4:12]

    @pl.when(tw == 1)
    def _():
        t_copy().wait_recv()
        block = tok[:, pl.ds(7 * wc, 7)].astype(F32).reshape(49, 16, C)
        x_now[...] = jnp.concatenate([block[:, 12:16], unpack(halo_t[wc])], axis=1)

    @pl.when(step < 8)
    def _():
        x = x_now[...].reshape(NPOS, C)
        x_out[0] = x.astype(BF16)
        mask_k, mask_q = mask_rows(ids, pos, tw, wc)
        normed, _ = norm_forward(x)
        first_in = (normed * gain1[...]).astype(BF16)
        rows = dot_nt(qkv_t[...], first_in)
        qkv_out[0, 0:C] = (rows[0:C] * (SCALE * LOG2E)).astype(BF16)
        qkv_out[0, C:] = rows[C:].astype(BF16)
        for h in range(HEADS):
            here = slice(HEAD * h, HEAD * (h + 1))
            q = jnp.concatenate([qkv_out[0, HEAD * h : HEAD * (h + 1)], mask_q], axis=0)
            k = jnp.concatenate([qkv_out[0, C + HEAD * h : C + HEAD * (h + 1)], mask_k], axis=0)
            v = qkv_out[0, 2 * C + HEAD * h : 2 * C + HEAD * (h + 1)]
            scores = dot_tn(k, q)
            top = jnp.max(scores, axis=0, keepdims=True)
            expon = jnp.exp2(scores - top)
            inverse = 1.0 / jnp.sum(expon, axis=0, keepdims=True)
            expon = expon.astype(BF16)
            exp_out[0, h] = expon
            inv_out[0, h : h + 1] = inverse
            att_out[0, here] = (dot_nn(v, expon) * inverse).astype(BF16)
        hidden = (x + dot_tn(att_out[0], proj[...])).astype(BF16)
        hid_out[0] = hidden
        hidden = hidden.astype(F32)
        normed, _ = norm_forward(hidden)
        second_in = (normed * gain2[...]).astype(BF16)
        result = hidden
        for part in range(4):
            cols = slice(256 * part, 256 * (part + 1))
            act, slope = gelu_and_slope(dot_nn(second_in, up_w[:, cols]))
            act = act.astype(BF16)
            act_out[0, :, cols] = act
            slope_out[0, :, cols] = slope.astype(BF16)
            result = result + dot_nn(act, down_w[cols])
        out_all[step] = result.astype(BF16)
        edge = jnp.where(place.odd == 1, result[336:392], result[0:56])
        edge_out[tw, wc] = edge.astype(BF16)

    @pl.when((tw == 0) & (wc == 3))
    def _():
        edge_copy(0).start()

    @pl.when(step == 7)
    def _():
        edge_copy(1).start()

    @pl.when(step == 8)
    def _():
        grad_reduce[...] = jnp.zeros_like(grad_reduce)
        grad_gain3[...] = jnp.zeros_like(grad_gain3)
        for k in (1, 2, 3):
            for part in range(2):
                gm_copy(k, part).wait()

        @pl.when(place.r == 0)
        def _():
            for part in range(2):
                gm_copy(0, part).wait()

        @pl.when(place.r != 0)
        def _():
            for part in range(2):
                gm_local(part).wait()

        edge_copy(0).wait()

    @pl.when(step == 9)
    def _():
        edge_copy(1).wait()

    @pl.when(step >= 8)
    def _():
        merge_half(
            step - 8, place.odd, out_all, edge_in, gm_in, gain3, reduce_w, grad_out, m_all,
            grad_gain3, rows_all, third_all, gm_rows, grad_reduce,
        )

    @pl.when(step == 9)
    def _():
        store_blocks(reduce_rows, 0, grad_reduce)
        for at in range(5):
            row_copy(at).wait_send()
        for n in range(4):
            remote(pack_t.at[n], halo_t.at[n], t_sems, n, place.at(-1, 0)).wait_send()


def whole(shape):
    return pl.BlockSpec(shape, lambda *_: (0,) * len(shape))


def by_window(shape):
    return pl.BlockSpec((1,) + shape, lambda s: (jnp.minimum(s, 7),) + (0,) * len(shape))


ANY_SPEC = pl.BlockSpec(memory_space=pl.ANY)
DMA = pltpu.SemaphoreType.DMA


def positions():
    at = jnp.arange(NPOS)
    rows = [at % 8, at // 56, (at // 8) % 7]
    return jnp.concatenate([jnp.stack(rows), jnp.zeros((5, NPOS), at.dtype)]).astype(F32)


def run_forward(tokens, gm, ids, *weights):
    saved = [
        ((NPOS, C), BF16),
        ((3 * C, NPOS), BF16),
        ((HEADS, NPOS, NPOS), BF16),
        ((HEADS, NPOS), F32),
        ((C, NPOS), BF16),
        ((NPOS, C), BF16),
        ((NPOS, HID), BF16),
        ((NPOS, HID), BF16),
    ]
    others = [
        ((3 * C, C), BF16),
        ((8, NPOS, C), BF16),
        ((4, 4, 14, 4, C3), BF16),
        ((4096, 128), BF16),
        ((1, 4 * C), F32),
    ]
    pos = positions()
    return pl.pallas_call(
        forward_kernel,
        grid=(10,),
        out_shape=[jax.ShapeDtypeStruct((8,) + shape, kind) for shape, kind in saved]
        + [jax.ShapeDtypeStruct(shape, kind) for shape, kind in others],
        in_specs=[ANY_SPEC, ANY_SPEC, whole(ids.shape), whole(pos.shape)]
        + [whole(w.shape) for w in weights],
        out_specs=[by_window(shape) for shape, _ in saved] + [whole(shape) for shape, _ in others],
        scratch_shapes=[
            pltpu.VMEM((7, 28, 16, C), BF16),
            pltpu.VMEM((49, 8, C), F32),
            pltpu.VMEM((4, 13, 16, C), BF16),
            pltpu.VMEM((4, 13, 16, C), BF16),
            pltpu.VMEM((2, 4, 56, C), BF16),
            pltpu.VMEM((2, 4, 56, C), BF16),
            pltpu.VMEM((4, 4, 14, 4, C3), BF16),
            pltpu.VMEM((8, NPOS, C), BF16),
            pltpu.VMEM((8, 28, 8, C), F32),
            pltpu.VMEM((448, 4 * C), BF16),
            pltpu.VMEM((448, C3), BF16),
            pltpu.VMEM((4 * C, C3), F32),
            DMA((2,)), DMA((5,)), DMA((5,)), DMA((4,)), DMA((4,)), DMA((8,)), DMA((8,)),
            DMA((2,)), DMA((2,)), DMA((2,)),
        ],
        compiler_params=pltpu.CompilerParams(
            vmem_limit_bytes=60 * MIB, collective_id=1, has_side_effects=True
        ),
        name="forward",
    )(tokens, gm, ids, pos, *weights)


ORDERS = (("x", "y", "z"), ("y", "z", "x"), ("z", "x", "y"))


def torus(n_tm):
    return {32: (4, 2, 4), 4: (2, 1, 2)}[n_tm]


class Torus:
    def __init__(self, dims):
        self.dims = dims
        _, n_yl, n_z = dims
        m, r = lax.axis_index("tm"), lax.axis_index("rows")
        self.core = lax.rem(r, 2)
        self.size = dims[0]
        self.at = {
            "x": m // (n_yl * n_z),
            "y": (r // 2) * n_yl + lax.rem(m // n_z, n_yl),
            "z": lax.rem(m, n_z),
        }

    def device(self, core=None, **moved):
        _, n_yl, n_z = self.dims
        at = {**self.at, **moved}
        core = self.core if core is None else core
        m = (at["x"] * n_yl + lax.rem(at["y"], n_yl)) * n_z + at["z"]
        return (m, (at["y"] // n_yl) * 2 + core)

    def partners(self, axis):
        places = [lax.rem(self.at[axis] + j, self.size) for j in range(1, self.size)]
        return [(place, self.device(**{axis: place})) for place in places]

    def other(self):
        return self.device(core=1 - self.core)

    def everyone(self):
        return [self.other()] + [dev for axis in "xyz" for _, dev in self.partners(axis)]


def at_rows(start, length):
    return pl.ds(pl.multiple_of(start, 16), length)


class Sum:
    def __init__(self, here, lengths, whole_last, source, total, base, scratch):
        self.here, self.lengths, self.whole_last = here, lengths, whole_last
        self.source, self.total, self.base = source, total, base
        self.core_in, *rest = scratch
        self.accs, self.ins = rest[0:3], rest[3:6]
        self.core_sems, self.rs_sems, self.ag_sems, self.back_sems = (
            tuple(rest[6 + 2 * n : 8 + 2 * n]) for n in range(4)
        )

    @staticmethod
    def scratch(size, lengths, whole_last):
        most, length = max(lengths), max(lengths)
        shapes = [(3, most, 128)]
        accs, ins = [], []
        for s in range(3):
            accs.append((3, length, 128))
            length = length if s == 2 and whole_last else length // size
            ins.append((3, size - 1, length, 128))
        sems = [(3,), (3,), (9 * (size - 1),), (9 * (size - 1),), (9 * (size - 1),), (9 * (size - 1),), (3,), (3,)]
        return [pltpu.VMEM(shape, BF16) for shape in shapes + accs + ins] + [DMA(n) for n in sems]

    def half(self, core, p):
        return core * sum(self.lengths) + sum(self.lengths[:p])

    def piece(self, p, s):
        start, length = self.half(self.here.core, p), self.lengths[p]
        for n in range(s):
            if not (n == 2 and self.whole_last):
                length = length // self.here.size
                start = start + self.here.at[ORDERS[p][n]] * length
        return start, length

    def core_copy(self, p):
        start = self.half(1 - self.here.core, p)
        return remote(
            self.source.at[at_rows(start, self.lengths[p])],
            self.core_in.at[p, 0 : self.lengths[p]],
            self.core_sems, p, self.here.other(),
        )

    def rs_copies(self, p, s):
        _, length = self.piece(p, s)
        whole_piece = s == 3 and self.whole_last
        return [
            remote(
                self.accs[s - 1].at[p, 0:length]
                if whole_piece
                else self.accs[s - 1].at[p, at_rows(place * length, length)],
                self.ins[s - 1].at[p, j, 0:length],
                self.rs_sems, (3 * (s - 1) + p) * (self.here.size - 1) + j, dev,
            )
            for j, (place, dev) in enumerate(self.here.partners(ORDERS[p][s - 1]))
        ]

    def ag_copies(self, p, s):
        start, length = self.piece(p, s)
        region = self.total.at[at_rows(self.base + start, length)]
        return [
            remote(region, region, self.ag_sems, (3 * (s - 1) + p) * (self.here.size - 1) + j, dev)
            for j, (_, dev) in enumerate(self.here.partners(ORDERS[p][s - 1]))
        ]

    def back_copy(self, p):
        start, length = self.piece(p, 0)
        region = self.total.at[at_rows(self.base + start, length)]
        return remote(region, region, self.back_sems, p, self.here.other())

    def start(self):
        for p in range(3):
            self.core_copy(p).start()

    def reduce(self, s):
        for p in range(3):
            start, length = self.piece(p, s)
            if s == 0:
                self.core_copy(p).wait_recv()
                value = self.source[at_rows(start, length)].astype(F32)
                value = value + self.core_in[p, 0:length].astype(F32)
            else:
                for copy in self.rs_copies(p, s):
                    copy.wait_recv()
                if s == 3 and self.whole_last:
                    value = self.accs[2][p, 0:length].astype(F32)
                else:
                    place = self.here.at[ORDERS[p][s - 1]]
                    value = self.accs[s - 1][p, at_rows(place * length, length)].astype(F32)
                for j in range(self.here.size - 1):
                    value = value + self.ins[s - 1][p, j, 0:length].astype(F32)
            if s < 3:
                self.accs[s][p, 0:length] = value.astype(BF16)
                for copy in self.rs_copies(p, s + 1):
                    copy.start()
            else:
                self.total[at_rows(self.base + start, length)] = value.astype(BF16)
                for copy in self.ag_copies(p, 2 if self.whole_last else 3):
                    copy.start()

    def gather(self, s):
        for p in range(3):
            for copy in self.ag_copies(p, s):
                copy.wait_recv()
            for copy in self.ag_copies(p, s - 1) if s > 1 else [self.back_copy(p)]:
                copy.start()

    def finish(self):
        for p in range(3):
            self.back_copy(p).wait()
            self.core_copy(p).wait_send()
            for s in (1, 2, 3):
                for copy in self.rs_copies(p, s):
                    copy.wait_send()
                if s < 3 or not self.whole_last:
                    for copy in self.ag_copies(p, s):
                        copy.wait_send()


SUMS = ((768, 768, 512), (1024, 768, 768), (512, 256, 256))
SUM_ROWS = tuple(2 * sum(lengths) for lengths in SUMS)
SUM_BASES = (0, SUM_ROWS[0], SUM_ROWS[0] + SUM_ROWS[1])


def backward_kernel(
    dims, grad_out, att_a, hid_in, act_in, slope_in, x_in, qkv_in, exp_in, inv_in, att_in,
    qkv_t, proj, gain1, gain2, up_w, down_w, reduce_rows, grad_gain3, pieces,
    totals, merged, grad_tokens,
    grad_hidden_all, grad_att_all, grad_rows_t, grad_qkv_t, grad_proj, grad_up, grad_down_t,
    grad_gain1, grad_gain2, late, final, pack_t, halo_t, rows_0, rows_1, rows_2, total,
    t_out, t_in, row_out, row_in, own_sem, m_out, m_in, m_own, total_sem, *sum_scratch,
):
    step = pl.program_id(0)
    tw, wc = 1 - lax.rem(step, 8) // 4, lax.rem(step, 4)
    window = 4 * tw + wc
    first_phase, second_phase = step < 8, step >= 8
    place, here = Place(), Torus(dims)
    t_sems, row_sems, m_sems = (t_out, t_in), (row_out, row_in), (m_out, m_in)
    each = len(sum_scratch) // 3
    sum_0, sum_1, sum_2 = (
        Sum(here, SUMS[n], True, rows, total, SUM_BASES[n], sum_scratch[each * n : each * (n + 1)])
        for n, rows in enumerate((rows_0, rows_1, rows_2))
    )

    def m_ends(k, n):
        c = lax.rem(place.r + k + 3, 4)
        start = 4 * place.r + 1 - place.r // 2
        first = (1 - place.odd, 3 - place.odd, 3)[n]
        count = (2, 1, 1)[n]
        return (
            pieces.at[c, pl.ds(first, count)],
            merged.at[pl.ds(lax.rem(start + first, 14), count)],
        )

    def m_copy(k, n):
        return remote(*m_ends(k, n), m_sems, 3 * k + n, place.owner(k)[0])

    def m_local(n):
        return pltpu.make_async_copy(*m_ends(0, n), m_own.at[n])

    def m_each(act_remote, act_local):
        for k in (1, 2, 3):
            act_remote(k, 0)
            act_remote(k, 1)

        @pl.when(place.r == 0)
        def _():
            act_remote(0, 0)
            act_remote(0, 1)

        @pl.when(place.r != 0)
        def _():
            act_local(0)
            act_local(1)

    def t_copy(n):
        return remote(pack_t.at[n], halo_t.at[n], t_sems, n, place.at(1, 0))

    def row_copy(at):
        a, b, n = RUNS[at]
        part, first = (at, 0) if at < 3 else (3, b - 21)
        return remote(
            final.at[part, 4:7, first : first + n], grad_tokens.at[0:3, a : a + n],
            row_sems, at, place.at(0, 1),
        )

    def own_copy(at):
        a, b, n = RUNS[at]
        part, first = (at, 0) if at < 3 else (3, b - 21)
        return pltpu.make_async_copy(
            final.at[part, 0:4, first : first + n], grad_tokens.at[3:7, a : a + n], own_sem.at[at]
        )

    def total_copy(n):
        region = pl.ds(SUM_BASES[n], SUM_ROWS[n])
        return pltpu.make_async_copy(total.at[region], totals.at[region], total_sem.at[n])

    @pl.when(step == 0)
    def _():
        for ref in (grad_qkv_t, grad_proj, grad_up, grad_down_t, grad_gain1, grad_gain2):
            ref[...] = jnp.zeros_like(ref)
        sources = [place.at(0, -1), place.at(-1, 0)] + [place.owner(k)[1] for k in (1, 2, 3)]
        rows_0[...] = reduce_rows[...]
        place.greet(sources + here.everyone(), place.owner(0)[1])
        sum_0.start()

    @pl.when(step == 2)
    def _():
        m_each(lambda k, n: m_copy(k, n).start(), lambda n: m_local(n).start())

        @pl.when(place.odd == 1)
        def _():
            for k in (1, 2, 3):
                m_copy(k, 2).start()
            m_local(2).start()

    @pl.when(first_phase)
    def _():
        grad_rows = grad_out[0]
        normed2, inverse2 = norm_forward(hid_in[0].astype(F32))
        second_in = (normed2 * gain2[...]).astype(BF16)
        grad_second = jnp.zeros((NPOS, C), F32)
        for part in range(4):
            cols = slice(256 * part, 256 * (part + 1))
            grad_down_t[:, cols] += dot_tn(grad_rows, act_in[0, :, cols])
            grad_act = dot_nt(grad_rows, down_w[cols])
            grad_up_in = (grad_act * slope_in[0, :, cols].astype(F32)).astype(BF16)
            grad_up[:, cols] += dot_tn(second_in, grad_up_in)
            grad_second = grad_second + dot_nt(grad_up_in, up_w[:, cols])
        grad_gain2[...] += jnp.sum(grad_second * normed2, axis=0, keepdims=True)
        back = norm_backward(normed2, inverse2, gain2[...], grad_second)
        grad_hidden = grad_rows.astype(F32) + back
        grad_hidden_all[window] = grad_hidden
        grad_hidden_b = grad_hidden.astype(BF16)
        grad_proj[...] += dot_nn(att_a[0], grad_hidden_b)
        grad_att_all[window] = dot_nt(proj[...], grad_hidden_b).astype(BF16)

    @pl.when(step == 7)
    def _():
        store_blocks(rows_1, 0, grad_up[...])
        store_blocks(rows_1, 8, grad_down_t[...].T)
        store_blocks(rows_1, 16, grad_proj[...])
        rows = [grad_gain2[:, 0:128], grad_gain2[:, 128:256]]
        rows += [grad_gain3[:, 128 * n : 128 * (n + 1)] for n in range(8)]
        rows.append(jnp.zeros((6, 128), F32))
        rows_1[18 * 256 : 18 * 256 + 16] = jnp.concatenate(rows, axis=0).astype(BF16)
        rows_1[18 * 256 + 16 :] = jnp.zeros((SUM_ROWS[1] - 18 * 256 - 16, 128), BF16)
        sum_1.start()

    for at, run in (
        (1, lambda: sum_0.reduce(0)),
        (3, lambda: sum_0.reduce(1)),
        (4, lambda: sum_0.reduce(2)),
        (5, lambda: sum_0.reduce(3)),
        (6, lambda: sum_0.gather(2)),
        (8, lambda: sum_0.gather(1)),
        (9, lambda: sum_1.reduce(0)),
        (10, lambda: sum_1.reduce(1)),
        (11, lambda: sum_1.reduce(2)),
        (12, lambda: sum_1.reduce(3)),
        (13, lambda: sum_1.gather(2)),
        (14, lambda: sum_1.gather(1)),
    ):
        pl.when(step == at)(run)

    @pl.when(second_phase)
    def _():
        for h in range(HEADS):
            at_q = slice(HEAD * h, HEAD * (h + 1))
            at_k = slice(C + HEAD * h, C + HEAD * (h + 1))
            at_v = slice(2 * C + HEAD * h, 2 * C + HEAD * (h + 1))
            expon = exp_in[0, h]
            incoming = grad_att_all[window, at_q].astype(F32) * inv_in[0, h : h + 1]
            incoming = incoming.astype(BF16)
            inner = incoming.astype(F32) * att_in[0, at_q].astype(F32)
            inner = jnp.sum(inner, axis=0, keepdims=True)
            grad_probs = dot_tn(qkv_in[0, at_v], incoming)
            grad_scores = (expon.astype(F32) * (grad_probs - inner)).astype(BF16)
            grad_rows_t[at_q] = (dot_nn(qkv_in[0, at_k], grad_scores) * SCALE).astype(BF16)
            grad_rows_t[at_k] = (dot_nt(qkv_in[0, at_q], grad_scores) * LN2).astype(BF16)
            grad_rows_t[at_v] = dot_nt(incoming, expon).astype(BF16)
        normed1, inverse1 = norm_forward(x_in[0].astype(F32))
        first_in = (normed1 * gain1[...]).astype(BF16)
        grad_qkv_t[...] += dot_nn(grad_rows_t[...], first_in)
        grad_first = dot_tn(grad_rows_t[...], qkv_t[...])
        grad_gain1[...] += jnp.sum(grad_first * normed1, axis=0, keepdims=True)
        back = norm_backward(normed1, inverse1, gain1[...], grad_first)
        block = (grad_hidden_all[window] + back).reshape(49, 8, C)

        @pl.when(tw == 1)
        def _():
            late[wc] = block[:, 0:4].astype(BF16)
            pack_t[wc] = pack(block[:, 4:8])
            t_copy(wc).start()

        @pl.when(tw == 0)
        def _():
            t_copy(wc).wait_recv()
            frames = jnp.concatenate([unpack(halo_t[wc]), block, late[wc].astype(F32)], axis=1)
            final[wc] = frames.astype(BF16).reshape(7, 7, 16, C)

    for part in range(4):

        @pl.when(step == 12 + part)
        def _(part=part):
            for at in runs_of(part):
                row_copy(at).start()
                own_copy(at).start()

    @pl.when(step == 15)
    def _():
        store_blocks(rows_2, 0, grad_qkv_t[...].T)
        rows = [grad_gain1[:, 0:128], grad_gain1[:, 128:256], jnp.zeros((14, 128), F32)]
        rows_2[1536:1552] = jnp.concatenate(rows, axis=0).astype(BF16)
        rows_2[1552:] = jnp.zeros((SUM_ROWS[2] - 1552, 128), BF16)
        sum_2.start()
        sum_0.finish()
        sum_1.finish()
        total_copy(0).start()
        total_copy(1).start()
        for s in range(4):
            sum_2.reduce(s)
        sum_2.gather(2)
        sum_2.gather(1)
        for at in range(5):
            row_copy(at).wait()
            own_copy(at).wait()
        for n in range(4):
            t_copy(n).wait_send()
        m_each(lambda k, n: m_copy(k, n).wait(), lambda n: m_local(n).wait())

        @pl.when(place.odd == 1)
        def _():
            for k in (1, 2, 3):
                m_copy(k, 2).wait_send()
            m_local(2).wait()
            m_copy(2, 2).wait_recv()

        @pl.when(place.odd == 0)
        def _():
            for k in (1, 3):
                m_copy(k, 2).wait_recv()

        sum_2.finish()
        total_copy(2).start()
        for n in range(3):
            total_copy(n).wait()


def run_backward(n_tm, grad_out, saved, *weights):
    sums = [(3 * C, C), (C, C), (C, HID), (C, HID), (1, C), (1, C)]
    dims = torus(n_tm)
    x, qkv, expon, inverse, att, hid, act, slope = saved
    *vmem_weights, _ = weights

    def window(step):
        return 4 * (1 - lax.rem(step, 8) // 4) + lax.rem(step, 4)

    def in_first(array):
        shape = array.shape[1:]
        return pl.BlockSpec(
            (1,) + shape, lambda s: (window(jnp.minimum(s, 7)),) + (0,) * len(shape)
        )

    def in_second(array):
        shape = array.shape[1:]
        return pl.BlockSpec(
            (1,) + shape, lambda s: (window(jnp.maximum(s - 8, 0)),) + (0,) * len(shape)
        )

    first, second = (grad_out, att, hid, act, slope), (x, qkv, expon, inverse, att)
    return pl.pallas_call(
        lambda *refs: backward_kernel(dims, *refs),
        grid=(16,),
        out_shape=[
            jax.ShapeDtypeStruct((sum(SUM_ROWS), 128), BF16),
            jax.ShapeDtypeStruct((14, 14, 4, C3), BF16),
            jax.ShapeDtypeStruct((7, 28, 16, C), BF16),
        ],
        in_specs=[in_first(array) for array in first]
        + [in_second(array) for array in second]
        + [whole(w.shape) for w in vmem_weights]
        + [ANY_SPEC],
        out_specs=[ANY_SPEC] * 3,
        scratch_shapes=[
            pltpu.VMEM((8, NPOS, C), F32),
            pltpu.VMEM((8, C, NPOS), BF16),
            pltpu.VMEM((3 * C, NPOS), BF16),
        ]
        + [pltpu.VMEM(shape, F32) for shape in sums]
        + [
            pltpu.VMEM((4, 49, 4, C), BF16),
            pltpu.VMEM((4, 7, 7, 16, C), BF16),
            pltpu.VMEM((4, 13, 16, C), BF16),
            pltpu.VMEM((4, 13, 16, C), BF16),
            *(pltpu.VMEM((n, 128), BF16) for n in (*SUM_ROWS, sum(SUM_ROWS))),
            DMA((4,)), DMA((4,)), DMA((5,)), DMA((5,)), DMA((5,)), DMA((12,)), DMA((12,)), DMA((3,)),
            DMA((3,)),
        ]
        + [shape for lengths in SUMS for shape in Sum.scratch(dims[0], lengths, True)],
        compiler_params=pltpu.CompilerParams(
            vmem_limit_bytes=58 * MIB, collective_id=2, has_side_effects=True
        ),
        name="backward",
    )(*first, *second, *weights)


def spread_kernel(
    reduce_in, up_in, down_in, proj_in, qkv_in, gains_in, gain1_in,
    qkv, proj, up, down, reduce_w, gain1, gain2, gain3,
):
    step = pl.program_id(0)
    for ref, blocks in ((qkv, qkv_in), (up, up_in), (down, down_in), (reduce_w, reduce_in)):
        for b in range(ref.shape[1] // 128):
            ref[:, 128 * b : 128 * (b + 1)] = blocks[b].astype(F32)

    @pl.when(step == 0)
    def _():
        for b in range(2):
            proj[:, 128 * b : 128 * (b + 1)] = proj_in[b].astype(F32)
        gains, first = gains_in[0, 0:16].astype(F32), gain1_in[0, 0:16].astype(F32)
        for ref, rows, start in ((gain1, first, 0), (gain2, gains, 0), (gain3, gains, 2)):
            for n in range(ref.shape[1] // 128):
                ref[:, 128 * n : 128 * (n + 1)] = rows[start + n : start + n + 1]


def run_spread(totals):
    shapes = [(C, 3 * C), (C, C), (C, HID), (HID, C), (4 * C, C3), (1, C), (1, C), (1, 4 * C)]
    wide = lambda count: pl.BlockSpec((256, 256), lambda s: (0, jnp.minimum(s, count - 1)))

    def blocks(count, first, steps):
        return pl.BlockSpec(
            (count, 256, 128), lambda s: (first // count + jnp.minimum(s, steps - 1), 0, 0)
        )

    return pl.pallas_call(
        spread_kernel,
        grid=(4,),
        out_shape=[jax.ShapeDtypeStruct(shape, F32) for shape in shapes],
        in_specs=[
            blocks(4, 0, 4), blocks(2, 16, 4), blocks(2, 24, 4), blocks(2, 32, 1), blocks(2, 36, 3),
            blocks(1, 34, 1), blocks(1, 42, 1),
        ],
        out_specs=[
            wide(3),
            whole((C, C)),
            wide(4),
            pl.BlockSpec((256, C), lambda s: (s, 0)),
            pl.BlockSpec((256, C3), lambda s: (s, 0)),
            whole((1, C)),
            whole((1, C)),
            whole((1, 4 * C)),
        ],
        compiler_params=pltpu.CompilerParams(vmem_limit_bytes=32 * MIB),
        name="spread",
    )(*[totals] * 7)


def local(
    tokens, region_ids, gain_attn, qkv_weight, proj_weight, gain_mlp, up_weight, down_weight,
    gain_merge, reduce_weight, grad_merged,
):
    n_tm = lax.axis_size("tm")
    gain1, gain2, gain3 = (g.reshape(1, -1) for g in (gain_attn, gain_mlp, gain_merge))
    *saved, qkv_t, grad_out, pieces, reduce_rows, grad_gain3 = run_forward(
        tokens.transpose(1, 2, 0, 3), grad_merged.transpose(1, 2, 0, 3),
        region_ids.transpose(1, 0, 2), qkv_weight, proj_weight, gain1, gain2, up_weight, down_weight,
        gain3, reduce_weight,
    )
    totals, merged, grad_tokens = run_backward(
        n_tm, grad_out, saved, qkv_t, proj_weight, gain1, gain2, up_weight, down_weight,
        reduce_rows, grad_gain3, pieces,
    )
    *grads, gain1, gain2, gain3 = run_spread(totals.reshape(-1, 256, 128))
    return (
        merged.transpose(2, 0, 1, 3),
        grad_tokens.transpose(2, 0, 1, 3),
        *grads,
        gain1.reshape(-1),
        gain2.reshape(-1),
        gain3.reshape(-1),
    )


def solution(mesh):
    placed = (
        P("tm", "rows", None, None),
        P("tm", "rows", None),
        P(), P(), P(), P(), P(), P(), P(), P(),
        P(("tm", "rows"), None, None, None),
    )
    return jax.shard_map(
        local,
        mesh=mesh,
        in_specs=placed,
        out_specs=(
            P(("tm", "rows"), None, None, None),
            P("tm", "rows", None, None),
            P(), P(), P(), P(), P(), P(), P(), P(),
        ),
        check_vma=False,
    )
```

```python
import math

import jax
import jax.numpy as jnp
from jax import lax
from jax.experimental import pallas as pl
from jax.experimental.pallas import tpu as pltpu
from jax.sharding import PartitionSpec as P

HEADS = 8
HEAD = 32
NPOS = 392
C = 256
HID = 1024
C3 = 512
EPS = 1e-05
LOG2E = 1.4426950408889634
LN2 = 0.6931471805599453
SCALE = 1.0 / math.sqrt(HEAD)
FAR = 1e30
F32 = jnp.float32
BF16 = jnp.bfloat16
MIB = 1024 * 1024


def dot_nn(left, right):
    return lax.dot_general(left, right, (((1,), (0,)), ((), ())), preferred_element_type=F32)


def dot_nt(left, right):
    return lax.dot_general(left, right, (((1,), (1,)), ((), ())), preferred_element_type=F32)


def dot_tn(left, right):
    return lax.dot_general(left, right, (((0,), (0,)), ((), ())), preferred_element_type=F32)


def norm_forward(values):
    centre = jnp.mean(values, axis=-1, keepdims=True)
    centred = values - centre
    spread = jnp.mean(centred * centred, axis=-1, keepdims=True)
    inverse = lax.rsqrt(spread + EPS)
    return centred * inverse, inverse


def norm_backward(normed, inverse, gain, incoming):
    gated = incoming * gain
    first_mean = jnp.mean(gated, axis=-1, keepdims=True)
    second_mean = jnp.mean(gated * normed, axis=-1, keepdims=True)
    return inverse * (gated - first_mean - normed * second_mean)


def gelu_and_slope(up):
    size = jnp.abs(up)
    t = pl.reciprocal(1.0 + (0.3275911 * 0.7071067811865476) * size, approx=True)
    bell = jnp.exp2((-0.5 * LOG2E) * (up * up))
    series = 0.5 * 1.061405429 * t - 0.5 * 1.453152027
    series = series * t + 0.5 * 1.421413741
    series = series * t - 0.5 * 0.284496736
    series = series * t + 0.5 * 0.254829592
    tail = series * t * bell
    cdf = jnp.where(up >= 0.0, 1.0 - tail, tail)
    return up * cdf, cdf + up * (bell * 0.3989422804014327)


MESH = pl.DeviceIdType.MESH
RUNS = ((3, 0, 7), (10, 7, 7), (17, 14, 7), (24, 21, 4), (0, 25, 3))


def runs_of(wc):
    return range(wc, wc + 1) if wc < 3 else range(3, 5)


class Place:
    def __init__(self):
        self.m, self.r = lax.axis_index("tm"), lax.axis_index("rows")
        self.n_tm = lax.axis_size("tm")
        self.odd = lax.rem(self.r, 2)
        self.edge = jnp.where(self.r == 0, 1, 0)

    def at(self, dm, dr):
        return (lax.rem(self.m + dm + self.n_tm, self.n_tm), lax.rem(self.r + dr + 4, 4))

    def across(self):
        return (self.m, 3 - self.r)

    def holder(self, k):
        r = lax.rem(self.r - k + 4, 4)
        return self.at(-self.edge, k), self.at(jnp.where(r == 0, 1, 0), -k)

    def owner(self, k):
        r = lax.rem(self.r + k, 4)
        return self.at(jnp.where(r == 0, 1, 0), k), self.at(-self.edge, -k)

    def greet(self, sources, extra):
        barrier = pltpu.get_barrier_semaphore()
        for dev in sources:
            pl.semaphore_signal(barrier, inc=1, device_id=dev, device_id_type=MESH)

        @pl.when(self.r == 0)
        def _():
            pl.semaphore_signal(barrier, inc=1, device_id=extra, device_id_type=MESH)
            pl.semaphore_wait(barrier, len(sources) + 1)

        @pl.when(self.r != 0)
        def _():
            pl.semaphore_wait(barrier, len(sources))


def remote(src, dst, sems, n, dev):
    return pltpu.make_async_remote_copy(
        src_ref=src, dst_ref=dst, send_sem=sems[0].at[n], recv_sem=sems[1].at[n],
        device_id=dev, device_id_type=MESH,
    )


def pack(quarters):
    padded = jnp.concatenate([quarters, jnp.zeros((3, 4, C), F32)], axis=0).reshape(13, 4, 4, C)
    return jnp.concatenate([padded[:, n] for n in range(4)], axis=1).astype(BF16)


def unpack(packed):
    wide = packed.astype(F32)
    parts = [wide[:, 4 * n : 4 * (n + 1)].reshape(13, 1, 4, C) for n in range(4)]
    return jnp.concatenate(parts, axis=1).reshape(52, 4, C)[0:49]


def store_blocks(flat, first, values):
    height, width = values.shape
    for a in range(height // 256):
        for b in range(width // 128):
            at = 256 * (first + a * (width // 128) + b)
            part = values[256 * a : 256 * (a + 1), 128 * b : 128 * (b + 1)]
            flat[at : at + 256] = part.astype(BF16)


def column_runs(wc):
    if wc < 3:
        return [(7 * wc + 3, 0, 7)]
    return [(24, 0, 4), (0, 4, 7)]


def merge_half(
    tw, odd, out_all, edge, gm, gain3, reduce_w, grad_out, m_all, grad_gain, rows, third_all, gm_rows,
    grad_reduce,
):
    for wc in range(4):
        block = out_all[4 * tw + wc].astype(F32).reshape(7, 7, 8, C)
        strip = edge[tw, wc].astype(F32).reshape(7, 8, C)
        for start, first, last in column_runs(wc):
            cols = slice(start, start + last - first)
            rows[pl.ds(1 - odd, 7), cols] = block[:, first:last]
            rows[7 * odd, cols] = strip[first:last]

    gain = gain3[...]
    for a in range(4):
        upper = rows[2 * a].reshape(14, 2, 8, C)
        lower = rows[2 * a + 1].reshape(14, 2, 8, C)
        joined = jnp.concatenate(
            [upper[:, 0], lower[:, 0], upper[:, 1], lower[:, 1]], axis=-1
        ).reshape(112, 4 * C)
        normed, inverse = norm_forward(joined)
        third = normed * gain
        merged = dot_nn(third.astype(BF16), reduce_w[...]).reshape(14, 8, C3)
        m_all[2 * tw, a] = merged[:, 0:4].astype(BF16)
        m_all[2 * tw + 1, a] = merged[:, 4:8].astype(BF16)
        grads = jnp.concatenate(
            [gm[2 * tw, a].astype(F32), gm[2 * tw + 1, a].astype(F32)], axis=1
        )
        grads = grads.reshape(112, C3).astype(BF16)
        gz = dot_nt(grads, reduce_w[...])
        gz_sum = jnp.sum(gz * normed, axis=0, keepdims=True)
        if a == 0:
            counted = jnp.where((odd == 0) & (tw == 1), 0.0, 1.0)
        elif a == 3:
            counted = jnp.where((odd == 1) & (tw == 0), 0.0, 1.0)
        else:
            counted = None
        if counted is not None:
            third = third * counted
            gz_sum = gz_sum * counted
        grad_gain[...] += gz_sum
        third_all[112 * a : 112 * (a + 1)] = third.astype(BF16)
        gm_rows[112 * a : 112 * (a + 1)] = grads
        back = norm_backward(normed, inverse, gain, gz).reshape(14, 8, 4 * C)
        pieces = [back[:, :, C * n : C * (n + 1)].reshape(14, 1, 8, C) for n in range(4)]
        rows[2 * a] = jnp.concatenate([pieces[0], pieces[2]], axis=1).reshape(28, 8, C)
        rows[2 * a + 1] = jnp.concatenate([pieces[1], pieces[3]], axis=1).reshape(28, 8, C)
    grad_reduce[...] += dot_tn(third_all[...], gm_rows[...])
    for wc in range(4):
        runs = [
            rows[pl.ds(1 - odd, 7), start : start + last - first]
            for start, first, last in column_runs(wc)
        ]
        block = runs[0] if len(runs) == 1 else jnp.concatenate(runs, axis=1)
        grad_out[4 * tw + wc] = block.reshape(NPOS, C).astype(BF16)


def mask_rows(ids, pos, tw, wc):
    lane = lax.broadcasted_iota(jnp.int32, (1, 28), 1)
    first = lane == 7 * wc
    here = (lane >= 7 * wc) & (lane < 7 * wc + 7)
    frames = ids[0, pl.ds(pl.multiple_of(8 * tw, 8), 8), :]
    rows = ids[:, pl.ds(pl.multiple_of(8 * tw, 8), 8), :]

    def count(bits, kept):
        kept_bits = jnp.where(kept, bits.astype(F32), 0.0)
        return jnp.sum(jnp.sum(kept_bits, axis=0, keepdims=True), axis=1, keepdims=True)

    past = [
        count((frames >> 2) & 1, first),
        count(jnp.concatenate([(rows[i, 0:1] >> 1) & 1 for i in range(7)], axis=0), first),
        count(frames[0:1] & 1, here),
    ]
    bits = [
        jnp.where(pos[n : n + 1] >= extent - past[n], 1.0, 0.0)
        for n, extent in enumerate((8.0, 7.0, 7.0))
    ]
    none = [jnp.zeros((10, NPOS), F32)]
    keys = jnp.concatenate([v for b in bits for v in (b, 1.0 - b)] + none, axis=0)
    queries = jnp.concatenate([v for b in bits for v in (1.0 - b, b)] + none, axis=0) * -FAR
    return keys.astype(BF16), queries.astype(BF16)


def forward_kernel(
    tokens, gm, ids, pos, qkv_w, proj, gain1, gain2, up_w, down_w, gain3, reduce_w,
    x_out, qkv_out, exp_out, inv_out, att_out, hid_out, act_out, slope_out, qkv_t, grad_out, m_all,
    reduce_rows, grad_gain3,
    tok, x_now, pack_t, halo_t, edge_out, edge_in, gm_in, out_all, rows_all, third_all, gm_rows,
    grad_reduce, own_sem, row_out, row_in, t_out, t_in, gm_out_sem, gm_in_sem, gm_own, edge_out_sem,
    edge_in_sem,
):
    step = pl.program_id(0)
    tw, wc = step // 4, lax.rem(step, 4)
    place = Place()
    row_sems, t_sems = (row_out, row_in), (t_out, t_in)
    gm_sems, edge_sems = (gm_out_sem, gm_in_sem), (edge_out_sem, edge_in_sem)

    def own_copies():
        return [
            pltpu.make_async_copy(
                tokens.at[3:7, a : a + n], tok.at[0:4, b : b + n], own_sem.at[at]
            )
            for at, (a, b, n) in enumerate(((3, 0, 25), (0, 25, 3)))
        ]

    def row_copy(at):
        a, b, n = RUNS[at]
        return remote(
            tokens.at[0:3, a : a + n], tok.at[4:7, b : b + n], row_sems, at, place.at(0, -1)
        )

    def t_copy():
        return remote(pack_t.at[wc], halo_t.at[wc], t_sems, wc, place.at(-1, 0))

    def gm_copy(k, part):
        dev, _ = place.holder(k)
        band = lax.rem(place.r + k, 4)
        first = lax.rem(4 * band + 1 - band // 2 + 2 * part, 14)
        slot = lax.rem(place.r + 3, 4)
        src, dst = gm.at[pl.ds(first, 2)], gm_in.at[slot, 2 * part : 2 * part + 2]
        return remote(src, dst, gm_sems, 2 * k + part, dev)

    def gm_local(part):
        band = place.r
        first = lax.rem(4 * band + 1 - band // 2 + 2 * part, 14)
        slot = lax.rem(place.r + 3, 4)
        return pltpu.make_async_copy(
            gm.at[pl.ds(first, 2)], gm_in.at[slot, 2 * part : 2 * part + 2], gm_own.at[part]
        )

    def edge_copy(half):
        return remote(edge_out.at[half], edge_in.at[half], edge_sems, half, place.across())

    @pl.when((tw == 0) & (wc == 0))
    def _():
        for copy in own_copies():
            copy.start()
        sources = [place.at(0, 1), place.at(1, 0), place.across()]
        place.greet(sources + [place.holder(k)[1] for k in (1, 2, 3)], place.holder(0)[1])
        for at in range(5):
            row_copy(at).start()
        qkv_t[...] = qkv_w[...].astype(F32).T.astype(BF16)
        for copy in own_copies():
            copy.wait()

    @pl.when((tw == 0) & (wc == 1))
    def _():
        for k in (1, 2, 3):
            for part in range(2):
                gm_copy(k, part).start()

        @pl.when(place.r == 0)
        def _():
            for part in range(2):
                gm_copy(0, part).start()

        @pl.when(place.r != 0)
        def _():
            for part in range(2):
                gm_local(part).start()

    for window in range(4):

        @pl.when((tw == 0) & (wc == window))
        def _(window=window):
            for at in runs_of(window):
                row_copy(at).wait_recv()

    @pl.when(tw == 0)
    def _():
        block = tok[:, pl.ds(7 * wc, 7)].astype(F32).reshape(49, 16, C)
        pack_t[wc] = pack(block[:, 0:4])
        t_copy().start()
        x_now[...] = block[:, 4:12]

    @pl.when(tw == 1)
    def _():
        t_copy().wait_recv()
        block = tok[:, pl.ds(7 * wc, 7)].astype(F32).reshape(49, 16, C)
        x_now[...] = jnp.concatenate([block[:, 12:16], unpack(halo_t[wc])], axis=1)

    @pl.when(step < 8)
    def _():
        x = x_now[...].reshape(NPOS, C)
        x_out[0] = x.astype(BF16)
        mask_k, mask_q = mask_rows(ids, pos, tw, wc)
        normed, _ = norm_forward(x)
        first_in = (normed * gain1[...]).astype(BF16)
        rows = dot_nt(qkv_t[...], first_in)
        qkv_out[0, 0:C] = (rows[0:C] * (SCALE * LOG2E)).astype(BF16)
        qkv_out[0, C:] = rows[C:].astype(BF16)
        for h in range(HEADS):
            here = slice(HEAD * h, HEAD * (h + 1))
            q = jnp.concatenate([qkv_out[0, HEAD * h : HEAD * (h + 1)], mask_q], axis=0)
            k = jnp.concatenate([qkv_out[0, C + HEAD * h : C + HEAD * (h + 1)], mask_k], axis=0)
            v = qkv_out[0, 2 * C + HEAD * h : 2 * C + HEAD * (h + 1)]
            scores = dot_tn(k, q)
            top = jnp.max(scores, axis=0, keepdims=True)
            expon = jnp.exp2(scores - top)
            inverse = 1.0 / jnp.sum(expon, axis=0, keepdims=True)
            expon = expon.astype(BF16)
            exp_out[0, h] = expon
            inv_out[0, h : h + 1] = inverse
            att_out[0, here] = (dot_nn(v, expon) * inverse).astype(BF16)
        hidden = (x + dot_tn(att_out[0], proj[...])).astype(BF16)
        hid_out[0] = hidden
        hidden = hidden.astype(F32)
        normed, _ = norm_forward(hidden)
        second_in = (normed * gain2[...]).astype(BF16)
        result = hidden
        for part in range(4):
            cols = slice(256 * part, 256 * (part + 1))
            act, slope = gelu_and_slope(dot_nn(second_in, up_w[:, cols]))
            act = act.astype(BF16)
            act_out[0, :, cols] = act
            slope_out[0, :, cols] = slope.astype(BF16)
            result = result + dot_nn(act, down_w[cols])
        out_all[step] = result.astype(BF16)
        edge = jnp.where(place.odd == 1, result[336:392], result[0:56])
        edge_out[tw, wc] = edge.astype(BF16)

    @pl.when((tw == 0) & (wc == 3))
    def _():
        edge_copy(0).start()

    @pl.when(step == 7)
    def _():
        edge_copy(1).start()

    @pl.when(step == 8)
    def _():
        grad_reduce[...] = jnp.zeros_like(grad_reduce)
        grad_gain3[...] = jnp.zeros_like(grad_gain3)
        for k in (1, 2, 3):
            for part in range(2):
                gm_copy(k, part).wait()

        @pl.when(place.r == 0)
        def _():
            for part in range(2):
                gm_copy(0, part).wait()

        @pl.when(place.r != 0)
        def _():
            for part in range(2):
                gm_local(part).wait()

        edge_copy(0).wait()

    @pl.when(step == 9)
    def _():
        edge_copy(1).wait()

    @pl.when(step >= 8)
    def _():
        merge_half(
            step - 8, place.odd, out_all, edge_in, gm_in, gain3, reduce_w, grad_out, m_all,
            grad_gain3, rows_all, third_all, gm_rows, grad_reduce,
        )

    @pl.when(step == 9)
    def _():
        store_blocks(reduce_rows, 0, grad_reduce)
        for at in range(5):
            row_copy(at).wait_send()
        for n in range(4):
            remote(pack_t.at[n], halo_t.at[n], t_sems, n, place.at(-1, 0)).wait_send()


def whole(shape):
    return pl.BlockSpec(shape, lambda *_: (0,) * len(shape))


def by_window(shape):
    return pl.BlockSpec((1,) + shape, lambda s: (jnp.minimum(s, 7),) + (0,) * len(shape))


ANY_SPEC = pl.BlockSpec(memory_space=pl.ANY)
DMA = pltpu.SemaphoreType.DMA


def positions():
    at = jnp.arange(NPOS)
    rows = [at % 8, at // 56, (at // 8) % 7]
    return jnp.concatenate([jnp.stack(rows), jnp.zeros((5, NPOS), at.dtype)]).astype(F32)


def run_forward(tokens, gm, ids, *weights):
    saved = [
        ((NPOS, C), BF16),
        ((3 * C, NPOS), BF16),
        ((HEADS, NPOS, NPOS), BF16),
        ((HEADS, NPOS), F32),
        ((C, NPOS), BF16),
        ((NPOS, C), BF16),
        ((NPOS, HID), BF16),
        ((NPOS, HID), BF16),
    ]
    others = [
        ((3 * C, C), BF16),
        ((8, NPOS, C), BF16),
        ((4, 4, 14, 4, C3), BF16),
        ((4096, 128), BF16),
        ((1, 4 * C), F32),
    ]
    pos = positions()
    return pl.pallas_call(
        forward_kernel,
        grid=(10,),
        out_shape=[jax.ShapeDtypeStruct((8,) + shape, kind) for shape, kind in saved]
        + [jax.ShapeDtypeStruct(shape, kind) for shape, kind in others],
        in_specs=[ANY_SPEC, ANY_SPEC, whole(ids.shape), whole(pos.shape)]
        + [whole(w.shape) for w in weights],
        out_specs=[by_window(shape) for shape, _ in saved] + [whole(shape) for shape, _ in others],
        scratch_shapes=[
            pltpu.VMEM((7, 28, 16, C), BF16),
            pltpu.VMEM((49, 8, C), F32),
            pltpu.VMEM((4, 13, 16, C), BF16),
            pltpu.VMEM((4, 13, 16, C), BF16),
            pltpu.VMEM((2, 4, 56, C), BF16),
            pltpu.VMEM((2, 4, 56, C), BF16),
            pltpu.VMEM((4, 4, 14, 4, C3), BF16),
            pltpu.VMEM((8, NPOS, C), BF16),
            pltpu.VMEM((8, 28, 8, C), F32),
            pltpu.VMEM((448, 4 * C), BF16),
            pltpu.VMEM((448, C3), BF16),
            pltpu.VMEM((4 * C, C3), F32),
            DMA((2,)), DMA((5,)), DMA((5,)), DMA((4,)), DMA((4,)), DMA((8,)), DMA((8,)),
            DMA((2,)), DMA((2,)), DMA((2,)),
        ],
        compiler_params=pltpu.CompilerParams(
            vmem_limit_bytes=60 * MIB, collective_id=1, has_side_effects=True
        ),
        name="forward",
    )(tokens, gm, ids, pos, *weights)


ORDERS = (("x", "y", "z"), ("y", "z", "x"), ("z", "x", "y"))


def torus(n_tm):
    return {32: (4, 2, 4), 4: (2, 1, 2)}[n_tm]


class Torus:
    def __init__(self, dims):
        self.dims = dims
        _, n_yl, n_z = dims
        m, r = lax.axis_index("tm"), lax.axis_index("rows")
        self.core = lax.rem(r, 2)
        self.size = dims[0]
        self.at = {
            "x": m // (n_yl * n_z),
            "y": (r // 2) * n_yl + lax.rem(m // n_z, n_yl),
            "z": lax.rem(m, n_z),
        }

    def device(self, core=None, **moved):
        _, n_yl, n_z = self.dims
        at = {**self.at, **moved}
        core = self.core if core is None else core
        m = (at["x"] * n_yl + lax.rem(at["y"], n_yl)) * n_z + at["z"]
        return (m, (at["y"] // n_yl) * 2 + core)

    def partners(self, axis):
        places = [lax.rem(self.at[axis] + j, self.size) for j in range(1, self.size)]
        return [(place, self.device(**{axis: place})) for place in places]

    def other(self):
        return self.device(core=1 - self.core)

    def everyone(self):
        return [self.other()] + [dev for axis in "xyz" for _, dev in self.partners(axis)]


def at_rows(start, length):
    return pl.ds(pl.multiple_of(start, 16), length)


class Sum:
    def __init__(self, here, lengths, whole_last, source, total, base, scratch):
        self.here, self.lengths, self.whole_last = here, lengths, whole_last
        self.source, self.total, self.base = source, total, base
        self.core_in, *rest = scratch
        self.accs, self.ins = rest[0:3], rest[3:6]
        self.core_sems, self.rs_sems, self.ag_sems, self.back_sems = (
            tuple(rest[6 + 2 * n : 8 + 2 * n]) for n in range(4)
        )

    @staticmethod
    def scratch(size, lengths, whole_last):
        most, length = max(lengths), max(lengths)
        shapes = [(3, most, 128)]
        accs, ins = [], []
        for s in range(3):
            accs.append((3, length, 128))
            length = length if s == 2 and whole_last else length // size
            ins.append((3, size - 1, length, 128))
        sems = [(3,), (3,), (9 * (size - 1),), (9 * (size - 1),), (9 * (size - 1),), (9 * (size - 1),), (3,), (3,)]
        return [pltpu.VMEM(shape, BF16) for shape in shapes + accs + ins] + [DMA(n) for n in sems]

    def half(self, core, p):
        return core * sum(self.lengths) + sum(self.lengths[:p])

    def piece(self, p, s):
        start, length = self.half(self.here.core, p), self.lengths[p]
        for n in range(s):
            if not (n == 2 and self.whole_last):
                length = length // self.here.size
                start = start + self.here.at[ORDERS[p][n]] * length
        return start, length

    def core_copy(self, p):
        start = self.half(1 - self.here.core, p)
        return remote(
            self.source.at[at_rows(start, self.lengths[p])],
            self.core_in.at[p, 0 : self.lengths[p]],
            self.core_sems, p, self.here.other(),
        )

    def rs_copies(self, p, s):
        _, length = self.piece(p, s)
        whole_piece = s == 3 and self.whole_last
        return [
            remote(
                self.accs[s - 1].at[p, 0:length]
                if whole_piece
                else self.accs[s - 1].at[p, at_rows(place * length, length)],
                self.ins[s - 1].at[p, j, 0:length],
                self.rs_sems, (3 * (s - 1) + p) * (self.here.size - 1) + j, dev,
            )
            for j, (place, dev) in enumerate(self.here.partners(ORDERS[p][s - 1]))
        ]

    def ag_copies(self, p, s):
        start, length = self.piece(p, s)
        region = self.total.at[at_rows(self.base + start, length)]
        return [
            remote(region, region, self.ag_sems, (3 * (s - 1) + p) * (self.here.size - 1) + j, dev)
            for j, (_, dev) in enumerate(self.here.partners(ORDERS[p][s - 1]))
        ]

    def back_copy(self, p):
        start, length = self.piece(p, 0)
        region = self.total.at[at_rows(self.base + start, length)]
        return remote(region, region, self.back_sems, p, self.here.other())

    def start(self):
        for p in range(3):
            self.core_copy(p).start()

    def reduce(self, s):
        for p in range(3):
            start, length = self.piece(p, s)
            if s == 0:
                self.core_copy(p).wait_recv()
                value = self.source[at_rows(start, length)].astype(F32)
                value = value + self.core_in[p, 0:length].astype(F32)
            else:
                for copy in self.rs_copies(p, s):
                    copy.wait_recv()
                if s == 3 and self.whole_last:
                    value = self.accs[2][p, 0:length].astype(F32)
                else:
                    place = self.here.at[ORDERS[p][s - 1]]
                    value = self.accs[s - 1][p, at_rows(place * length, length)].astype(F32)
                for j in range(self.here.size - 1):
                    value = value + self.ins[s - 1][p, j, 0:length].astype(F32)
            if s < 3:
                self.accs[s][p, 0:length] = value.astype(BF16)
                for copy in self.rs_copies(p, s + 1):
                    copy.start()
            else:
                self.total[at_rows(self.base + start, length)] = value.astype(BF16)
                for copy in self.ag_copies(p, 2 if self.whole_last else 3):
                    copy.start()

    def gather(self, s):
        for p in range(3):
            for copy in self.ag_copies(p, s):
                copy.wait_recv()
            for copy in self.ag_copies(p, s - 1) if s > 1 else [self.back_copy(p)]:
                copy.start()

    def finish(self):
        for p in range(3):
            self.back_copy(p).wait()
            self.core_copy(p).wait_send()
            for s in (1, 2, 3):
                for copy in self.rs_copies(p, s):
                    copy.wait_send()
                if s < 3 or not self.whole_last:
                    for copy in self.ag_copies(p, s):
                        copy.wait_send()


SUMS = ((2048, 2048, 1024), (512, 256, 256))
SUM_ROWS = tuple(2 * sum(lengths) for lengths in SUMS)
SUM_BASES = (0, SUM_ROWS[0])


def backward_kernel(
    dims, grad_out, att_a, hid_in, act_in, slope_in, x_in, qkv_in, inv_in, att_in, exp_hbm,
    qkv_t, proj, gain1, gain2, up_w, down_w, reduce_rows, grad_gain3, pieces,
    totals, merged, grad_tokens,
    exp_two, grad_hidden_all, grad_att_all, grad_rows_t, grad_qkv_t, grad_proj, grad_up,
    grad_down_t, grad_gain1, grad_gain2, late, final, pack_t, halo_t, early_rows, late_rows, total,
    in_sem, exp_sem,
    t_out, t_in, row_out, row_in, own_sem, m_out, m_in, m_own, total_sem, *sum_scratch,
):
    step = pl.program_id(0)
    tw, wc = 1 - lax.rem(step, 8) // 4, lax.rem(step, 4)
    window = 4 * tw + wc
    first_phase, second_phase = step < 8, step >= 8
    place, here = Place(), Torus(dims)
    t_sems, row_sems, m_sems = (t_out, t_in), (row_out, row_in), (m_out, m_in)
    each = len(sum_scratch) // 2
    early, last = (
        Sum(here, SUMS[n], True, rows, total, SUM_BASES[n], sum_scratch[each * n : each * (n + 1)])
        for n, rows in enumerate((early_rows, late_rows))
    )

    def reduce_copy():
        return pltpu.make_async_copy(reduce_rows, early_rows.at[0:4096], in_sem.at[0])

    def exp_copy(at):
        source = 4 * (1 - lax.rem(at, 8) // 4) + lax.rem(at, 4)
        slot = lax.rem(at, 2)
        return pltpu.make_async_copy(exp_hbm.at[source], exp_two.at[slot], exp_sem.at[slot])

    def m_ends(k, n):
        c = lax.rem(place.r + k + 3, 4)
        start = 4 * place.r + 1 - place.r // 2
        first = (1 - place.odd, 3 - place.odd, 3)[n]
        count = (2, 1, 1)[n]
        return (
            pieces.at[c, pl.ds(first, count)],
            merged.at[pl.ds(lax.rem(start + first, 14), count)],
        )

    def m_copy(k, n):
        return remote(*m_ends(k, n), m_sems, 3 * k + n, place.owner(k)[0])

    def m_local(n):
        return pltpu.make_async_copy(*m_ends(0, n), m_own.at[n])

    def m_each(act_remote, act_local):
        for k in (1, 2, 3):
            act_remote(k, 0)
            act_remote(k, 1)

        @pl.when(place.r == 0)
        def _():
            act_remote(0, 0)
            act_remote(0, 1)

        @pl.when(place.r != 0)
        def _():
            act_local(0)
            act_local(1)

    def t_copy(n):
        return remote(pack_t.at[n], halo_t.at[n], t_sems, n, place.at(1, 0))

    def row_copy(at):
        a, b, n = RUNS[at]
        part, first = (at, 0) if at < 3 else (3, b - 21)
        return remote(
            final.at[part, 4:7, first : first + n], grad_tokens.at[0:3, a : a + n],
            row_sems, at, place.at(0, 1),
        )

    def own_copy(at):
        a, b, n = RUNS[at]
        part, first = (at, 0) if at < 3 else (3, b - 21)
        return pltpu.make_async_copy(
            final.at[part, 0:4, first : first + n], grad_tokens.at[3:7, a : a + n], own_sem.at[at]
        )

    def total_copy(n):
        region = pl.ds(SUM_BASES[n], SUM_ROWS[n])
        return pltpu.make_async_copy(total.at[region], totals.at[region], total_sem.at[n])

    @pl.when(step == 0)
    def _():
        reduce_copy().start()
        for ref in (grad_qkv_t, grad_proj, grad_up, grad_down_t, grad_gain1, grad_gain2):
            ref[...] = jnp.zeros_like(ref)
        sources = [place.at(0, -1), place.at(-1, 0)] + [place.owner(k)[1] for k in (1, 2, 3)]
        place.greet(sources + here.everyone(), place.owner(0)[1])
        m_each(lambda k, n: m_copy(k, n).start(), lambda n: m_local(n).start())

        @pl.when(place.odd == 1)
        def _():
            for k in (1, 2, 3):
                m_copy(k, 2).start()
            m_local(2).start()

    @pl.when(first_phase)
    def _():
        grad_rows = grad_out[0]
        normed2, inverse2 = norm_forward(hid_in[0].astype(F32))
        second_in = (normed2 * gain2[...]).astype(BF16)
        grad_second = jnp.zeros((NPOS, C), F32)
        for part in range(4):
            cols = slice(256 * part, 256 * (part + 1))
            grad_down_t[:, cols] += dot_tn(grad_rows, act_in[0, :, cols])
            grad_act = dot_nt(grad_rows, down_w[cols])
            grad_up_in = (grad_act * slope_in[0, :, cols].astype(F32)).astype(BF16)
            grad_up[:, cols] += dot_tn(second_in, grad_up_in)
            grad_second = grad_second + dot_nt(grad_up_in, up_w[:, cols])
        grad_gain2[...] += jnp.sum(grad_second * normed2, axis=0, keepdims=True)
        back = norm_backward(normed2, inverse2, gain2[...], grad_second)
        grad_hidden = grad_rows.astype(F32) + back
        grad_hidden_all[window] = grad_hidden
        grad_hidden_b = grad_hidden.astype(BF16)
        grad_proj[...] += dot_nn(att_a[0], grad_hidden_b)
        grad_att_all[window] = dot_nt(proj[...], grad_hidden_b).astype(BF16)

    @pl.when(step == 7)
    def _():
        store_blocks(early_rows, 16, grad_up[...])
        store_blocks(early_rows, 24, grad_down_t[...].T)
        store_blocks(early_rows, 32, grad_proj[...])
        rows = [grad_gain2[:, 0:128], grad_gain2[:, 128:256]]
        rows += [grad_gain3[:, 128 * n : 128 * (n + 1)] for n in range(8)]
        rows.append(jnp.zeros((6, 128), F32))
        early_rows[34 * 256 : 34 * 256 + 16] = jnp.concatenate(rows, axis=0).astype(BF16)
        early_rows[34 * 256 + 16 :] = jnp.zeros((SUM_ROWS[0] - 34 * 256 - 16, 128), BF16)
        reduce_copy().wait()
        early.start()

    for at, run in (
        (9, lambda: early.reduce(0)),
        (11, lambda: early.reduce(1)),
        (12, lambda: early.reduce(2)),
        (13, lambda: early.reduce(3)),
        (14, lambda: early.gather(2)),
    ):
        pl.when(step == at)(run)

    @pl.when((step >= 7) & (step < 15))
    def _():
        exp_copy(step + 1).start()

    @pl.when(second_phase)
    def _():
        exp_copy(step).wait()
        slot = lax.rem(step, 2)
        for h in range(HEADS):
            at_q = slice(HEAD * h, HEAD * (h + 1))
            at_k = slice(C + HEAD * h, C + HEAD * (h + 1))
            at_v = slice(2 * C + HEAD * h, 2 * C + HEAD * (h + 1))
            expon = exp_two[slot, h]
            incoming = grad_att_all[window, at_q].astype(F32) * inv_in[0, h : h + 1]
            incoming = incoming.astype(BF16)
            inner = incoming.astype(F32) * att_in[0, at_q].astype(F32)
            inner = jnp.sum(inner, axis=0, keepdims=True)
            grad_probs = dot_tn(qkv_in[0, at_v], incoming)
            grad_scores = (expon.astype(F32) * (grad_probs - inner)).astype(BF16)
            grad_rows_t[at_q] = (dot_nn(qkv_in[0, at_k], grad_scores) * SCALE).astype(BF16)
            grad_rows_t[at_k] = (dot_nt(qkv_in[0, at_q], grad_scores) * LN2).astype(BF16)
            grad_rows_t[at_v] = dot_nt(incoming, expon).astype(BF16)
        normed1, inverse1 = norm_forward(x_in[0].astype(F32))
        first_in = (normed1 * gain1[...]).astype(BF16)
        grad_qkv_t[...] += dot_nn(grad_rows_t[...], first_in)
        grad_first = dot_tn(grad_rows_t[...], qkv_t[...])
        grad_gain1[...] += jnp.sum(grad_first * normed1, axis=0, keepdims=True)
        back = norm_backward(normed1, inverse1, gain1[...], grad_first)
        block = (grad_hidden_all[window] + back).reshape(49, 8, C)

        @pl.when(tw == 1)
        def _():
            late[wc] = block[:, 0:4].astype(BF16)
            pack_t[wc] = pack(block[:, 4:8])
            t_copy(wc).start()

        @pl.when(tw == 0)
        def _():
            t_copy(wc).wait_recv()
            frames = jnp.concatenate([unpack(halo_t[wc]), block, late[wc].astype(F32)], axis=1)
            final[wc] = frames.astype(BF16).reshape(7, 7, 16, C)

    @pl.when(step == 15)
    def _():
        store_blocks(late_rows, 0, grad_qkv_t[...].T)
        rows = [grad_gain1[:, 0:128], grad_gain1[:, 128:256], jnp.zeros((14, 128), F32)]
        late_rows[1536:1552] = jnp.concatenate(rows, axis=0).astype(BF16)
        late_rows[1552:] = jnp.zeros((SUM_ROWS[1] - 1552, 128), BF16)
        last.start()

    for part in range(4):

        @pl.when(step == 12 + part)
        def _(part=part):
            for at in runs_of(part):
                row_copy(at).start()
                own_copy(at).start()

    @pl.when(step == 15)
    def _():
        last.reduce(0)
        early.gather(1)
        last.reduce(1)
        last.reduce(2)
        last.reduce(3)
        early.finish()
        total_copy(0).start()
        last.gather(2)
        last.gather(1)
        for at in range(5):
            row_copy(at).wait()
            own_copy(at).wait()
        for n in range(4):
            t_copy(n).wait_send()
        m_each(lambda k, n: m_copy(k, n).wait(), lambda n: m_local(n).wait())

        @pl.when(place.odd == 1)
        def _():
            for k in (1, 2, 3):
                m_copy(k, 2).wait_send()
            m_local(2).wait()
            m_copy(2, 2).wait_recv()

        @pl.when(place.odd == 0)
        def _():
            for k in (1, 3):
                m_copy(k, 2).wait_recv()

        last.finish()
        total_copy(1).start()
        for n in range(2):
            total_copy(n).wait()


def run_backward(n_tm, grad_out, saved, *weights):
    sums = [(3 * C, C), (C, C), (C, HID), (C, HID), (1, C), (1, C)]
    dims = torus(n_tm)
    x, qkv, expon, inverse, att, hid, act, slope = saved
    *vmem_weights, _, grad_gain3, _ = weights

    def window(step):
        return 4 * (1 - lax.rem(step, 8) // 4) + lax.rem(step, 4)

    def in_first(array):
        shape = array.shape[1:]
        return pl.BlockSpec(
            (1,) + shape, lambda s: (window(jnp.minimum(s, 7)),) + (0,) * len(shape)
        )

    def in_second(array):
        shape = array.shape[1:]
        return pl.BlockSpec(
            (1,) + shape, lambda s: (window(jnp.maximum(s, 8)),) + (0,) * len(shape)
        )

    first, second = (grad_out, att, hid, act, slope), (x, qkv, inverse, att)
    return pl.pallas_call(
        lambda *refs: backward_kernel(dims, *refs),
        grid=(16,),
        out_shape=[
            jax.ShapeDtypeStruct((sum(SUM_ROWS), 128), BF16),
            jax.ShapeDtypeStruct((14, 14, 4, C3), BF16),
            jax.ShapeDtypeStruct((7, 28, 16, C), BF16),
        ],
        in_specs=[in_first(array) for array in first]
        + [in_second(array) for array in second]
        + [ANY_SPEC]
        + [whole(w.shape) for w in vmem_weights]
        + [ANY_SPEC, whole(grad_gain3.shape), ANY_SPEC],
        out_specs=[ANY_SPEC] * 3,
        scratch_shapes=[
            pltpu.VMEM((2, HEADS, NPOS, NPOS), BF16),
            pltpu.VMEM((8, NPOS, C), F32),
            pltpu.VMEM((8, C, NPOS), BF16),
            pltpu.VMEM((3 * C, NPOS), BF16),
        ]
        + [pltpu.VMEM(shape, F32) for shape in sums]
        + [
            pltpu.VMEM((4, 49, 4, C), BF16),
            pltpu.VMEM((4, 7, 7, 16, C), BF16),
            pltpu.VMEM((4, 13, 16, C), BF16),
            pltpu.VMEM((4, 13, 16, C), BF16),
            *(pltpu.VMEM((n, 128), BF16) for n in (*SUM_ROWS, sum(SUM_ROWS))),
            DMA((1,)), DMA((2,)),
            DMA((4,)), DMA((4,)), DMA((5,)), DMA((5,)), DMA((5,)), DMA((12,)), DMA((12,)), DMA((3,)),
            DMA((2,)),
        ]
        + [shape for lengths in SUMS for shape in Sum.scratch(dims[0], lengths, True)],
        compiler_params=pltpu.CompilerParams(
            vmem_limit_bytes=58 * MIB, collective_id=2, has_side_effects=True
        ),
        name="backward",
    )(*first, *second, expon, *weights)


def spread_kernel(
    reduce_in, up_in, down_in, proj_in, qkv_in, gains_in, gain1_in,
    qkv, proj, up, down, reduce_w, gain1, gain2, gain3,
):
    step = pl.program_id(0)
    for ref, blocks in ((qkv, qkv_in), (up, up_in), (down, down_in), (reduce_w, reduce_in)):
        for b in range(ref.shape[1] // 128):
            ref[:, 128 * b : 128 * (b + 1)] = blocks[b].astype(F32)

    @pl.when(step == 0)
    def _():
        for b in range(2):
            proj[:, 128 * b : 128 * (b + 1)] = proj_in[b].astype(F32)
        gains, first = gains_in[0, 0:16].astype(F32), gain1_in[0, 0:16].astype(F32)
        for ref, rows, start in ((gain1, first, 0), (gain2, gains, 0), (gain3, gains, 2)):
            for n in range(ref.shape[1] // 128):
                ref[:, 128 * n : 128 * (n + 1)] = rows[start + n : start + n + 1]


def run_spread(totals):
    shapes = [(C, 3 * C), (C, C), (C, HID), (HID, C), (4 * C, C3), (1, C), (1, C), (1, 4 * C)]
    wide = lambda count: pl.BlockSpec((256, 256), lambda s: (0, jnp.minimum(s, count - 1)))

    def blocks(count, first, steps):
        return pl.BlockSpec(
            (count, 256, 128), lambda s: (first // count + jnp.minimum(s, steps - 1), 0, 0)
        )

    return pl.pallas_call(
        spread_kernel,
        grid=(4,),
        out_shape=[jax.ShapeDtypeStruct(shape, F32) for shape in shapes],
        in_specs=[
            blocks(4, 0, 4), blocks(2, 16, 4), blocks(2, 24, 4), blocks(2, 32, 1), blocks(2, 40, 3),
            blocks(1, 34, 1), blocks(1, 46, 1),
        ],
        out_specs=[
            wide(3),
            whole((C, C)),
            wide(4),
            pl.BlockSpec((256, C), lambda s: (s, 0)),
            pl.BlockSpec((256, C3), lambda s: (s, 0)),
            whole((1, C)),
            whole((1, C)),
            whole((1, 4 * C)),
        ],
        compiler_params=pltpu.CompilerParams(vmem_limit_bytes=32 * MIB),
        name="spread",
    )(*[totals] * 7)


def local(
    tokens, region_ids, gain_attn, qkv_weight, proj_weight, gain_mlp, up_weight, down_weight,
    gain_merge, reduce_weight, grad_merged,
):
    n_tm = lax.axis_size("tm")
    gain1, gain2, gain3 = (g.reshape(1, -1) for g in (gain_attn, gain_mlp, gain_merge))
    *saved, qkv_t, grad_out, pieces, reduce_rows, grad_gain3 = run_forward(
        tokens.transpose(1, 2, 0, 3), grad_merged.transpose(1, 2, 0, 3),
        region_ids.transpose(1, 0, 2), qkv_weight, proj_weight, gain1, gain2, up_weight, down_weight,
        gain3, reduce_weight,
    )
    totals, merged, grad_tokens = run_backward(
        n_tm, grad_out, saved, qkv_t, proj_weight, gain1, gain2, up_weight, down_weight,
        reduce_rows, grad_gain3, pieces,
    )
    *grads, gain1, gain2, gain3 = run_spread(totals.reshape(-1, 256, 128))
    return (
        merged.transpose(2, 0, 1, 3),
        grad_tokens.transpose(2, 0, 1, 3),
        *grads,
        gain1.reshape(-1),
        gain2.reshape(-1),
        gain3.reshape(-1),
    )


def solution(mesh):
    placed = (
        P("tm", "rows", None, None),
        P("tm", "rows", None),
        P(), P(), P(), P(), P(), P(), P(), P(),
        P(("tm", "rows"), None, None, None),
    )
    return jax.shard_map(
        local,
        mesh=mesh,
        in_specs=placed,
        out_specs=(
            P(("tm", "rows"), None, None, None),
            P("tm", "rows", None, None),
            P(), P(), P(), P(), P(), P(), P(), P(),
        ),
        check_vma=False,
    )
```

```python
import math

import jax
import jax.numpy as jnp
from jax import lax
from jax.experimental import pallas as pl
from jax.experimental.pallas import tpu as pltpu
from jax.sharding import PartitionSpec as P

HEADS = 8
HEAD = 32
NPOS = 392
C = 256
HID = 1024
C3 = 512
EPS = 1e-05
LOG2E = 1.4426950408889634
LN2 = 0.6931471805599453
SCALE = 1.0 / math.sqrt(HEAD)
FAR = 1e30
F32 = jnp.float32
BF16 = jnp.bfloat16
MIB = 1024 * 1024


def dot_nn(left, right):
    return lax.dot_general(left, right, (((1,), (0,)), ((), ())), preferred_element_type=F32)


def dot_nt(left, right):
    return lax.dot_general(left, right, (((1,), (1,)), ((), ())), preferred_element_type=F32)


def dot_tn(left, right):
    return lax.dot_general(left, right, (((0,), (0,)), ((), ())), preferred_element_type=F32)


def norm_forward(values):
    centre = jnp.mean(values, axis=-1, keepdims=True)
    centred = values - centre
    spread = jnp.mean(centred * centred, axis=-1, keepdims=True)
    inverse = lax.rsqrt(spread + EPS)
    return centred * inverse, inverse


def norm_backward(normed, inverse, gain, incoming):
    gated = incoming * gain
    first_mean = jnp.mean(gated, axis=-1, keepdims=True)
    second_mean = jnp.mean(gated * normed, axis=-1, keepdims=True)
    return inverse * (gated - first_mean - normed * second_mean)


def gelu_and_slope(up):
    size = jnp.abs(up)
    t = pl.reciprocal(1.0 + (0.3275911 * 0.7071067811865476) * size, approx=True)
    bell = jnp.exp2((-0.5 * LOG2E) * (up * up))
    series = 0.5 * 1.061405429 * t - 0.5 * 1.453152027
    series = series * t + 0.5 * 1.421413741
    series = series * t - 0.5 * 0.284496736
    series = series * t + 0.5 * 0.254829592
    tail = series * t * bell
    cdf = jnp.where(up >= 0.0, 1.0 - tail, tail)
    return up * cdf, cdf + up * (bell * 0.3989422804014327)


MESH = pl.DeviceIdType.MESH
RUNS = ((3, 0, 7), (10, 7, 7), (17, 14, 7), (24, 21, 4), (0, 25, 3))


def runs_of(wc):
    return range(wc, wc + 1) if wc < 3 else range(3, 5)


class Place:
    def __init__(self):
        self.m, self.r = lax.axis_index("tm"), lax.axis_index("rows")
        self.n_tm = lax.axis_size("tm")
        self.odd = lax.rem(self.r, 2)
        self.edge = jnp.where(self.r == 0, 1, 0)

    def at(self, dm, dr):
        return (lax.rem(self.m + dm + self.n_tm, self.n_tm), lax.rem(self.r + dr + 4, 4))

    def across(self):
        return (self.m, 3 - self.r)

    def holder(self, k):
        r = lax.rem(self.r - k + 4, 4)
        return self.at(-self.edge, k), self.at(jnp.where(r == 0, 1, 0), -k)

    def owner(self, k):
        r = lax.rem(self.r + k, 4)
        return self.at(jnp.where(r == 0, 1, 0), k), self.at(-self.edge, -k)

    def greet(self, sources, extra):
        barrier = pltpu.get_barrier_semaphore()
        for dev in sources:
            pl.semaphore_signal(barrier, inc=1, device_id=dev, device_id_type=MESH)

        @pl.when(self.r == 0)
        def _():
            pl.semaphore_signal(barrier, inc=1, device_id=extra, device_id_type=MESH)
            pl.semaphore_wait(barrier, len(sources) + 1)

        @pl.when(self.r != 0)
        def _():
            pl.semaphore_wait(barrier, len(sources))


def remote(src, dst, sems, n, dev):
    return pltpu.make_async_remote_copy(
        src_ref=src, dst_ref=dst, send_sem=sems[0].at[n], recv_sem=sems[1].at[n],
        device_id=dev, device_id_type=MESH,
    )


def pack(quarters):
    padded = jnp.concatenate([quarters, jnp.zeros((3, 4, C), F32)], axis=0).reshape(13, 4, 4, C)
    return jnp.concatenate([padded[:, n] for n in range(4)], axis=1).astype(BF16)


def unpack(packed):
    wide = packed.astype(F32)
    parts = [wide[:, 4 * n : 4 * (n + 1)].reshape(13, 1, 4, C) for n in range(4)]
    return jnp.concatenate(parts, axis=1).reshape(52, 4, C)[0:49]


def store_blocks(flat, first, values):
    height, width = values.shape
    for a in range(height // 256):
        for b in range(width // 128):
            at = 256 * (first + a * (width // 128) + b)
            part = values[256 * a : 256 * (a + 1), 128 * b : 128 * (b + 1)]
            flat[at : at + 256] = part.astype(BF16)


def column_runs(wc):
    if wc < 3:
        return [(7 * wc + 3, 0, 7)]
    return [(24, 0, 4), (0, 4, 7)]


def merge_half(
    tw, odd, out_all, edge, gm, gain3, reduce_w, grad_out, m_all, grad_gain, rows, third_all, gm_rows,
    grad_reduce,
):
    for wc in range(4):
        block = out_all[4 * tw + wc].astype(F32).reshape(7, 7, 8, C)
        strip = edge[tw, wc].astype(F32).reshape(7, 8, C)
        for start, first, last in column_runs(wc):
            cols = slice(start, start + last - first)
            rows[pl.ds(1 - odd, 7), cols] = block[:, first:last]
            rows[7 * odd, cols] = strip[first:last]

    gain = gain3[...]
    for a in range(4):
        upper = rows[2 * a].reshape(14, 2, 8, C)
        lower = rows[2 * a + 1].reshape(14, 2, 8, C)
        joined = jnp.concatenate(
            [upper[:, 0], lower[:, 0], upper[:, 1], lower[:, 1]], axis=-1
        ).reshape(112, 4 * C)
        normed, inverse = norm_forward(joined)
        third = normed * gain
        merged = dot_nn(third.astype(BF16), reduce_w[...]).reshape(14, 8, C3)
        m_all[2 * tw, a] = merged[:, 0:4].astype(BF16)
        m_all[2 * tw + 1, a] = merged[:, 4:8].astype(BF16)
        grads = jnp.concatenate(
            [gm[2 * tw, a].astype(F32), gm[2 * tw + 1, a].astype(F32)], axis=1
        )
        grads = grads.reshape(112, C3).astype(BF16)
        gz = dot_nt(grads, reduce_w[...])
        gz_sum = jnp.sum(gz * normed, axis=0, keepdims=True)
        if a == 0:
            counted = jnp.where((odd == 0) & (tw == 1), 0.0, 1.0)
        elif a == 3:
            counted = jnp.where((odd == 1) & (tw == 0), 0.0, 1.0)
        else:
            counted = None
        if counted is not None:
            third = third * counted
            gz_sum = gz_sum * counted
        grad_gain[...] += gz_sum
        third_all[112 * a : 112 * (a + 1)] = third.astype(BF16)
        gm_rows[112 * a : 112 * (a + 1)] = grads
        back = norm_backward(normed, inverse, gain, gz).reshape(14, 8, 4 * C)
        pieces = [back[:, :, C * n : C * (n + 1)].reshape(14, 1, 8, C) for n in range(4)]
        rows[2 * a] = jnp.concatenate([pieces[0], pieces[2]], axis=1).reshape(28, 8, C)
        rows[2 * a + 1] = jnp.concatenate([pieces[1], pieces[3]], axis=1).reshape(28, 8, C)
    grad_reduce[...] += dot_tn(third_all[...], gm_rows[...])
    for wc in range(4):
        runs = [
            rows[pl.ds(1 - odd, 7), start : start + last - first]
            for start, first, last in column_runs(wc)
        ]
        block = runs[0] if len(runs) == 1 else jnp.concatenate(runs, axis=1)
        grad_out[4 * tw + wc] = block.reshape(NPOS, C).astype(BF16)


def mask_rows(ids, pos, tw, wc):
    lane = lax.broadcasted_iota(jnp.int32, (1, 28), 1)
    first = lane == 7 * wc
    here = (lane >= 7 * wc) & (lane < 7 * wc + 7)
    frames = ids[0, pl.ds(pl.multiple_of(8 * tw, 8), 8), :]
    rows = ids[:, pl.ds(pl.multiple_of(8 * tw, 8), 8), :]

    def count(bits, kept):
        kept_bits = jnp.where(kept, bits.astype(F32), 0.0)
        return jnp.sum(jnp.sum(kept_bits, axis=0, keepdims=True), axis=1, keepdims=True)

    past = [
        count((frames >> 2) & 1, first),
        count(jnp.concatenate([(rows[i, 0:1] >> 1) & 1 for i in range(7)], axis=0), first),
        count(frames[0:1] & 1, here),
    ]
    bits = [
        jnp.where(pos[n : n + 1] >= extent - past[n], 1.0, 0.0)
        for n, extent in enumerate((8.0, 7.0, 7.0))
    ]
    none = [jnp.zeros((10, NPOS), F32)]
    keys = jnp.concatenate([v for b in bits for v in (b, 1.0 - b)] + none, axis=0)
    queries = jnp.concatenate([v for b in bits for v in (1.0 - b, b)] + none, axis=0) * -FAR
    return keys.astype(BF16), queries.astype(BF16)


def forward_kernel(
    tokens, gm, ids, pos, qkv_w, proj, gain1, gain2, up_w, down_w, gain3, reduce_w,
    x_out, qkv_out, exp_out, inv_out, att_out, hid_out, act_out, slope_out, qkv_t, grad_out, m_all,
    reduce_rows, grad_gain3,
    tok, x_now, pack_t, halo_t, edge_out, edge_in, gm_in, out_all, rows_all, third_all, gm_rows,
    grad_reduce, own_sem, row_out, row_in, t_out, t_in, gm_out_sem, gm_in_sem, gm_own, edge_out_sem,
    edge_in_sem,
):
    step = pl.program_id(0)
    tw, wc = step // 4, lax.rem(step, 4)
    place = Place()
    row_sems, t_sems = (row_out, row_in), (t_out, t_in)
    gm_sems, edge_sems = (gm_out_sem, gm_in_sem), (edge_out_sem, edge_in_sem)

    def own_copies():
        return [
            pltpu.make_async_copy(
                tokens.at[3:7, a : a + n], tok.at[0:4, b : b + n], own_sem.at[at]
            )
            for at, (a, b, n) in enumerate(((3, 0, 25), (0, 25, 3)))
        ]

    def row_copy(at):
        a, b, n = RUNS[at]
        return remote(
            tokens.at[0:3, a : a + n], tok.at[4:7, b : b + n], row_sems, at, place.at(0, -1)
        )

    def t_copy():
        return remote(pack_t.at[wc], halo_t.at[wc], t_sems, wc, place.at(-1, 0))

    def gm_copy(k, part):
        dev, _ = place.holder(k)
        band = lax.rem(place.r + k, 4)
        first = lax.rem(4 * band + 1 - band // 2 + 2 * part, 14)
        slot = lax.rem(place.r + 3, 4)
        src, dst = gm.at[pl.ds(first, 2)], gm_in.at[slot, 2 * part : 2 * part + 2]
        return remote(src, dst, gm_sems, 2 * k + part, dev)

    def gm_local(part):
        band = place.r
        first = lax.rem(4 * band + 1 - band // 2 + 2 * part, 14)
        slot = lax.rem(place.r + 3, 4)
        return pltpu.make_async_copy(
            gm.at[pl.ds(first, 2)], gm_in.at[slot, 2 * part : 2 * part + 2], gm_own.at[part]
        )

    def edge_copy(half):
        return remote(edge_out.at[half], edge_in.at[half], edge_sems, half, place.across())

    @pl.when((tw == 0) & (wc == 0))
    def _():
        for copy in own_copies():
            copy.start()
        sources = [place.at(0, 1), place.at(1, 0), place.across()]
        place.greet(sources + [place.holder(k)[1] for k in (1, 2, 3)], place.holder(0)[1])
        for at in range(5):
            row_copy(at).start()
        qkv_t[...] = qkv_w[...].astype(F32).T.astype(BF16)
        for copy in own_copies():
            copy.wait()

    @pl.when((tw == 0) & (wc == 1))
    def _():
        for k in (1, 2, 3):
            for part in range(2):
                gm_copy(k, part).start()

        @pl.when(place.r == 0)
        def _():
            for part in range(2):
                gm_copy(0, part).start()

        @pl.when(place.r != 0)
        def _():
            for part in range(2):
                gm_local(part).start()

    for window in range(4):

        @pl.when((tw == 0) & (wc == window))
        def _(window=window):
            for at in runs_of(window):
                row_copy(at).wait_recv()

    @pl.when(tw == 0)
    def _():
        block = tok[:, pl.ds(7 * wc, 7)].astype(F32).reshape(49, 16, C)
        pack_t[wc] = pack(block[:, 0:4])
        t_copy().start()
        x_now[...] = block[:, 4:12]

    @pl.when(tw == 1)
    def _():
        t_copy().wait_recv()
        block = tok[:, pl.ds(7 * wc, 7)].astype(F32).reshape(49, 16, C)
        x_now[...] = jnp.concatenate([block[:, 12:16], unpack(halo_t[wc])], axis=1)

    @pl.when(step < 8)
    def _():
        x = x_now[...].reshape(NPOS, C)
        x_out[0] = x.astype(BF16)
        mask_k, mask_q = mask_rows(ids, pos, tw, wc)
        normed, _ = norm_forward(x)
        first_in = (normed * gain1[...]).astype(BF16)
        rows = dot_nt(qkv_t[...], first_in)
        qkv_out[0, 0:C] = (rows[0:C] * (SCALE * LOG2E)).astype(BF16)
        qkv_out[0, C:] = rows[C:].astype(BF16)
        for h in range(HEADS):
            here = slice(HEAD * h, HEAD * (h + 1))
            q = jnp.concatenate([qkv_out[0, HEAD * h : HEAD * (h + 1)], mask_q], axis=0)
            k = jnp.concatenate([qkv_out[0, C + HEAD * h : C + HEAD * (h + 1)], mask_k], axis=0)
            v = qkv_out[0, 2 * C + HEAD * h : 2 * C + HEAD * (h + 1)]
            scores = dot_tn(k, q)
            top = jnp.max(scores, axis=0, keepdims=True)
            expon = jnp.exp2(scores - top)
            inverse = 1.0 / jnp.sum(expon, axis=0, keepdims=True)
            expon = expon.astype(BF16)
            exp_out[0, h] = expon
            inv_out[0, h : h + 1] = inverse
            att_out[0, here] = (dot_nn(v, expon) * inverse).astype(BF16)
        hidden = (x + dot_tn(att_out[0], proj[...])).astype(BF16)
        hid_out[0] = hidden
        hidden = hidden.astype(F32)
        normed, _ = norm_forward(hidden)
        second_in = (normed * gain2[...]).astype(BF16)
        result = hidden
        for part in range(4):
            cols = slice(256 * part, 256 * (part + 1))
            act, slope = gelu_and_slope(dot_nn(second_in, up_w[:, cols]))
            act = act.astype(BF16)
            act_out[0, :, cols] = act
            slope_out[0, :, cols] = slope.astype(BF16)
            result = result + dot_nn(act, down_w[cols])
        out_all[step] = result.astype(BF16)
        edge = jnp.where(place.odd == 1, result[336:392], result[0:56])
        edge_out[tw, wc] = edge.astype(BF16)

    @pl.when((tw == 0) & (wc == 3))
    def _():
        edge_copy(0).start()

    @pl.when(step == 7)
    def _():
        edge_copy(1).start()

    @pl.when(step == 8)
    def _():
        grad_reduce[...] = jnp.zeros_like(grad_reduce)
        grad_gain3[...] = jnp.zeros_like(grad_gain3)
        for k in (1, 2, 3):
            for part in range(2):
                gm_copy(k, part).wait()

        @pl.when(place.r == 0)
        def _():
            for part in range(2):
                gm_copy(0, part).wait()

        @pl.when(place.r != 0)
        def _():
            for part in range(2):
                gm_local(part).wait()

        edge_copy(0).wait()

    @pl.when(step == 9)
    def _():
        edge_copy(1).wait()

    @pl.when(step >= 8)
    def _():
        merge_half(
            step - 8, place.odd, out_all, edge_in, gm_in, gain3, reduce_w, grad_out, m_all,
            grad_gain3, rows_all, third_all, gm_rows, grad_reduce,
        )

    @pl.when(step == 9)
    def _():
        store_blocks(reduce_rows, 0, grad_reduce)
        for at in range(5):
            row_copy(at).wait_send()
        for n in range(4):
            remote(pack_t.at[n], halo_t.at[n], t_sems, n, place.at(-1, 0)).wait_send()


def whole(shape):
    return pl.BlockSpec(shape, lambda *_: (0,) * len(shape))


def by_window(shape):
    return pl.BlockSpec((1,) + shape, lambda s: (jnp.minimum(s, 7),) + (0,) * len(shape))


ANY_SPEC = pl.BlockSpec(memory_space=pl.ANY)
DMA = pltpu.SemaphoreType.DMA


def positions():
    at = jnp.arange(NPOS)
    rows = [at % 8, at // 56, (at // 8) % 7]
    return jnp.concatenate([jnp.stack(rows), jnp.zeros((5, NPOS), at.dtype)]).astype(F32)


def run_forward(tokens, gm, ids, *weights):
    saved = [
        ((NPOS, C), BF16),
        ((3 * C, NPOS), BF16),
        ((HEADS, NPOS, NPOS), BF16),
        ((HEADS, NPOS), F32),
        ((C, NPOS), BF16),
        ((NPOS, C), BF16),
        ((NPOS, HID), BF16),
        ((NPOS, HID), BF16),
    ]
    others = [
        ((3 * C, C), BF16),
        ((8, NPOS, C), BF16),
        ((4, 4, 14, 4, C3), BF16),
        ((4096, 128), BF16),
        ((1, 4 * C), F32),
    ]
    pos = positions()
    return pl.pallas_call(
        forward_kernel,
        grid=(10,),
        out_shape=[jax.ShapeDtypeStruct((8,) + shape, kind) for shape, kind in saved]
        + [jax.ShapeDtypeStruct(shape, kind) for shape, kind in others],
        in_specs=[ANY_SPEC, ANY_SPEC, whole(ids.shape), whole(pos.shape)]
        + [whole(w.shape) for w in weights],
        out_specs=[by_window(shape) for shape, _ in saved] + [whole(shape) for shape, _ in others],
        scratch_shapes=[
            pltpu.VMEM((7, 28, 16, C), BF16),
            pltpu.VMEM((49, 8, C), F32),
            pltpu.VMEM((4, 13, 16, C), BF16),
            pltpu.VMEM((4, 13, 16, C), BF16),
            pltpu.VMEM((2, 4, 56, C), BF16),
            pltpu.VMEM((2, 4, 56, C), BF16),
            pltpu.VMEM((4, 4, 14, 4, C3), BF16),
            pltpu.VMEM((8, NPOS, C), BF16),
            pltpu.VMEM((8, 28, 8, C), F32),
            pltpu.VMEM((448, 4 * C), BF16),
            pltpu.VMEM((448, C3), BF16),
            pltpu.VMEM((4 * C, C3), F32),
            DMA((2,)), DMA((5,)), DMA((5,)), DMA((4,)), DMA((4,)), DMA((8,)), DMA((8,)),
            DMA((2,)), DMA((2,)), DMA((2,)),
        ],
        compiler_params=pltpu.CompilerParams(
            vmem_limit_bytes=60 * MIB, collective_id=1, has_side_effects=True
        ),
        name="forward",
    )(tokens, gm, ids, pos, *weights)


ORDERS = (("x", "y", "z"), ("y", "z", "x"), ("z", "x", "y"))


def torus(n_tm):
    return {32: (4, 2, 4), 4: (2, 1, 2)}[n_tm]


class Torus:
    def __init__(self, dims):
        self.dims = dims
        _, n_yl, n_z = dims
        m, r = lax.axis_index("tm"), lax.axis_index("rows")
        self.core = lax.rem(r, 2)
        self.size = dims[0]
        self.at = {
            "x": m // (n_yl * n_z),
            "y": (r // 2) * n_yl + lax.rem(m // n_z, n_yl),
            "z": lax.rem(m, n_z),
        }

    def device(self, core=None, **moved):
        _, n_yl, n_z = self.dims
        at = {**self.at, **moved}
        core = self.core if core is None else core
        m = (at["x"] * n_yl + lax.rem(at["y"], n_yl)) * n_z + at["z"]
        return (m, (at["y"] // n_yl) * 2 + core)

    def partners(self, axis):
        places = [lax.rem(self.at[axis] + j, self.size) for j in range(1, self.size)]
        return [(place, self.device(**{axis: place})) for place in places]

    def other(self):
        return self.device(core=1 - self.core)

    def everyone(self):
        return [self.other()] + [dev for axis in "xyz" for _, dev in self.partners(axis)]


def at_rows(start, length):
    return pl.ds(pl.multiple_of(start, 16), length)


class Sum:
    def __init__(self, here, lengths, whole_last, source, total, base, scratch):
        self.here, self.lengths, self.whole_last = here, lengths, whole_last
        self.source, self.total, self.base = source, total, base
        self.core_in, *rest = scratch
        self.accs, self.ins = rest[0:3], rest[3:6]
        self.core_sems, self.rs_sems, self.ag_sems, self.back_sems = (
            tuple(rest[6 + 2 * n : 8 + 2 * n]) for n in range(4)
        )

    @staticmethod
    def scratch(size, lengths, whole_last):
        most, length = max(lengths), max(lengths)
        shapes = [(3, most, 128)]
        accs, ins = [], []
        for s in range(3):
            accs.append((3, length, 128))
            length = length if s == 2 and whole_last else length // size
            ins.append((3, size - 1, length, 128))
        sems = [(3,), (3,), (9 * (size - 1),), (9 * (size - 1),), (9 * (size - 1),), (9 * (size - 1),), (3,), (3,)]
        return [pltpu.VMEM(shape, BF16) for shape in shapes + accs + ins] + [DMA(n) for n in sems]

    def half(self, core, p):
        return core * sum(self.lengths) + sum(self.lengths[:p])

    def piece(self, p, s):
        start, length = self.half(self.here.core, p), self.lengths[p]
        for n in range(s):
            if not (n == 2 and self.whole_last):
                length = length // self.here.size
                start = start + self.here.at[ORDERS[p][n]] * length
        return start, length

    def core_copy(self, p):
        start = self.half(1 - self.here.core, p)
        return remote(
            self.source.at[at_rows(start, self.lengths[p])],
            self.core_in.at[p, 0 : self.lengths[p]],
            self.core_sems, p, self.here.other(),
        )

    def rs_copies(self, p, s):
        _, length = self.piece(p, s)
        whole_piece = s == 3 and self.whole_last
        return [
            remote(
                self.accs[s - 1].at[p, 0:length]
                if whole_piece
                else self.accs[s - 1].at[p, at_rows(place * length, length)],
                self.ins[s - 1].at[p, j, 0:length],
                self.rs_sems, (3 * (s - 1) + p) * (self.here.size - 1) + j, dev,
            )
            for j, (place, dev) in enumerate(self.here.partners(ORDERS[p][s - 1]))
        ]

    def ag_copies(self, p, s):
        start, length = self.piece(p, s)
        region = self.total.at[at_rows(self.base + start, length)]
        return [
            remote(region, region, self.ag_sems, (3 * (s - 1) + p) * (self.here.size - 1) + j, dev)
            for j, (_, dev) in enumerate(self.here.partners(ORDERS[p][s - 1]))
        ]

    def back_copy(self, p):
        start, length = self.piece(p, 0)
        region = self.total.at[at_rows(self.base + start, length)]
        return remote(region, region, self.back_sems, p, self.here.other())

    def start(self):
        for p in range(3):
            self.core_copy(p).start()

    def reduce(self, s):
        for p in range(3):
            start, length = self.piece(p, s)
            if s == 0:
                self.core_copy(p).wait_recv()
                value = self.source[at_rows(start, length)].astype(F32)
                value = value + self.core_in[p, 0:length].astype(F32)
            else:
                for copy in self.rs_copies(p, s):
                    copy.wait_recv()
                if s == 3 and self.whole_last:
                    value = self.accs[2][p, 0:length].astype(F32)
                else:
                    place = self.here.at[ORDERS[p][s - 1]]
                    value = self.accs[s - 1][p, at_rows(place * length, length)].astype(F32)
                for j in range(self.here.size - 1):
                    value = value + self.ins[s - 1][p, j, 0:length].astype(F32)
            if s < 3:
                self.accs[s][p, 0:length] = value.astype(BF16)
                for copy in self.rs_copies(p, s + 1):
                    copy.start()
            else:
                self.total[at_rows(self.base + start, length)] = value.astype(BF16)
                for copy in self.ag_copies(p, 2 if self.whole_last else 3):
                    copy.start()

    def gather(self, s):
        for p in range(3):
            for copy in self.ag_copies(p, s):
                copy.wait_recv()
            for copy in self.ag_copies(p, s - 1) if s > 1 else [self.back_copy(p)]:
                copy.start()

    def finish(self):
        for p in range(3):
            self.back_copy(p).wait()
            self.core_copy(p).wait_send()
            for s in (1, 2, 3):
                for copy in self.rs_copies(p, s):
                    copy.wait_send()
                if s < 3 or not self.whole_last:
                    for copy in self.ag_copies(p, s):
                        copy.wait_send()


SUMS = ((2048, 2048, 1024), (512, 256, 256))
SUM_ROWS = tuple(2 * sum(lengths) for lengths in SUMS)
SUM_BASES = (0, SUM_ROWS[0])


def backward_kernel(
    dims, grad_out, att_a, hid_in, act_in, slope_in, x_in, qkv_in, inv_in, att_in, exp_hbm,
    qkv_t, proj, gain1, gain2, up_w, down_w, reduce_rows, grad_gain3, pieces,
    totals, merged, grad_tokens,
    exp_two, grad_hidden_all, grad_att_all, grad_rows_t, grad_qkv_t, grad_proj, grad_up,
    grad_down_t, grad_gain1, grad_gain2, late, final, pack_t, halo_t, early_rows, late_rows, total,
    in_sem, exp_sem,
    t_out, t_in, row_out, row_in, own_sem, m_out, m_in, m_own, total_sem, *sum_scratch,
):
    step = pl.program_id(0)
    tw, wc = 1 - lax.rem(step, 8) // 4, lax.rem(step, 4)
    window = 4 * tw + wc
    first_phase, second_phase = step < 8, step >= 8
    place, here = Place(), Torus(dims)
    t_sems, row_sems, m_sems = (t_out, t_in), (row_out, row_in), (m_out, m_in)
    each = len(sum_scratch) // 2
    early, last = (
        Sum(here, SUMS[n], True, rows, total, SUM_BASES[n], sum_scratch[each * n : each * (n + 1)])
        for n, rows in enumerate((early_rows, late_rows))
    )

    def reduce_copy():
        return pltpu.make_async_copy(reduce_rows, early_rows.at[0:4096], in_sem.at[0])

    def exp_copy(at):
        source = 4 * (1 - lax.rem(at, 8) // 4) + lax.rem(at, 4)
        slot = lax.rem(at, 2)
        return pltpu.make_async_copy(exp_hbm.at[source], exp_two.at[slot], exp_sem.at[slot])

    def m_ends(k, n):
        c = lax.rem(place.r + k + 3, 4)
        start = 4 * place.r + 1 - place.r // 2
        first = (1 - place.odd, 3 - place.odd, 3)[n]
        count = (2, 1, 1)[n]
        return (
            pieces.at[c, pl.ds(first, count)],
            merged.at[pl.ds(lax.rem(start + first, 14), count)],
        )

    def m_copy(k, n):
        return remote(*m_ends(k, n), m_sems, 3 * k + n, place.owner(k)[0])

    def m_local(n):
        return pltpu.make_async_copy(*m_ends(0, n), m_own.at[n])

    def m_each(act_remote, act_local):
        for k in (1, 2, 3):
            act_remote(k, 0)
            act_remote(k, 1)

        @pl.when(place.r == 0)
        def _():
            act_remote(0, 0)
            act_remote(0, 1)

        @pl.when(place.r != 0)
        def _():
            act_local(0)
            act_local(1)

    def t_copy(n):
        return remote(pack_t.at[n], halo_t.at[n], t_sems, n, place.at(1, 0))

    def row_copy(at):
        a, b, n = RUNS[at]
        part, first = (at, 0) if at < 3 else (3, b - 21)
        return remote(
            final.at[part, 4:7, first : first + n], grad_tokens.at[0:3, a : a + n],
            row_sems, at, place.at(0, 1),
        )

    def own_copy(at):
        a, b, n = RUNS[at]
        part, first = (at, 0) if at < 3 else (3, b - 21)
        return pltpu.make_async_copy(
            final.at[part, 0:4, first : first + n], grad_tokens.at[3:7, a : a + n], own_sem.at[at]
        )

    def total_copy(n):
        region = pl.ds(SUM_BASES[n], SUM_ROWS[n])
        return pltpu.make_async_copy(total.at[region], totals.at[region], total_sem.at[n])

    @pl.when(step == 0)
    def _():
        reduce_copy().start()
        for ref in (grad_qkv_t, grad_proj, grad_up, grad_down_t, grad_gain1, grad_gain2):
            ref[...] = jnp.zeros_like(ref)
        sources = [place.at(0, -1), place.at(-1, 0)] + [place.owner(k)[1] for k in (1, 2, 3)]
        place.greet(sources + here.everyone(), place.owner(0)[1])
        m_each(lambda k, n: m_copy(k, n).start(), lambda n: m_local(n).start())

        @pl.when(place.odd == 1)
        def _():
            for k in (1, 2, 3):
                m_copy(k, 2).start()
            m_local(2).start()

    @pl.when(first_phase)
    def _():
        grad_rows = grad_out[0]
        normed2, inverse2 = norm_forward(hid_in[0].astype(F32))
        second_in = (normed2 * gain2[...]).astype(BF16)
        grad_second = jnp.zeros((NPOS, C), F32)
        for part in range(4):
            cols = slice(256 * part, 256 * (part + 1))
            grad_down_t[:, cols] += dot_tn(grad_rows, act_in[0, :, cols])
            grad_act = dot_nt(grad_rows, down_w[cols])
            grad_up_in = (grad_act * slope_in[0, :, cols].astype(F32)).astype(BF16)
            grad_up[:, cols] += dot_tn(second_in, grad_up_in)
            grad_second = grad_second + dot_nt(grad_up_in, up_w[:, cols])
        grad_gain2[...] += jnp.sum(grad_second * normed2, axis=0, keepdims=True)
        back = norm_backward(normed2, inverse2, gain2[...], grad_second)
        grad_hidden = grad_rows.astype(F32) + back
        grad_hidden_all[window] = grad_hidden
        grad_hidden_b = grad_hidden.astype(BF16)
        grad_proj[...] += dot_nn(att_a[0], grad_hidden_b)
        grad_att_all[window] = dot_nt(proj[...], grad_hidden_b).astype(BF16)

    @pl.when(step == 7)
    def _():
        store_blocks(early_rows, 16, grad_up[...])
        store_blocks(early_rows, 24, grad_down_t[...].T)
        store_blocks(early_rows, 32, grad_proj[...])
        rows = [grad_gain2[:, 0:128], grad_gain2[:, 128:256]]
        rows += [grad_gain3[:, 128 * n : 128 * (n + 1)] for n in range(8)]
        rows.append(jnp.zeros((6, 128), F32))
        early_rows[34 * 256 : 34 * 256 + 16] = jnp.concatenate(rows, axis=0).astype(BF16)
        early_rows[34 * 256 + 16 :] = jnp.zeros((SUM_ROWS[0] - 34 * 256 - 16, 128), BF16)
        reduce_copy().wait()
        early.start()

    for at, run in (
        (9, lambda: early.reduce(0)),
        (11, lambda: early.reduce(1)),
        (12, lambda: early.reduce(2)),
        (13, lambda: early.reduce(3)),
        (14, lambda: early.gather(2)),
    ):
        pl.when(step == at)(run)

    @pl.when((step >= 7) & (step < 15))
    def _():
        exp_copy(step + 1).start()

    @pl.when(second_phase)
    def _():
        exp_copy(step).wait()
        slot = lax.rem(step, 2)
        for h in range(HEADS):
            at_q = slice(HEAD * h, HEAD * (h + 1))
            at_k = slice(C + HEAD * h, C + HEAD * (h + 1))
            at_v = slice(2 * C + HEAD * h, 2 * C + HEAD * (h + 1))
            expon = exp_two[slot, h]
            incoming = grad_att_all[window, at_q].astype(F32) * inv_in[0, h : h + 1]
            incoming = incoming.astype(BF16)
            inner = incoming.astype(F32) * att_in[0, at_q].astype(F32)
            inner = jnp.sum(inner, axis=0, keepdims=True)
            grad_probs = dot_tn(qkv_in[0, at_v], incoming)
            grad_scores = (expon.astype(F32) * (grad_probs - inner)).astype(BF16)
            grad_rows_t[at_q] = (dot_nn(qkv_in[0, at_k], grad_scores) * SCALE).astype(BF16)
            grad_rows_t[at_k] = (dot_nt(qkv_in[0, at_q], grad_scores) * LN2).astype(BF16)
            grad_rows_t[at_v] = dot_nt(incoming, expon).astype(BF16)
        normed1, inverse1 = norm_forward(x_in[0].astype(F32))
        first_in = (normed1 * gain1[...]).astype(BF16)
        grad_qkv_t[...] += dot_nn(grad_rows_t[...], first_in)
        grad_first = dot_tn(grad_rows_t[...], qkv_t[...])
        grad_gain1[...] += jnp.sum(grad_first * normed1, axis=0, keepdims=True)
        back = norm_backward(normed1, inverse1, gain1[...], grad_first)
        block = (grad_hidden_all[window] + back).reshape(49, 8, C)

        @pl.when(tw == 1)
        def _():
            late[wc] = block[:, 0:4].astype(BF16)
            pack_t[wc] = pack(block[:, 4:8])
            t_copy(wc).start()

        @pl.when(tw == 0)
        def _():
            t_copy(wc).wait_recv()
            frames = jnp.concatenate([unpack(halo_t[wc]), block, late[wc].astype(F32)], axis=1)
            final[wc] = frames.astype(BF16).reshape(7, 7, 16, C)

    @pl.when(step == 15)
    def _():
        store_blocks(late_rows, 0, grad_qkv_t[...].T)
        rows = [grad_gain1[:, 0:128], grad_gain1[:, 128:256], jnp.zeros((14, 128), F32)]
        late_rows[1536:1552] = jnp.concatenate(rows, axis=0).astype(BF16)
        late_rows[1552:] = jnp.zeros((SUM_ROWS[1] - 1552, 128), BF16)
        last.start()

    for part in range(4):

        @pl.when(step == 12 + part)
        def _(part=part):
            for at in runs_of(part):
                row_copy(at).start()
                own_copy(at).start()

    @pl.when(step == 15)
    def _():
        last.reduce(0)
        early.gather(1)
        last.reduce(1)
        last.reduce(2)
        last.reduce(3)
        early.finish()
        total_copy(0).start()
        last.gather(2)
        last.gather(1)
        for at in range(5):
            row_copy(at).wait()
            own_copy(at).wait()
        for n in range(4):
            t_copy(n).wait_send()
        m_each(lambda k, n: m_copy(k, n).wait(), lambda n: m_local(n).wait())

        @pl.when(place.odd == 1)
        def _():
            for k in (1, 2, 3):
                m_copy(k, 2).wait_send()
            m_local(2).wait()
            m_copy(2, 2).wait_recv()

        @pl.when(place.odd == 0)
        def _():
            for k in (1, 3):
                m_copy(k, 2).wait_recv()

        last.finish()
        total_copy(1).start()
        for n in range(2):
            total_copy(n).wait()


def run_backward(n_tm, grad_out, saved, *weights):
    sums = [(3 * C, C), (C, C), (C, HID), (C, HID), (1, C), (1, C)]
    dims = torus(n_tm)
    x, qkv, expon, inverse, att, hid, act, slope = saved
    *vmem_weights, _, grad_gain3, _ = weights

    def window(step):
        return 4 * (1 - lax.rem(step, 8) // 4) + lax.rem(step, 4)

    def in_first(array):
        shape = array.shape[1:]
        return pl.BlockSpec(
            (1,) + shape, lambda s: (window(jnp.minimum(s, 7)),) + (0,) * len(shape)
        )

    def in_second(array):
        shape = array.shape[1:]
        return pl.BlockSpec(
            (1,) + shape, lambda s: (window(jnp.maximum(s, 8)),) + (0,) * len(shape)
        )

    first, second = (grad_out, att, hid, act, slope), (x, qkv, inverse, att)
    return pl.pallas_call(
        lambda *refs: backward_kernel(dims, *refs),
        grid=(16,),
        out_shape=[
            jax.ShapeDtypeStruct((sum(SUM_ROWS), 128), BF16),
            jax.ShapeDtypeStruct((14, 14, 4, C3), BF16),
            jax.ShapeDtypeStruct((7, 28, 16, C), BF16),
        ],
        in_specs=[in_first(array) for array in first]
        + [in_second(array) for array in second]
        + [ANY_SPEC]
        + [whole(w.shape) for w in vmem_weights]
        + [ANY_SPEC, whole(grad_gain3.shape), ANY_SPEC],
        out_specs=[ANY_SPEC] * 3,
        scratch_shapes=[
            pltpu.VMEM((2, HEADS, NPOS, NPOS), BF16),
            pltpu.VMEM((8, NPOS, C), F32),
            pltpu.VMEM((8, C, NPOS), BF16),
            pltpu.VMEM((3 * C, NPOS), BF16),
        ]
        + [pltpu.VMEM(shape, F32) for shape in sums]
        + [
            pltpu.VMEM((4, 49, 4, C), BF16),
            pltpu.VMEM((4, 7, 7, 16, C), BF16),
            pltpu.VMEM((4, 13, 16, C), BF16),
            pltpu.VMEM((4, 13, 16, C), BF16),
            *(pltpu.VMEM((n, 128), BF16) for n in (*SUM_ROWS, sum(SUM_ROWS))),
            DMA((1,)), DMA((2,)),
            DMA((4,)), DMA((4,)), DMA((5,)), DMA((5,)), DMA((5,)), DMA((12,)), DMA((12,)), DMA((3,)),
            DMA((2,)),
        ]
        + [shape for lengths in SUMS for shape in Sum.scratch(dims[0], lengths, True)],
        compiler_params=pltpu.CompilerParams(
            vmem_limit_bytes=58 * MIB, collective_id=2, has_side_effects=True
        ),
        name="backward",
    )(*first, *second, expon, *weights)


def spread_kernel(
    reduce_in, up_in, down_in, proj_in, qkv_in, gains_in, gain1_in,
    qkv, proj, up, down, reduce_w, gain1, gain2, gain3,
):
    step = pl.program_id(0)
    for ref, blocks in ((qkv, qkv_in), (up, up_in), (down, down_in), (reduce_w, reduce_in)):
        for b in range(ref.shape[1] // 128):
            ref[:, 128 * b : 128 * (b + 1)] = blocks[b].astype(F32)

    @pl.when(step == 0)
    def _():
        for b in range(2):
            proj[:, 128 * b : 128 * (b + 1)] = proj_in[b].astype(F32)
        gains, first = gains_in[0, 0:16].astype(F32), gain1_in[0, 0:16].astype(F32)
        for ref, rows, start in ((gain1, first, 0), (gain2, gains, 0), (gain3, gains, 2)):
            for n in range(ref.shape[1] // 128):
                ref[:, 128 * n : 128 * (n + 1)] = rows[start + n : start + n + 1]


def run_spread(totals):
    shapes = [(C, 3 * C), (C, C), (C, HID), (HID, C), (4 * C, C3), (1, C), (1, C), (1, 4 * C)]
    wide = lambda count: pl.BlockSpec((256, 256), lambda s: (0, jnp.minimum(s, count - 1)))

    def blocks(count, first, steps):
        return pl.BlockSpec(
            (count, 256, 128), lambda s: (first // count + jnp.minimum(s, steps - 1), 0, 0)
        )

    return pl.pallas_call(
        spread_kernel,
        grid=(4,),
        out_shape=[jax.ShapeDtypeStruct(shape, F32) for shape in shapes],
        in_specs=[
            blocks(4, 0, 4), blocks(2, 16, 4), blocks(2, 24, 4), blocks(2, 32, 1), blocks(2, 40, 3),
            blocks(1, 34, 1), blocks(1, 46, 1),
        ],
        out_specs=[
            wide(3),
            whole((C, C)),
            wide(4),
            pl.BlockSpec((256, C), lambda s: (s, 0)),
            pl.BlockSpec((256, C3), lambda s: (s, 0)),
            whole((1, C)),
            whole((1, C)),
            whole((1, 4 * C)),
        ],
        compiler_params=pltpu.CompilerParams(vmem_limit_bytes=60 * MIB),
        name="spread",
    )(*[totals] * 7)


def local(
    tokens, region_ids, gain_attn, qkv_weight, proj_weight, gain_mlp, up_weight, down_weight,
    gain_merge, reduce_weight, grad_merged,
):
    n_tm = lax.axis_size("tm")
    gain1, gain2, gain3 = (g.reshape(1, -1) for g in (gain_attn, gain_mlp, gain_merge))
    *saved, qkv_t, grad_out, pieces, reduce_rows, grad_gain3 = run_forward(
        tokens.transpose(1, 2, 0, 3), grad_merged.transpose(1, 2, 0, 3),
        region_ids.transpose(1, 0, 2), qkv_weight, proj_weight, gain1, gain2, up_weight, down_weight,
        gain3, reduce_weight,
    )
    totals, merged, grad_tokens = run_backward(
        n_tm, grad_out, saved, qkv_t, proj_weight, gain1, gain2, up_weight, down_weight,
        reduce_rows, grad_gain3, pieces,
    )
    *grads, gain1, gain2, gain3 = run_spread(totals.reshape(-1, 256, 128))
    return (
        merged.transpose(2, 0, 1, 3),
        grad_tokens.transpose(2, 0, 1, 3),
        *grads,
        gain1.reshape(-1),
        gain2.reshape(-1),
        gain3.reshape(-1),
    )


def solution(mesh):
    placed = (
        P("tm", "rows", None, None),
        P("tm", "rows", None),
        P(), P(), P(), P(), P(), P(), P(), P(),
        P(("tm", "rows"), None, None, None),
    )
    return jax.shard_map(
        local,
        mesh=mesh,
        in_specs=placed,
        out_specs=(
            P(("tm", "rows"), None, None, None),
            P("tm", "rows", None, None),
            P(), P(), P(), P(), P(), P(), P(), P(),
        ),
        check_vma=False,
    )
```
